32 devices in a mesh: groups: 2 (over x), src: 2 (over core), chan: 8 (over z, y).
Axes of the slice: x: 2, y: 2, z: 4, core: 2. Of those that a mesh axis runs over, the one named last changes fastest.
Arguments:
- residual_input: bfloat16 [32, 8192], P('groups', ('src', 'chan')), parts along dimension 0, may hold values from -6 to 6
- query_heads: bfloat16 [32, 8192], P(('groups', 'src', 'chan')), parts along dimension 0, may hold values from -9 to 9
- new_keyval: bfloat16 [32, 2048], P(('groups', 'src', 'chan')), parts along dimension 0, may hold values from -6 to 6
- cache_pages: bfloat16 [256, 16, 2048], P(('groups', 'src', 'chan')), parts along dimension 0, may hold values from -6 to 6
- prompt_lengths: int32 [32], P('groups'), parts along dimension 0, may hold values from 1 to 256, as said below
- page_owner: int32 [256], P(('groups', 'src', 'chan')), parts along dimension 0, may hold values from 0 to 15, as said below
- page_index: int32 [256], P(('groups', 'src', 'chan')), parts along dimension 0, may hold values from 0 to 15, as said below
- mamba_state: float32 [32, 16, 8192], P(('groups', 'src', 'chan')), parts along dimension 0, may hold values from -6 to 6
- conv_state: float32 [32, 3, 8192], P(('groups', 'src', 'chan')), parts along dimension 0, may hold values from -6 to 6
- out_heads: bfloat16 [8192, 8192], P(None, ('src', 'chan')), may hold values from -0.125 to 0.125
- in_values: bfloat16 [8192, 8192], P(None, ('src', 'chan')), may hold values from -0.0625 to 0.0625
- in_gates: bfloat16 [8192, 8192], P(None, ('src', 'chan')), may hold values from -0.0625 to 0.0625
- conv_taps: float32 [4, 8192], P(None, ('src', 'chan')), may hold values from -3 to 3
- conv_offset: float32 [8192], P(('src', 'chan')), may hold values from -0.6 to 0.6
- state_proj: bfloat16 [8192, 544], P(('src', 'chan')), may hold values from -0.0625 to 0.0625
- step_proj: bfloat16 [512, 8192], P(None, ('src', 'chan')), may hold values from -0.25 to 0.25
- step_bias: float32 [8192], P(('src', 'chan')), may hold values from -4 to -1
- decay_log: float32 [16, 8192], P(None, ('src', 'chan')), may hold values from 0 to 2.77
- skip_gain: float32 [8192], P(('src', 'chan')), may hold values from 0.5 to 1.5
- mamba_down: bfloat16 [8192, 8192], P(('src', 'chan')), may hold values from -0.09375 to 0.09375
Outputs:
- hidden_out: bfloat16 [32, 8192], P('groups', ('src', 'chan')), parts along dimension 0
- mamba_next: float32 [32, 16, 8192], P('groups', None, ('src', 'chan')), parts along dimension 0
- conv_next: float32 [32, 3, 8192], P('groups', None, ('src', 'chan')), parts along dimension 0
The draws below stay inside these ranges and needn't reach their ends.
There are 2 independent parts, one for each index of `groups`. The reference program is written for one: setup_inputs(seed, part) draws one part's arguments, and reference() takes and returns one part's arrays. A program takes and returns all parts, laid end to end along the dimension named above; an argument that names none is the same for every part. Nothing has to cross between parts.
Inputs may be any that keep to these rules, and one draw needn't show every extreme that they name: Request r has ceil(prompt_lengths[r] / 16) cache pages, at most 16; some request has 16 full pages. `page_owner`: every cache page belongs to a request; the 8 pages held by one prefill shard belong to different requests. `page_index`: the pages of request r carry the places 0 to ceil(prompt_lengths[r] / 16) - 1, each once.
All inputs are finite; a program needn't handle non-finite values.
Results may differ from the reference program's by a relative error of at most 0.0065.
Values may be sent and summed in bfloat16 or wider, within the bound.
No kernel may reach another device: no remote copies, remote signals or barrier semaphores. Data moves between devices by JAX's collectives and lax.ppermute only.
A program may use at most 128 MiB of HBM per device.

```python
import math
import jax
import jax.numpy as jnp
from jax import lax

D = 8192
E = 8192
NS = 16
KW = 4
DTR = 512
QH = 64
KVH = 8
HD = 128
PT = 16
ROWS = 16
PAGES_SRC = 8
PAGES = 128


def page_layout(key):
    streams = jax.random.split(key, 5)
    pair_count = ROWS // 2
    paired = jax.random.randint(streams[0], (pair_count,), 1, ROWS)
    counts = jnp.concatenate([paired, ROWS - paired])
    second = jax.random.randint(streams[1], (), 1, ROWS - 1)
    counts = counts.at[0].set(ROWS).at[pair_count].set(1)
    counts = counts.at[1].set(second).at[pair_count + 1].set(ROWS - 1 - second)
    counts = counts[jax.random.permutation(streams[2], ROWS)]
    filled = jax.random.randint(streams[3], (ROWS,), 1, PT + 1)
    filled = jnp.where(counts == ROWS, PT, filled)
    lengths = ((counts - 1) * PT + filled).astype(jnp.int32)
    page_ends = jnp.cumsum(counts)
    starts = page_ends - counts
    position = jnp.arange(PAGES, dtype=jnp.int32)
    request = jnp.sum((position[:, None] >= page_ends[None, :]).astype(jnp.int32), axis=1)
    request_ids = jnp.arange(ROWS, dtype=jnp.int32)
    page_number = position - jnp.sum(jnp.where(request[:, None] == request_ids[None, :], starts[None, :], 0), axis=1)
    sources = jax.random.permutation(streams[4], ROWS)
    where_held = sources[position % ROWS] * PAGES_SRC + position // ROWS
    owner_table = jnp.zeros((PAGES,), jnp.int32).at[where_held].set(request.astype(jnp.int32))
    index_table = jnp.zeros((PAGES,), jnp.int32).at[where_held].set(page_number.astype(jnp.int32))
    return (lengths, owner_table, index_table)


def draw_prompt_lengths(key, part):
    return page_layout(key)[0]


def draw_page_owner(key, part):
    return page_layout(key)[1]


def draw_page_index(key, part):
    return page_layout(key)[2]


def draw_query_heads(key, part):
    key = jax.random.fold_in(key, 7)
    second = jax.random.fold_in(key, 1)
    drawn = jnp.clip(1.5 * jax.random.normal(second, (ROWS, KVH, QH // KVH, HD)), -9.0, 9.0)
    return drawn.reshape(ROWS, QH * HD).astype(jnp.bfloat16)


def draw_cache_pages(key, part):
    key = jax.random.fold_in(key, 8)
    second = jax.random.fold_in(key, 1)
    drawn = jnp.clip(jax.random.normal(second, (PAGES, PT, 2, KVH, HD)), -6.0, 6.0)
    return drawn.reshape(PAGES, PT, 2 * KVH * HD).astype(jnp.bfloat16)


def spiked(result, stream_key, source, target, parts, factor):
    owner, partner = [(jnp.arange(result.shape[dim]) // (result.shape[dim] // parts)).reshape([-1 if axis == dim else 1 for axis in range(result.ndim)]) for dim in (source, target)]
    chosen = jax.random.permutation(stream_key, parts)[partner]
    strong = (owner == chosen) | (owner == (partner + parts // 2) % parts)
    return jnp.where(strong, factor * result, result)


def block_scale(stream_key, dims, cuts, smallest, top_value):
    factor_of, own = 1.0, jax.random.fold_in(stream_key, 6)
    for dim, parts in cuts:
        steps = jnp.exp(jax.random.uniform(jax.random.fold_in(own, dim), (parts,), jnp.float32, smallest / len(cuts), top_value / len(cuts)))
        factor_of = factor_of * jnp.repeat(steps, dims[dim] // parts).reshape([-1 if axis == dim else 1 for axis in range(len(dims))])
    return factor_of


def centred(rng, shape, width, bound, pieces=(), kind=jnp.bfloat16):
    factor_of = block_scale(rng, shape, pieces, -0.22, 0.18) if pieces else 1.0
    values = jax.random.normal(rng, shape, jnp.float32) * width * factor_of
    return jnp.minimum(jnp.maximum(values, -bound), bound).astype(kind)


def heavy_noise(own_key, dims, spread, limit, cuts, heavy, kind=jnp.bfloat16):
    entries = spread * jax.random.normal(own_key, dims, jnp.float32)
    if cuts:
        entries = entries * block_scale(own_key, dims, cuts, -0.22, 0.18)
    return jnp.clip(spiked(entries, jax.random.fold_in(own_key, 3), *heavy), -limit, limit).astype(kind)


def setup_inputs(seed: int = 0, part: int = 0) -> dict:
    seeds = jax.random.split(jax.random.key(seed), 21)
    part_keys = jax.random.split(jax.random.fold_in(seeds[20], part), 21)
    return {
        "residual_input": centred(part_keys[0], (ROWS, D), 1.0, 6.0, ((1, 16),)),
        "query_heads": draw_query_heads(jax.random.fold_in(jax.random.fold_in(seeds[20], part), 71), part),
        "new_keyval": centred(part_keys[2], (ROWS, 2 * KVH * HD), 1.0, 6.0, ((0, 16),)),
        "cache_pages": draw_cache_pages(jax.random.fold_in(jax.random.fold_in(seeds[20], part), 71), part),
        "prompt_lengths": draw_prompt_lengths(jax.random.fold_in(jax.random.fold_in(seeds[20], part), 71), part),
        "page_owner": draw_page_owner(jax.random.fold_in(jax.random.fold_in(seeds[20], part), 71), part),
        "page_index": draw_page_index(jax.random.fold_in(jax.random.fold_in(seeds[20], part), 71), part),
        "mamba_state": centred(part_keys[7], (ROWS, NS, E), 1.0, 6.0, ((0, 16),), jnp.float32),
        "conv_state": centred(part_keys[8], (ROWS, KW - 1, E), 1.0, 6.0, ((0, 16),), jnp.float32),
        "out_heads": centred(seeds[9], (QH * HD, D), (QH * HD // 4) ** -0.5, 0.125, ((1, 16),)),
        "in_values": centred(seeds[10], (D, E), D ** -0.5, 0.0625, ((1, 16),)),
        "in_gates": centred(seeds[11], (D, E), D ** -0.5, 0.0625, ((1, 16),)),
        "conv_taps": centred(seeds[12], (KW, E), KW ** -0.5, 3.0, ((1, 16),), jnp.float32),
        "conv_offset": jnp.clip(jax.random.uniform(seeds[13], (E,), jnp.float32, -0.6, 0.6) * block_scale(seeds[13], (E,), ((0, 16),), -0.4, 0.0), -0.6, 0.6),
        "state_proj": centred(seeds[14], (E, DTR + 2 * NS), E ** -0.5, 0.0625, ((0, 16),)),
        "step_proj": centred(seeds[15], (DTR, E), DTR ** -0.5, 0.25, ((1, 16),)),
        "step_bias": jnp.clip(-4.0 + 3.0 * jax.random.uniform(seeds[16], (E,), jnp.float32) ** block_scale(seeds[16], (E,), ((0, 16),), -0.2, 0.2), -4.0, -1.0),
        "decay_log": jnp.clip(2.77 * jax.random.uniform(seeds[17], (NS, E), jnp.float32) ** block_scale(seeds[17], (NS, E), ((1, 16),), -0.2, 0.2), 0.0, 2.77),
        "skip_gain": jnp.clip(0.5 + 1.0 * jax.random.uniform(seeds[18], (E,), jnp.float32) ** block_scale(seeds[18], (E,), ((0, 16),), -0.2, 0.2), 0.5, 1.5),
        "mamba_down": heavy_noise(seeds[19], (E, D), E ** -0.5, 0.09375, ((0, 16),), (0, 1, 16, 2.0)),
    }


NEGATIVE = -1e+30

def page_terms(scores, usable, values):
    masked = jnp.where(usable[:, None, None, :], scores, NEGATIVE)
    page_peak = lax.optimization_barrier(jnp.max(masked, axis=-1))
    weights = jnp.where(usable[:, None, None, :], jnp.exp(masked - page_peak[..., None]), 0.0)
    page_total = lax.optimization_barrier(jnp.sum(weights, axis=-1))
    rounded = lax.optimization_barrier(weights.astype(jnp.bfloat16))
    page_sum = jnp.einsum('skgt,stkd->skgd', rounded.astype(jnp.float32), values.astype(jnp.float32))
    return (page_peak, page_total, page_sum)

def reference(residual_input, query_heads, new_keyval, cache_pages, prompt_lengths, page_owner, page_index, mamba_state, conv_state, out_heads, in_values, in_gates, conv_taps, conv_offset, state_proj, step_proj, step_bias, decay_log, skip_gain, mamba_down):
    group_size = QH // KVH
    score_scale = 1.0 / math.sqrt(HD)
    queries = query_heads.reshape(ROWS, KVH, group_size, HD)
    page_blocks = cache_pages.reshape(PAGES, PT, 2, KVH, HD)
    chosen = queries[page_owner]
    owner_lengths = prompt_lengths[page_owner]
    offsets = jnp.arange(PT, dtype=jnp.int32)
    usable = page_index[:, None] * PT + offsets[None, :] < owner_lengths[:, None]
    scores = jnp.einsum('skgd,stkd->skgt', chosen.astype(jnp.float32), page_blocks[:, :, 0].astype(jnp.float32)) * score_scale
    page_peak, page_total, page_sum = page_terms(scores, usable, page_blocks[:, :, 1])
    new_token = new_keyval.reshape(ROWS, 2, KVH, HD)
    own_score = jnp.einsum('rkgd,rkd->rkg', queries.astype(jnp.float32), new_token[:, 0].astype(jnp.float32)) * score_scale
    row_peak = jnp.maximum(own_score, jax.ops.segment_max(page_peak, page_owner, num_segments=ROWS))
    factor = jnp.exp(page_peak - row_peak[page_owner])
    own_factor = jnp.exp(own_score - row_peak)
    numer = jax.ops.segment_sum(factor[..., None] * page_sum, page_owner, num_segments=ROWS)
    numer = numer + own_factor[..., None] * new_token[:, 1].astype(jnp.float32)[:, :, None, :]
    denom = jax.ops.segment_sum(factor * page_total, page_owner, num_segments=ROWS) + own_factor
    attended = (numer / denom[..., None]).reshape(ROWS, QH * HD).astype(jnp.bfloat16)
    attention_out = jnp.dot(attended, out_heads, preferred_element_type=jnp.float32)
    hidden_mid = (residual_input.astype(jnp.float32) + attention_out).astype(jnp.bfloat16)
    widened = hidden_mid.astype(jnp.float32)
    inverse_rms = lax.rsqrt(lax.optimization_barrier(jnp.sum(widened * widened, axis=1)) / D + 1e-06)
    value_proj = jnp.dot(hidden_mid, in_values, preferred_element_type=jnp.float32) * inverse_rms[:, None]
    gate_proj = jnp.dot(hidden_mid, in_gates, preferred_element_type=jnp.float32) * inverse_rms[:, None]
    window = jnp.concatenate([conv_state, value_proj[:, None, :]], axis=1)
    conv_next = window[:, 1:, :]
    x_act = jax.nn.silu(lax.optimization_barrier(jnp.sum(window * conv_taps[None], axis=1)) + conv_offset[None, :])
    x_low = x_act.astype(jnp.bfloat16)
    projected = jnp.dot(x_low, state_proj, preferred_element_type=jnp.float32)
    step_low = projected[:, :DTR].astype(jnp.bfloat16)
    b_part = projected[:, DTR:DTR + NS]
    c_part = projected[:, DTR + NS:]
    step = jax.nn.softplus(jnp.dot(step_low, step_proj, preferred_element_type=jnp.float32) + step_bias[None, :])
    decay_factor = jnp.exp(-step[:, None, :] * jnp.exp(decay_log)[None])
    mamba_next = decay_factor * mamba_state + (step * x_act)[:, None, :] * b_part[:, :, None]
    gated = ((lax.optimization_barrier(jnp.sum(mamba_next * c_part[:, :, None], axis=1)) + skip_gain[None, :] * x_act) * jax.nn.silu(gate_proj)).astype(jnp.bfloat16)
    down_sum = jnp.dot(gated, mamba_down, preferred_element_type=jnp.float32)
    hidden_out = (hidden_mid.astype(jnp.float32) + down_sum).astype(jnp.bfloat16)
    return (hidden_out, mamba_next, conv_next)
```

```python
import functools
import math

import jax
import jax.numpy as jnp
from jax import lax
from jax.experimental import pallas as pl
from jax.experimental.pallas import tpu as pltpu
from jax.sharding import PartitionSpec as P

D = 8192
NS = 16
DTR = 512
QH = 64
KVH = 8
HD = 128
G = QH // KVH
LANES = 128
NEGATIVE = -1e30
F32 = jnp.float32
BF16 = jnp.bfloat16
VM = pltpu.VMEM


def round_up(value, step):
    return -(-value // step) * step


def vmem(count):
    return [pl.BlockSpec(memory_space=pltpu.VMEM)] * count


def smem(count):
    return [pl.BlockSpec(memory_space=pltpu.SMEM)] * count


def hbm(count):
    return [pl.BlockSpec(memory_space=pl.ANY)] * count


def params(mib):
    return pltpu.CompilerParams(vmem_limit_bytes=mib * 2**20)


def cost(flops, nbytes):
    return pl.CostEstimate(flops=flops, bytes_accessed=nbytes, transcendentals=0)


def swap(x):
    return lax.ppermute(x, "src", [(0, 1), (1, 0)])


def exchange(x):
    return lax.all_to_all(x, "chan", split_axis=0, concat_axis=0, tiled=True)


def pack_kernel(nchan, query_ref, state_ref, conv_ref, out_ref, heads):
    devices = out_ref.shape[0]
    cols = state_ref.shape[2] // devices
    blocks = cols // LANES
    half = QH // 2
    for h in range(QH):
        heads[h : h + 1, :] = query_ref[0:1, h * HD : (h + 1) * HD].astype(F32)
    tail_at = half + NS * blocks
    tail_rows = out_ref.shape[1] - tail_at
    for i in range(devices):
        side = i // nchan
        out_ref[i, 0:half, :] = heads[side * half : (side + 1) * half, :].astype(BF16)
        rows = []
        for b in range(blocks):
            at = i * cols + b * LANES
            out_ref[i, half + b * NS : half + (b + 1) * NS, :] = state_ref[0, :, at : at + LANES].astype(BF16)
            for w in range(conv_ref.shape[0]):
                rows.append(conv_ref[w, 0:1, at : at + LANES])
        rows.append(jnp.zeros((tail_rows - len(rows), LANES), F32))
        out_ref[i, tail_at : tail_at + tail_rows, :] = jnp.concatenate(rows, axis=0).astype(BF16)


def attend_kernel(
    nchan,
    recv_ref,
    pages_ref,
    other_pages_ref,
    newkv_ref,
    other_newkv_ref,
    owner_ref,
    other_owner_ref,
    index_ref,
    other_index_ref,
    lengths_ref,
    out_ref,
    queries,
    result,
    stats,
    ordered,
):
    rows = recv_ref.shape[0]
    held, tokens = pages_ref.shape[0], pages_ref.shape[1]
    c = lax.axis_index("src")
    d = lax.axis_index("chan")
    half_kv = KVH // 2
    scale = 1.0 / math.sqrt(HD)
    count = 2 * held * tokens
    token = lax.broadcasted_iota(jnp.int32, (1, count), 1)
    page = token // tokens
    offset = token % tokens
    owner_of = jnp.full((1, count), -1, jnp.int32)
    for j in range(2 * held):
        owners, indexes = (owner_ref, index_ref) if j < held else (other_owner_ref, other_index_ref)
        owner = owners[j % held]
        left = lengths_ref[owner] - indexes[j % held] * tokens
        owner_of = jnp.where((page == j) & (offset < left), owner, owner_of)
    row_request = lax.broadcasted_iota(jnp.int32, (rows * G, 1), 0) // G
    mask = row_request == owner_of
    lane16 = lax.broadcasted_iota(jnp.int32, (1, 16), 1)
    new_owner = jnp.where(lane16 == 0, c * nchan + d, jnp.where(lane16 == 1, (1 - c) * nchan + d, -1))
    new_mask = row_request == new_owner
    lane = lax.broadcasted_iota(jnp.int32, (1, LANES), 1)
    collected = jnp.zeros((rows * G, LANES), F32)
    queries[...] = recv_ref[:, 0 : QH // 2, :].astype(F32)
    contract = (((1,), (1,)), ((), ()))
    per_chip = (QH // 2) // nchan
    for k in range(half_kv):
        key_at = pl.multiple_of(c * (half_kv * HD) + k * HD, HD)
        value_at = pl.multiple_of(KVH * HD + c * (half_kv * HD) + k * HD, HD)

        def both(at):
            pages = [r[:, :, pl.ds(at, HD)].reshape(held * tokens, HD) for r in (pages_ref, other_pages_ref)]
            fresh = [r[0:1, pl.ds(at, HD)].astype(F32) for r in (newkv_ref, other_newkv_ref)]
            fresh = jnp.concatenate(fresh + [jnp.zeros((14, HD), F32)], axis=0).astype(BF16)
            return jnp.concatenate(pages, axis=0), fresh

        keys, new_keys = both(key_at)
        values, new_values = both(value_at)
        q = queries[:, k * G : (k + 1) * G, :].reshape(rows * G, HD).astype(BF16)
        scores = lax.dot_general(q, keys, contract, preferred_element_type=F32) * scale
        new_scores = lax.dot_general(q, new_keys, contract, preferred_element_type=F32) * scale
        scores = jnp.where(mask, scores, NEGATIVE)
        new_scores = jnp.where(new_mask, new_scores, NEGATIVE)
        peak = jnp.maximum(jnp.max(scores, axis=1, keepdims=True), jnp.max(new_scores, axis=1, keepdims=True))
        weight = jnp.where(mask, jnp.exp(scores - peak), 0.0)
        new_weight = jnp.where(new_mask, jnp.exp(new_scores - peak), 0.0)
        total = jnp.sum(weight, axis=1, keepdims=True) + jnp.sum(new_weight, axis=1, keepdims=True)
        some = total > 0.0
        safe = jnp.where(some, total, 1.0)
        numer = jnp.dot(weight.astype(BF16), values, preferred_element_type=F32)
        numer = numer + jnp.dot(new_weight.astype(BF16), new_values, preferred_element_type=F32)
        collected = jnp.where(lane == k, jnp.where(some, peak + jnp.log(safe), NEGATIVE), collected)
        result[...] = numer / safe
        for g in range(G):
            head = k * G + g
            place = (head % per_chip) * rows
            out_ref[head // per_chip, place : place + rows, :] = result[pl.ds(g, rows, stride=G), :].astype(BF16)
    stats[...] = collected
    for g in range(G):
        ordered[g * rows : (g + 1) * rows, :] = stats[pl.ds(g, rows, stride=G), :]
    turned = ordered[...].T
    pieces = []
    rest = turned[0:8, :]
    for _ in range(3):
        piece = rest.astype(BF16).astype(F32)
        rest = rest - piece
        for k in range(half_kv):
            for j in range(rows * G // LANES):
                pieces.append(piece[k : k + 1, j * LANES : (j + 1) * LANES])
    chunk = per_chip * rows
    stat_rows = out_ref.shape[1] - chunk
    if stat_rows > len(pieces):
        pieces.append(jnp.zeros((stat_rows - len(pieces), LANES), F32))
    packed = jnp.concatenate(pieces, axis=0).astype(BF16)
    for i in range(nchan):
        out_ref[i, chunk : chunk + stat_rows, :] = packed


def combine_kernel(rows, recv_ref, out_ref, pieces, logs, turned):
    nchan = recv_ref.shape[0]
    per_chip = (QH // 2) // nchan
    chunk = per_chip * rows
    stat_rows = recv_ref.shape[1] - chunk
    vectors = (KVH // 2) * rows * G // LANES
    first = lax.axis_index("chan") * chunk
    row = first // LANES
    pieces[...] = recv_ref[:, chunk : chunk + stat_rows, :].astype(F32)
    logs[...] = jnp.zeros_like(logs)
    for s in range(nchan):
        logs[s : s + 1, :] = (
            pieces[s, pl.ds(row, 1), :] + pieces[s, pl.ds(row + vectors, 1), :] + pieces[s, pl.ds(row + 2 * vectors, 1), :]
        )
    found = logs[0:nchan, :]
    weight = jnp.exp(found - jnp.max(found, axis=0, keepdims=True))
    logs[0:nchan, :] = weight / jnp.sum(weight, axis=0, keepdims=True)
    turned[...] = logs[...].T
    mine = turned[pl.ds(pl.multiple_of(first % LANES, chunk), chunk), :]
    total = jnp.zeros((chunk, LANES), F32)
    for s in range(nchan):
        total = total + recv_ref[s, 0:chunk, :].astype(F32) * mine[:, s : s + 1]
    total = total.astype(BF16)
    for i in range(nchan):
        for h in range(per_chip):
            out_ref[i, :, h * HD : (h + 1) * HD] = total[h * rows : (h + 1) * rows, :]


def weight_copies(weight, buffer, sems, nchan):
    c = lax.axis_index("src")
    depth = weight.shape[0] // (2 * nchan)
    copies = []
    for side in range(2):
        for i in range(nchan):
            start = ((c if side == 0 else 1 - c) * nchan + i) * depth
            slot = side * nchan + i
            copies.append(
                pltpu.make_async_copy(
                    weight.at[pl.ds(pl.multiple_of(start, depth), depth), :],
                    buffer.at[pl.ds(slot * depth, depth), :],
                    sems.at[slot],
                )
            )
    return copies


def streamed_dot(copies, own, other, buffer, nchan):
    depth = buffer.shape[0] // (2 * nchan)
    total = None
    for side, ref in ((0, own), (1, other)):
        for i in range(nchan):
            slot = side * nchan + i
            copies[slot].wait()
            part = jnp.dot(ref[i], buffer[slot * depth : (slot + 1) * depth, :], preferred_element_type=F32)
            total = part if total is None else total + part
    return total


def out_kernel(nchan, own, other, residual, weight, out_ref, buffer, sems):
    copies = weight_copies(weight, buffer, sems, nchan)
    for copy in copies:
        copy.start()
    total = streamed_dot(copies, own, other, buffer, nchan)
    hidden = (residual[...].astype(F32) + total).astype(BF16)
    for i in range(nchan):
        out_ref[i] = hidden


def values_kernel(
    nchan, first_row, own, other, arrived, taps, offset, state_proj, weight, conv_out, act_out, rms_out, proj_out, buffer, sems
):
    copies = weight_copies(weight, buffer, sems, nchan)
    for copy in copies:
        copy.start()
    rows, cols = act_out.shape
    squares = jnp.zeros((rows, 1), F32)
    for ref in (own, other):
        for i in range(nchan):
            wide = ref[i].astype(F32)
            squares = squares + jnp.sum(wide * wide, axis=1, keepdims=True)
    inverse = lax.rsqrt(squares / D + 1e-06)
    rms_out[...] = jnp.broadcast_to(inverse, rms_out.shape)
    steps = conv_out.shape[0]
    blocks = cols // LANES
    tail = arrived[:, first_row:, :].astype(F32)
    past = [
        jnp.concatenate([tail[:, b * steps + w, :] for b in range(blocks)], axis=1) for w in range(steps)
    ]
    value = streamed_dot(copies, own, other, buffer, nchan) * inverse
    window = past + [value]
    mixed = jnp.zeros((rows, cols), F32)
    for w in range(steps + 1):
        mixed = mixed + window[w] * taps[w : w + 1, :]
        if w > 0:
            conv_out[w - 1] = window[w]
    mixed = mixed + offset[...]
    act = mixed / (1.0 + jnp.exp(-mixed))
    act_out[...] = act
    part = lax.dot_general(act.astype(BF16), state_proj[...], (((1,), (1,)), ((), ())), preferred_element_type=F32)
    part = part.astype(BF16)
    width = part.shape[1]
    for i in range(nchan):
        proj_out[i] = jnp.zeros(proj_out.shape[1:], BF16)
        proj_out[i, :, 0:width] = part


def gates_kernel(nchan, own, other, rms, weight, out_ref, buffer, sems):
    copies = weight_copies(weight, buffer, sems, nchan)
    for copy in copies:
        copy.start()
    gate = streamed_dot(copies, own, other, buffer, nchan) * rms[:, 0:1]
    out_ref[...] = gate / (1.0 + jnp.exp(-gate))


def down_copies(weight, buffer, sems, half):
    width = weight.shape[1] // 2
    pieces = sems.shape[0]
    step = width // pieces
    copies = []
    for i in range(pieces):
        start = pl.multiple_of(half * width + i * step, step)
        copies.append(
            pltpu.make_async_copy(weight.at[:, pl.ds(start, step)], buffer.at[:, pl.ds(i * step, step)], sems.at[i])
        )
    return copies


def down_product(copies, gated, buffer, out_ref):
    nchan, rows, cols = out_ref.shape
    step = buffer.shape[1] // len(copies)
    for i, copy in enumerate(copies):
        copy.wait()
        part = jnp.dot(gated, buffer[:, i * step : (i + 1) * step], preferred_element_type=F32).astype(BF16)
        for j in range(step // cols):
            out_ref[i * (step // cols) + j] = part[:, j * cols : (j + 1) * cols]


def scan_kernel(
    state_row,
    own,
    other,
    arrived,
    act_ref,
    gate_ref,
    step_proj,
    step_bias,
    decay_log,
    skip_gain,
    weight,
    next_out,
    gated_out,
    send_out,
    turned,
    mixed,
    buffer,
    sems,
):
    copies = down_copies(weight, buffer, sems, 1 - lax.axis_index("src"))
    for copy in copies:
        copy.start()
    nchan, rows = own.shape[0], own.shape[1]
    cols = act_ref.shape[1]
    blocks = cols // LANES
    projected = jnp.zeros(own.shape[1:], F32)
    for ref in (own, other):
        for i in range(nchan):
            projected = projected + ref[i].astype(F32)
    act = act_ref[...]
    raw = jnp.dot(projected[:, 0:DTR].astype(BF16), step_proj[...], preferred_element_type=F32) + step_bias[...]
    step = jnp.maximum(raw, 0.0) + jnp.log1p(jnp.exp(-jnp.abs(raw)))
    turned[...] = jnp.zeros_like(turned)
    turned[0:rows, :] = projected[:, DTR : DTR + LANES]
    mats = turned[...].T
    rate = -jnp.exp(decay_log[...])
    fed = step * act
    for r in range(rows):
        b_col = mats[0:NS, r : r + 1]
        c_col = mats[NS : 2 * NS, r : r + 1]
        for b in range(blocks):
            at = b * LANES
            lanes = slice(at, at + LANES)
            state = arrived[r, state_row + b * NS : state_row + (b + 1) * NS, :].astype(F32)
            after = jnp.exp(step[r : r + 1, lanes] * rate[:, lanes]) * state + fed[r : r + 1, lanes] * b_col
            next_out[r, :, lanes] = after
            mixed[r : r + 1, lanes] = jnp.sum(after * c_col, axis=0, keepdims=True)
    gated = ((mixed[...] + skip_gain[...] * act) * gate_ref[...]).astype(BF16)
    gated_out[...] = gated
    down_product(copies, gated, buffer, send_out)


def down_kernel(gated, weight, out_ref, buffer, sems):
    copies = down_copies(weight, buffer, sems, lax.axis_index("src"))
    for copy in copies:
        copy.start()
    down_product(copies, gated[...], buffer, out_ref)


def on_device(
    residual_input,
    query_heads,
    new_keyval,
    cache_pages,
    prompt_lengths,
    page_owner,
    page_index,
    mamba_state,
    conv_state,
    out_heads,
    in_values,
    in_gates,
    conv_taps,
    conv_offset,
    state_proj,
    step_proj,
    step_bias,
    decay_log,
    skip_gain,
    mamba_down,
):
    nchan = lax.axis_size("chan")
    devices = 2 * nchan
    rows, cols = residual_input.shape
    blocks = cols // LANES
    half = QH // 2
    steps = conv_state.shape[1]
    conv_row = half + NS * blocks
    pack_rows = round_up(conv_row + steps * blocks, 16)
    call = pl.pallas_call
    shape = jax.ShapeDtypeStruct

    other_pages = swap(cache_pages)
    other_newkv = swap(new_keyval)
    other_owner = swap(page_owner)
    other_index = swap(page_index)
    packed = call(
        functools.partial(pack_kernel, nchan),
        out_shape=shape((devices, pack_rows, LANES), BF16),
        in_specs=vmem(3),
        out_specs=vmem(1)[0],
        scratch_shapes=[VM((QH, HD), F32)],
        compiler_params=params(16),
        name="pack",
    )(query_heads, mamba_state, jnp.transpose(conv_state, (1, 0, 2)))
    arrived = lax.all_to_all(packed, ("src", "chan"), split_axis=0, concat_axis=0, tiled=True)

    chunk = (half // nchan) * rows
    stat_rows = round_up(3 * (KVH // 2) * rows * G // LANES, 16)
    partials = call(
        functools.partial(attend_kernel, nchan),
        out_shape=shape((nchan, chunk + stat_rows, LANES), BF16),
        in_specs=vmem(5) + smem(5),
        out_specs=vmem(1)[0],
        scratch_shapes=[
            VM((rows, half, HD), F32),
            VM((rows * G, LANES), F32),
            VM((rows * G, LANES), F32),
            VM((rows * G, LANES), F32),
        ],
        compiler_params=params(32),
        name="attend",
    )(
        arrived,
        cache_pages,
        other_pages,
        new_keyval,
        other_newkv,
        page_owner,
        other_owner,
        page_index,
        other_index,
        prompt_lengths,
    )
    merged = exchange(partials)
    attended = call(
        functools.partial(combine_kernel, rows),
        out_shape=shape((nchan, rows, cols), BF16),
        in_specs=vmem(1),
        out_specs=vmem(1)[0],
        scratch_shapes=[VM((nchan, stat_rows, LANES), F32), VM((LANES, LANES), F32), VM((LANES, LANES), F32)],
        compiler_params=params(16),
        name="combine",
    )(merged)
    att_own = exchange(attended)
    att_other = swap(att_own)

    weight_buffers = [VM((D, cols), BF16), pltpu.SemaphoreType.DMA((devices,))]
    weight_cost = cost(2 * rows * D * cols, 2 * D * cols)
    hidden = call(
        functools.partial(out_kernel, nchan),
        out_shape=shape((nchan, rows, cols), BF16),
        in_specs=vmem(3) + hbm(1),
        out_specs=vmem(1)[0],
        scratch_shapes=weight_buffers,
        compiler_params=params(24),
        cost_estimate=weight_cost,
        name="out",
    )(att_own, att_other, residual_input, out_heads)
    hid_own = exchange(hidden)
    hid_other = swap(hid_own)

    width = round_up(state_proj.shape[1], LANES)
    conv_next, act, rms, part = call(
        functools.partial(values_kernel, nchan, conv_row),
        out_shape=(
            shape((steps, rows, cols), F32),
            shape((rows, cols), F32),
            shape((rows, LANES), F32),
            shape((nchan, rows, width), BF16),
        ),
        in_specs=vmem(6) + hbm(1),
        out_specs=tuple(vmem(4)),
        scratch_shapes=weight_buffers,
        compiler_params=params(24),
        cost_estimate=weight_cost,
        name="values",
    )(hid_own, hid_other, arrived, conv_taps, conv_offset[None, :], state_proj.T, in_values)
    proj_own = exchange(part)
    gate = call(
        functools.partial(gates_kernel, nchan),
        out_shape=shape((rows, cols), F32),
        in_specs=vmem(3) + hbm(1),
        out_specs=vmem(1)[0],
        scratch_shapes=weight_buffers,
        compiler_params=params(24),
        cost_estimate=weight_cost,
        name="gates",
    )(hid_own, hid_other, rms, in_gates)
    proj_other = swap(proj_own)

    pieces = 4
    down_buffers = [VM((cols, D // 2), BF16), pltpu.SemaphoreType.DMA((pieces,))]
    mamba_next, gated, send = call(
        functools.partial(scan_kernel, half),
        out_shape=(
            shape((rows, NS, cols), F32),
            shape((rows, cols), BF16),
            shape((nchan, rows, cols), BF16),
        ),
        in_specs=vmem(9) + hbm(1),
        out_specs=tuple(vmem(3)),
        scratch_shapes=[VM((LANES, LANES), F32), VM((rows, cols), F32)] + down_buffers,
        compiler_params=params(24),
        name="scan",
    )(
        proj_own,
        proj_other,
        arrived,
        act,
        gate,
        step_proj,
        step_bias[None, :],
        decay_log,
        skip_gain[None, :],
        mamba_down,
    )
    taken = swap(send)
    keep = call(
        down_kernel,
        out_shape=shape((nchan, rows, cols), BF16),
        in_specs=vmem(1) + hbm(1),
        out_specs=vmem(1)[0],
        scratch_shapes=down_buffers,
        compiler_params=params(24),
        cost_estimate=cost(rows * D * cols, D * cols),
        name="down",
    )(gated, mamba_down)
    summed = (keep.astype(F32) + taken.astype(F32)).astype(BF16)
    final = exchange(summed)
    down_sum = jnp.sum(final.astype(F32), axis=0)
    hidden_out = (hidden[0].astype(F32) + down_sum).astype(BF16)
    return (hidden_out, mamba_next, jnp.transpose(conv_next, (1, 0, 2)))


def solution(mesh):
    owners = ("groups", "src", "chan")
    channels = ("src", "chan")
    placed = (
        P("groups", channels),
        P(owners, None),
        P(owners, None),
        P(owners, None, None),
        P("groups"),
        P(owners),
        P(owners),
        P(owners, None, None),
        P(owners, None, None),
        P(None, channels),
        P(None, channels),
        P(None, channels),
        P(None, channels),
        P(channels),
        P(channels, None),
        P(None, channels),
        P(channels),
        P(None, channels),
        P(channels),
        P(channels, None),
    )
    return jax.shard_map(
        on_device,
        mesh=mesh,
        in_specs=placed,
        out_specs=(P("groups", channels), P("groups", None, channels), P("groups", None, channels)),
        check_vma=False,
    )
```

```python
import functools
import math

import jax
import jax.numpy as jnp
from jax import lax
from jax.experimental import pallas as pl
from jax.experimental.pallas import tpu as pltpu
from jax.sharding import PartitionSpec as P

D = 8192
NS = 16
DTR = 512
QH = 64
KVH = 8
HD = 128
G = QH // KVH
LANES = 128
NEGATIVE = -1e30
LOWEST = -1e20
F32 = jnp.float32
BF16 = jnp.bfloat16
VM = pltpu.VMEM


def round_up(value, step):
    return -(-value // step) * step


def vmem(count):
    return [pl.BlockSpec(memory_space=pltpu.VMEM)] * count


def smem(count):
    return [pl.BlockSpec(memory_space=pltpu.SMEM)] * count


def hbm(count):
    return [pl.BlockSpec(memory_space=pltpu.HBM)] * count


def params(mib):
    return pltpu.CompilerParams(vmem_limit_bytes=mib * 2**20)


def cost(flops, nbytes):
    return pl.CostEstimate(flops=flops, bytes_accessed=nbytes, transcendentals=0)


def swap(x):
    return lax.ppermute(x, "src", [(0, 1), (1, 0)])


def exchange(x):
    return lax.all_to_all(x, "chan", split_axis=0, concat_axis=0, tiled=True)


class Chunk:
    def __init__(self, nchan, held_tokens, blocks, steps):
        self.per = QH // nchan
        self.tokens = held_tokens
        self.owner_rows = held_tokens // LANES
        self.value = held_tokens
        self.misc = 2 * held_tokens
        self.query = self.misc + round_up(2 + self.owner_rows, 16)
        self.state = self.query + round_up(2 * self.per, 16)
        self.conv = NS * blocks
        self.state_rows = self.conv + round_up(steps * blocks, 16)
        self.rows = self.state + 2 * self.state_rows


def pack_kernel(
    nchan,
    lay,
    query_hbm,
    other_query,
    newkv_hbm,
    pages_hbm,
    state_hbm,
    conv_hbm,
    owner_hbm,
    index_hbm,
    lengths_hbm,
    out_ref,
    query,
    newkv,
    pages,
    state,
    conv,
    owners,
    indexes,
    lengths,
    sems,
):
    moves = (
        (pages_hbm, pages),
        (state_hbm, state),
        (conv_hbm, conv),
        (query_hbm, query),
        (newkv_hbm, newkv),
        (owner_hbm, owners),
        (index_hbm, indexes),
        (lengths_hbm, lengths),
    )
    copies = [pltpu.make_async_copy(src, dst, sems.at[i]) for i, (src, dst) in enumerate(moves)]
    for copy in copies:
        copy.start()
    c = lax.axis_index("src")
    held, page_tokens = pages.shape[0], pages.shape[1]
    cols = state.shape[2] // (2 * nchan)
    blocks = cols // LANES
    steps = conv.shape[0]
    rep = nchan // KVH
    for copy in copies[3:]:
        copy.wait()
    lane = lax.broadcasted_iota(jnp.int32, (1, LANES), 1)
    per_row = LANES // page_tokens
    owner_rows = []
    for i in range(lay.owner_rows):
        found = jnp.full((1, LANES), -1, jnp.int32)
        for j in range(per_row):
            owner = owners[i * per_row + j]
            left = lengths[owner] - indexes[i * per_row + j] * page_tokens
            found = jnp.where((lane // page_tokens == j) & (lane % page_tokens < left), owner, found)
        owner_rows.append(found.astype(F32))
    fill = lay.query - lay.misc - 2 - lay.owner_rows
    owner_rows.append(jnp.zeros((fill, LANES), F32))
    for d in range(nchan):
        at = (d // rep) * HD
        fresh = [newkv[0:1, x : x + HD].astype(F32) for x in (at, KVH * HD + at)]
        out_ref[d, lay.misc : lay.query, :] = jnp.concatenate(fresh + owner_rows, axis=0).astype(BF16)
        heads = []
        for ref in (query, other_query):
            for h in range(lay.per):
                place = (d * lay.per + h) * HD
                heads.append(ref[0:1, place : place + HD].astype(F32))
        spare = lay.state - lay.query - len(heads)
        if spare:
            heads.append(jnp.zeros((spare, LANES), F32))
        out_ref[d, lay.query : lay.state, :] = jnp.concatenate(heads, axis=0).astype(BF16)
    copies[0].wait()
    for d in range(nchan):
        at = (d // rep) * HD
        out_ref[d, 0 : lay.tokens, :] = pages[:, :, at : at + HD].reshape(lay.tokens, HD)
        at = KVH * HD + at
        out_ref[d, lay.value : lay.misc, :] = pages[:, :, at : at + HD].reshape(lay.tokens, HD)
    copies[1].wait()
    copies[2].wait()
    for side in range(2):
        first = (c if side == 0 else 1 - c) * (nchan * cols)
        for d in range(nchan):
            base = lay.state + side * lay.state_rows
            rows = []
            for b in range(blocks):
                lanes = pl.ds(pl.multiple_of(first + d * cols + b * LANES, LANES), LANES)
                out_ref[d, base + b * NS : base + (b + 1) * NS, :] = state[0, :, lanes].astype(BF16)
                for w in range(steps):
                    rows.append(conv[w, 0:1, lanes])
            spare = lay.state_rows - lay.conv - len(rows)
            rows.append(jnp.zeros((spare, LANES), F32))
            out_ref[d, base + lay.conv : base + lay.state_rows, :] = jnp.concatenate(rows, axis=0).astype(BF16)


def attend_kernel(lay, recv, out_ref, state_out, queries, scores):
    nchan = recv.shape[0]
    per, tokens = lay.per, lay.tokens
    c = lax.axis_index("src")
    count = nchan * per
    scale = 1.0 / math.sqrt(HD)
    contract = (((1,), (1,)), ((), ()))
    new_keys, new_values, owners = [], [], []
    for s in range(nchan):
        state_out[s] = recv[s, lay.state + lay.state_rows : lay.rows, :]
        heads = recv[s, lay.query : lay.state, :].astype(F32)
        queries[s * per : (s + 1) * per, :] = heads[0:per, :]
        queries[count + s * per : count + (s + 1) * per, :] = heads[per : 2 * per, :]
        misc = recv[s, lay.misc : lay.query, :].astype(F32)
        new_keys.append(misc[0:1, :])
        new_values.append(misc[1:2, :])
        owners.append(jnp.concatenate([misc[2 + i : 3 + i, :] for i in range(lay.owner_rows)], axis=1))
    fill = round_up(nchan, 16) - nchan
    if fill:
        new_keys.append(jnp.zeros((fill, HD), F32))
        new_values.append(jnp.zeros((fill, HD), F32))
    new_keys = jnp.concatenate(new_keys, axis=0).astype(BF16)
    new_values = jnp.concatenate(new_values, axis=0).astype(BF16)
    row = lax.broadcasted_iota(jnp.int32, (2 * count, 1), 0)
    side = jnp.where(row < count, c, 1 - c)
    request = side * nchan + (row % count) // per
    lane = lax.broadcasted_iota(jnp.int32, (1, nchan + fill), 1)
    new_owner = jnp.where(lane < nchan, c * nchan + lane, -1)
    q = queries[...].astype(BF16)
    new_scores = lax.dot_general(q, new_keys, contract, preferred_element_type=F32) * scale
    new_scores = jnp.where(request == new_owner, new_scores, NEGATIVE)
    wide = request.astype(F32)
    highest = None
    for s in range(nchan):
        part = lax.dot_general(q, recv[s, 0:tokens, :], contract, preferred_element_type=F32) * scale
        part = jnp.where(wide == owners[s], part, NEGATIVE)
        scores[:, s * tokens : (s + 1) * tokens] = part
        highest = part if highest is None else jnp.maximum(highest, part)
    peak = jnp.maximum(jnp.max(highest, axis=1, keepdims=True), jnp.max(new_scores, axis=1, keepdims=True))
    peak = jnp.maximum(peak, LOWEST)
    new_weight = jnp.exp(new_scores - peak)
    numer = jnp.dot(new_weight.astype(BF16), new_values, preferred_element_type=F32)
    summed = None
    for s in range(nchan):
        weight = jnp.exp(scores[:, s * tokens : (s + 1) * tokens] - peak)
        summed = weight if summed is None else summed + weight
        numer = numer + jnp.dot(weight.astype(BF16), recv[s, lay.value : lay.misc, :], preferred_element_type=F32)
    total = jnp.sum(summed, axis=1, keepdims=True) + jnp.sum(new_weight, axis=1, keepdims=True)
    out_ref[:, 0:HD] = numer
    lane = lax.broadcasted_iota(jnp.int32, (1, LANES), 1)
    out_ref[:, HD : HD + LANES] = jnp.where(lane == 0, peak, total)


def in_order(own, other, c):
    return jnp.where(c == 0, jnp.concatenate([own, other], axis=0), jnp.concatenate([other, own], axis=0))


def own_first(x, c):
    half = x.shape[0] // 2
    return in_order(x[:half], x[half:], c)


def merge_kernel(lay, own, other, out_ref, result):
    nchan = out_ref.shape[0]
    c = lax.axis_index("src")
    count = nchan * lay.per
    theirs = jnp.concatenate([other[count:, :], other[:count, :]], axis=0)
    ours = own[...]
    top = jnp.maximum(ours[:, HD : HD + 1], theirs[:, HD : HD + 1])
    numer, denom = 0.0, 0.0
    for part in (ours, theirs):
        factor = jnp.exp(part[:, HD : HD + 1] - top)
        numer = numer + factor * part[:, 0:HD]
        denom = denom + factor * part[:, HD + 1 : HD + 2]
    result[...] = numer / denom
    for h in range(lay.per):
        mine = result[pl.ds(h, nchan, stride=lay.per), :]
        rest = result[pl.ds(count + h, nchan, stride=lay.per), :]
        block = in_order(mine, rest, c).astype(BF16)
        for i in range(nchan):
            out_ref[i, :, h * HD : (h + 1) * HD] = block


def out_kernel(lhs, residual, weight, out_ref):
    total = residual[...].astype(F32)
    depth = lhs.shape[2]
    product = None
    for i in range(lhs.shape[0]):
        part = jnp.dot(lhs[i], weight[i * depth : (i + 1) * depth, :], preferred_element_type=F32)
        product = part if product is None else product + part
    hidden = (total + product).astype(BF16)
    for i in range(out_ref.shape[0]):
        out_ref[i] = hidden


def halves_dot(own, other, weight):
    c = lax.axis_index("src")
    nchan, depth = own.shape[0], own.shape[2]
    total = None
    for ref, half in ((own, c), (other, 1 - c)):
        for i in range(nchan):
            rows = pl.ds(pl.multiple_of((half * nchan + i) * depth, depth), depth)
            part = jnp.dot(ref[i], weight[rows, :], preferred_element_type=F32)
            total = part if total is None else total + part
    return total


def values_kernel(
    lay, own, other, arrived, other_state, taps, offset, state_proj, weight, conv_out, act_out, rms_out, proj_out
):
    c = lax.axis_index("src")
    nchan = own.shape[0]
    rows, cols = act_out.shape
    squares = jnp.zeros((rows, own.shape[2]), F32)
    for ref in (own, other):
        for i in range(nchan):
            wide = ref[i].astype(F32)
            squares = squares + wide * wide
    inverse = lax.rsqrt(jnp.sum(squares, axis=1, keepdims=True) / D + 1e-06)
    rms_out[...] = jnp.broadcast_to(inverse, rms_out.shape)
    steps = conv_out.shape[0]
    blocks = cols // LANES
    at = lay.state + lay.conv
    tails = (
        arrived[:, at : lay.state + lay.state_rows, :].astype(F32),
        other_state[:, lay.conv : lay.state_rows, :].astype(F32),
    )
    window = []
    for w in range(steps):
        sides = [jnp.concatenate([t[:, b * steps + w, :] for b in range(blocks)], axis=1) for t in tails]
        window.append(in_order(sides[0], sides[1], c))
    window.append(halves_dot(own, other, weight) * inverse)
    mixed = jnp.zeros((rows, cols), F32)
    for w in range(steps + 1):
        mixed = mixed + window[w] * taps[w : w + 1, :]
        if w > 0:
            conv_out[w - 1] = window[w]
    mixed = mixed + offset[...]
    act = mixed / (1.0 + jnp.exp(-mixed))
    act_out[...] = act
    part = lax.dot_general(act.astype(BF16), state_proj[...], (((1,), (1,)), ((), ())), preferred_element_type=F32)
    part = part.astype(BF16)
    width = part.shape[1]
    for i in range(nchan):
        proj_out[i] = jnp.zeros(proj_out.shape[1:], BF16)
        proj_out[i, :, 0:width] = part


def gates_kernel(own, other, rms, weight, out_ref):
    gate = halves_dot(own, other, weight) * rms[:, 0:1]
    out_ref[...] = gate / (1.0 + jnp.exp(-gate))


def down_product(gated, weight, half, out_ref):
    nchan, rows, cols = out_ref.shape
    step = max(cols, min(1024, nchan * cols))
    for i in range(nchan * cols // step):
        at = pl.multiple_of(half * (nchan * cols) + i * step, step)
        part = jnp.dot(gated, weight[:, pl.ds(at, step)], preferred_element_type=F32).astype(out_ref.dtype)
        for j in range(step // cols):
            out_ref[i * (step // cols) + j] = part[:, j * cols : (j + 1) * cols]


def scan_kernel(
    lay,
    own,
    other,
    arrived,
    other_state,
    act_ref,
    gate_ref,
    step_proj,
    step_bias,
    decay_log,
    skip_gain,
    weight,
    next_out,
    gated_out,
    send_out,
    turned,
    mixed,
):
    c = lax.axis_index("src")
    nchan, rows = own.shape[0], own.shape[1]
    cols = act_ref.shape[1]
    blocks = cols // LANES
    projected = jnp.zeros(own.shape[1:], F32)
    for ref in (own, other):
        for i in range(nchan):
            projected = projected + ref[i].astype(F32)
    act = act_ref[...]
    raw = jnp.dot(projected[:, 0:DTR].astype(BF16), step_proj[...], preferred_element_type=F32) + step_bias[...]
    step = jnp.maximum(raw, 0.0) + jnp.log1p(jnp.exp(-jnp.abs(raw)))
    turned[...] = jnp.zeros_like(turned)
    turned[0:rows, :] = own_first(projected[:, DTR : DTR + LANES], c)
    mats = turned[...].T
    rate = -jnp.exp(decay_log[...])
    fed = own_first(step * act, c)
    step = own_first(step, c)
    for side, states, base in ((0, arrived, lay.state), (1, other_state, 0)):
        for s in range(nchan):
            q = side * nchan + s
            place = (c if side == 0 else 1 - c) * nchan + s
            b_col = mats[0:NS, q : q + 1]
            c_col = mats[NS : 2 * NS, q : q + 1]
            for b in range(blocks):
                lanes = slice(b * LANES, (b + 1) * LANES)
                state = states[s, base + b * NS : base + (b + 1) * NS, :].astype(F32)
                after = jnp.exp(step[q : q + 1, lanes] * rate[:, lanes]) * state + fed[q : q + 1, lanes] * b_col
                next_out[place, :, lanes] = after
                mixed[q : q + 1, lanes] = jnp.sum(after * c_col, axis=0, keepdims=True)
    gated = ((own_first(mixed[...], c) + skip_gain[...] * act) * gate_ref[...]).astype(BF16)
    gated_out[...] = gated
    down_product(gated, weight, 1 - c, send_out)


def down_kernel(gated, weight, out_ref):
    down_product(gated[...], weight, lax.axis_index("src"), out_ref)


def on_device(
    residual_input,
    query_heads,
    new_keyval,
    cache_pages,
    prompt_lengths,
    page_owner,
    page_index,
    mamba_state,
    conv_state,
    out_heads,
    in_values,
    in_gates,
    conv_taps,
    conv_offset,
    state_proj,
    step_proj,
    step_bias,
    decay_log,
    skip_gain,
    mamba_down,
):
    nchan = lax.axis_size("chan")
    rows, cols = residual_input.shape
    steps = conv_state.shape[1]
    held, page_tokens = cache_pages.shape[0], cache_pages.shape[1]
    lay = Chunk(nchan, held * page_tokens, cols // LANES, steps)
    call = pl.pallas_call
    shape = jax.ShapeDtypeStruct

    other_query = swap(query_heads)
    conv_rows = jnp.transpose(conv_state, (1, 0, 2))
    packed = call(
        functools.partial(pack_kernel, nchan, lay),
        out_shape=shape((nchan, lay.rows, LANES), BF16),
        in_specs=hbm(1) + vmem(1) + hbm(7),
        out_specs=vmem(1)[0],
        scratch_shapes=[
            VM(query_heads.shape, BF16),
            VM(new_keyval.shape, BF16),
            VM(cache_pages.shape, BF16),
            VM(mamba_state.shape, F32),
            VM(conv_rows.shape, F32),
            pltpu.SMEM(page_owner.shape, jnp.int32),
            pltpu.SMEM(page_index.shape, jnp.int32),
            pltpu.SMEM(prompt_lengths.shape, jnp.int32),
            pltpu.SemaphoreType.DMA((8,)),
        ],
        compiler_params=params(16 if held < 16 else 40),
        name="pack",
    )(
        query_heads,
        other_query,
        new_keyval,
        cache_pages,
        mamba_state,
        conv_rows,
        page_owner,
        page_index,
        prompt_lengths,
    )
    arrived = exchange(packed)

    pairs = rows * lay.per
    partial, state_send = call(
        functools.partial(attend_kernel, lay),
        out_shape=(shape((pairs, HD + LANES), F32), shape((nchan, lay.state_rows, LANES), BF16)),
        in_specs=vmem(1),
        out_specs=tuple(vmem(2)),
        scratch_shapes=[VM((pairs, HD), F32), VM((pairs, nchan * lay.tokens), F32)],
        compiler_params=params(8 if held < 16 else 48),
        name="attend",
    )(arrived)
    other_partial = swap(partial)
    other_state = swap(state_send)
    attended = call(
        functools.partial(merge_kernel, lay),
        out_shape=shape((nchan, rows, lay.per * HD), BF16),
        in_specs=vmem(2),
        out_specs=vmem(1)[0],
        scratch_shapes=[VM((pairs, HD), F32)],
        compiler_params=params(8),
        name="merge",
    )(partial, other_partial)
    features = exchange(attended)

    weight_cost = cost(2 * rows * D * cols, 2 * D * cols)
    hidden = call(
        out_kernel,
        out_shape=shape((nchan, rows, cols), BF16),
        in_specs=vmem(3),
        out_specs=vmem(1)[0],
        compiler_params=params(16),
        cost_estimate=weight_cost,
        name="out",
    )(features, residual_input, out_heads)
    hid_own = exchange(hidden)
    hid_other = swap(hid_own)

    width = round_up(state_proj.shape[1], LANES)
    conv_next, act, rms, part = call(
        functools.partial(values_kernel, lay),
        out_shape=(
            shape((steps, rows, cols), F32),
            shape((rows, cols), F32),
            shape((rows, LANES), F32),
            shape((nchan, rows, width), BF16),
        ),
        in_specs=vmem(8),
        out_specs=tuple(vmem(4)),
        compiler_params=params(16),
        cost_estimate=weight_cost,
        name="values",
    )(hid_own, hid_other, arrived, other_state, conv_taps, conv_offset[None, :], state_proj.T, in_values)
    proj_own = exchange(part)
    gate = call(
        gates_kernel,
        out_shape=shape((rows, cols), F32),
        in_specs=vmem(4),
        out_specs=vmem(1)[0],
        compiler_params=params(16),
        cost_estimate=weight_cost,
        name="gates",
    )(hid_own, hid_other, rms, in_gates)
    proj_own, gate = lax.optimization_barrier((proj_own, gate))
    proj_other = swap(proj_own)

    mamba_next, gated, send = call(
        functools.partial(scan_kernel, lay),
        out_shape=(
            shape((rows, NS, cols), F32),
            shape((rows, cols), BF16),
            shape((nchan, rows, cols), BF16),
        ),
        in_specs=vmem(11),
        out_specs=tuple(vmem(3)),
        scratch_shapes=[VM((LANES, LANES), F32), VM((rows, cols), F32)],
        compiler_params=params(16),
        name="scan",
    )(
        proj_own,
        proj_other,
        arrived,
        other_state,
        act,
        gate,
        step_proj,
        step_bias[None, :],
        decay_log,
        skip_gain[None, :],
        mamba_down,
    )
    taken = swap(send)
    keep = call(
        down_kernel,
        out_shape=shape((nchan, rows, cols), F32),
        in_specs=vmem(2),
        out_specs=vmem(1)[0],
        compiler_params=params(16),
        cost_estimate=cost(rows * D * cols, D * cols),
        name="down",
    )(gated, mamba_down)
    summed = (keep + taken.astype(F32)).astype(BF16)
    final = exchange(summed)
    down_sum = jnp.sum(final.astype(F32), axis=0)
    hidden_out = (hidden[0].astype(F32) + down_sum).astype(BF16)
    return (hidden_out, mamba_next, jnp.transpose(conv_next, (1, 0, 2)))


def solution(mesh):
    owners = ("groups", "src", "chan")
    channels = ("src", "chan")
    placed = (
        P("groups", channels),
        P(owners, None),
        P(owners, None),
        P(owners, None, None),
        P("groups"),
        P(owners),
        P(owners),
        P(owners, None, None),
        P(owners, None, None),
        P(None, channels),
        P(None, channels),
        P(None, channels),
        P(None, channels),
        P(channels),
        P(channels, None),
        P(None, channels),
        P(channels),
        P(None, channels),
        P(channels),
        P(channels, None),
    )
    return jax.shard_map(
        on_device,
        mesh=mesh,
        in_specs=placed,
        out_specs=(P("groups", channels), P("groups", None, channels), P("groups", None, channels)),
        check_vma=False,
    )
```

```python
import functools
import math

import jax
import jax.numpy as jnp
from jax import lax
from jax.experimental import pallas as pl
from jax.experimental.pallas import tpu as pltpu
from jax.sharding import PartitionSpec as P

D = 8192
NS = 16
DTR = 512
QH = 64
KVH = 8
HD = 128
G = QH // KVH
LANES = 128
NEGATIVE = -1e30
LOWEST = -1e20
STREAM_MIB = 50
SHORT = 3 * 10**9
F32 = jnp.float32
BF16 = jnp.bfloat16
VM = pltpu.VMEM


def round_up(value, step):
    return -(-value // step) * step


def vmem(count):
    return [pl.BlockSpec(memory_space=pltpu.VMEM)] * count


def smem(count):
    return [pl.BlockSpec(memory_space=pltpu.SMEM)] * count


def hbm(count):
    return [pl.BlockSpec(memory_space=pltpu.HBM)] * count


def params(mib):
    return pltpu.CompilerParams(vmem_limit_bytes=mib * 2**20)


def cost(flops, nbytes):
    return pl.CostEstimate(flops=flops, bytes_accessed=nbytes, transcendentals=0)


def swap(x):
    return lax.ppermute(x, "src", [(0, 1), (1, 0)])


def exchange(x):
    return lax.all_to_all(x, "chan", split_axis=0, concat_axis=0, tiled=True)


class Chunk:
    def __init__(self, nchan, held_tokens, blocks, steps):
        self.per = QH // nchan
        self.tokens = held_tokens
        self.owner_rows = held_tokens // LANES
        self.value = held_tokens
        self.misc = 2 * held_tokens
        self.query = self.misc + round_up(2 + self.owner_rows, 16)
        self.conv = self.query + round_up(2 * self.per, 16)
        self.conv_rows = round_up(steps * blocks, 16)
        self.rows = self.conv + 2 * self.conv_rows


def pack_kernel(
    nchan,
    lay,
    query_hbm,
    other_hbm,
    newkv_hbm,
    pages_hbm,
    conv_hbm,
    owner_hbm,
    index_hbm,
    lengths_hbm,
    out_ref,
    query,
    other_query,
    newkv,
    pages,
    conv,
    owners,
    indexes,
    lengths,
    sems,
):
    moves = (
        (pages_hbm, pages),
        (conv_hbm, conv),
        (query_hbm, query),
        (other_hbm, other_query),
        (newkv_hbm, newkv),
        (owner_hbm, owners),
        (index_hbm, indexes),
        (lengths_hbm, lengths),
    )
    copies = [pltpu.make_async_copy(src, dst, sems.at[i]) for i, (src, dst) in enumerate(moves)]
    for copy in copies:
        copy.start()
    c = lax.axis_index("src")
    page_tokens = pages.shape[1]
    cols = conv.shape[2] // (2 * nchan)
    blocks = cols // LANES
    steps = conv.shape[0]
    rep = nchan // KVH
    for copy in copies[1:]:
        copy.wait()
    lane = lax.broadcasted_iota(jnp.int32, (1, LANES), 1)
    per_row = LANES // page_tokens
    owner_rows = []
    for i in range(lay.owner_rows):
        found = jnp.full((1, LANES), -1, jnp.int32)
        for j in range(per_row):
            owner = owners[i * per_row + j]
            left = lengths[owner] - indexes[i * per_row + j] * page_tokens
            found = jnp.where((lane // page_tokens == j) & (lane % page_tokens < left), owner, found)
        owner_rows.append(found.astype(F32))
    fill = lay.query - lay.misc - 2 - lay.owner_rows
    owner_rows.append(jnp.zeros((fill, LANES), F32))
    for d in range(nchan):
        at = (d // rep) * HD
        fresh = [newkv[0:1, x : x + HD].astype(F32) for x in (at, KVH * HD + at)]
        out_ref[d, lay.misc : lay.query, :] = jnp.concatenate(fresh + owner_rows, axis=0).astype(BF16)
        heads = []
        for ref in (query, other_query):
            for h in range(lay.per):
                place = (d * lay.per + h) * HD
                heads.append(ref[0:1, place : place + HD].astype(F32))
        spare = lay.conv - lay.query - len(heads)
        if spare:
            heads.append(jnp.zeros((spare, LANES), F32))
        out_ref[d, lay.query : lay.conv, :] = jnp.concatenate(heads, axis=0).astype(BF16)
    for side in range(2):
        first = (c if side == 0 else 1 - c) * (nchan * cols)
        for d in range(nchan):
            rows = []
            for b in range(blocks):
                lanes = pl.ds(pl.multiple_of(first + d * cols + b * LANES, LANES), LANES)
                for w in range(steps):
                    rows.append(conv[w, 0:1, lanes])
            rows.append(jnp.zeros((lay.conv_rows - len(rows), LANES), F32))
            base = lay.conv + side * lay.conv_rows
            out_ref[d, base : base + lay.conv_rows, :] = jnp.concatenate(rows, axis=0).astype(BF16)
    copies[0].wait()
    for d in range(nchan):
        at = (d // rep) * HD
        out_ref[d, 0 : lay.tokens, :] = pages[:, :, at : at + HD].reshape(lay.tokens, HD)
        at = KVH * HD + at
        out_ref[d, lay.value : lay.misc, :] = pages[:, :, at : at + HD].reshape(lay.tokens, HD)


def load_kernel(residual, state, residual_out, same, cross):
    c = lax.axis_index("src")
    nchan, _, cols = same.shape
    residual_out[...] = residual[...]
    for ref, half in ((same, c), (cross, 1 - c)):
        for d in range(nchan):
            lanes = pl.ds(pl.multiple_of((half * nchan + d) * cols, cols), cols)
            ref[d] = state[0, :, lanes].astype(BF16)


def attend_kernel(lay, recv, out_ref, conv_out, queries, scores):
    nchan = recv.shape[0]
    per, tokens = lay.per, lay.tokens
    c = lax.axis_index("src")
    count = nchan * per
    scale = 1.0 / math.sqrt(HD)
    contract = (((1,), (1,)), ((), ()))
    new_keys, new_values, owners = [], [], []
    for s in range(nchan):
        conv_out[s] = recv[s, lay.conv + lay.conv_rows : lay.rows, :]
        heads = recv[s, lay.query : lay.conv, :].astype(F32)
        queries[s * per : (s + 1) * per, :] = heads[0:per, :]
        queries[count + s * per : count + (s + 1) * per, :] = heads[per : 2 * per, :]
        misc = recv[s, lay.misc : lay.query, :].astype(F32)
        new_keys.append(misc[0:1, :])
        new_values.append(misc[1:2, :])
        owners.append(jnp.concatenate([misc[2 + i : 3 + i, :] for i in range(lay.owner_rows)], axis=1))
    fill = round_up(nchan, 16) - nchan
    if fill:
        new_keys.append(jnp.zeros((fill, HD), F32))
        new_values.append(jnp.zeros((fill, HD), F32))
    new_keys = jnp.concatenate(new_keys, axis=0).astype(BF16)
    new_values = jnp.concatenate(new_values, axis=0).astype(BF16)
    row = lax.broadcasted_iota(jnp.int32, (2 * count, 1), 0)
    side = jnp.where(row < count, c, 1 - c)
    request = side * nchan + (row % count) // per
    lane = lax.broadcasted_iota(jnp.int32, (1, nchan + fill), 1)
    new_owner = jnp.where(lane < nchan, c * nchan + lane, -1)
    q = queries[...].astype(BF16)
    new_scores = lax.dot_general(q, new_keys, contract, preferred_element_type=F32) * scale
    new_scores = jnp.where(request == new_owner, new_scores, NEGATIVE)
    wide = request.astype(F32)
    highest = None
    for s in range(nchan):
        part = lax.dot_general(q, recv[s, 0:tokens, :], contract, preferred_element_type=F32) * scale
        part = jnp.where(wide == owners[s], part, NEGATIVE)
        scores[:, s * tokens : (s + 1) * tokens] = part
        highest = part if highest is None else jnp.maximum(highest, part)
    peak = jnp.maximum(jnp.max(highest, axis=1, keepdims=True), jnp.max(new_scores, axis=1, keepdims=True))
    peak = jnp.maximum(peak, LOWEST)
    new_weight = jnp.exp(new_scores - peak)
    numer = jnp.dot(new_weight.astype(BF16), new_values, preferred_element_type=F32)
    summed = None
    for s in range(nchan):
        weight = jnp.exp(scores[:, s * tokens : (s + 1) * tokens] - peak)
        summed = weight if summed is None else summed + weight
        numer = numer + jnp.dot(weight.astype(BF16), recv[s, lay.value : lay.misc, :], preferred_element_type=F32)
    total = jnp.sum(summed, axis=1, keepdims=True) + jnp.sum(new_weight, axis=1, keepdims=True)
    out_ref[:, 0:HD] = numer
    lane = lax.broadcasted_iota(jnp.int32, (1, LANES), 1)
    out_ref[:, HD : HD + LANES] = jnp.where(lane == 0, peak, total)


def in_order(own, other, c):
    return jnp.where(c == 0, jnp.concatenate([own, other], axis=0), jnp.concatenate([other, own], axis=0))


def own_first(x, c):
    half = x.shape[0] // 2
    return in_order(x[:half], x[half:], c)


def merge_kernel(lay, own, other, out_ref, result):
    nchan = out_ref.shape[0]
    c = lax.axis_index("src")
    count = nchan * lay.per
    theirs = jnp.concatenate([other[count:, :], other[:count, :]], axis=0)
    ours = own[...]
    top = jnp.maximum(ours[:, HD : HD + 1], theirs[:, HD : HD + 1])
    numer, denom = 0.0, 0.0
    for part in (ours, theirs):
        factor = jnp.exp(part[:, HD : HD + 1] - top)
        numer = numer + factor * part[:, 0:HD]
        denom = denom + factor * part[:, HD + 1 : HD + 2]
    result[...] = numer / denom
    for h in range(lay.per):
        mine = result[pl.ds(h, nchan, stride=lay.per), :]
        rest = result[pl.ds(count + h, nchan, stride=lay.per), :]
        block = in_order(mine, rest, c).astype(BF16)
        for i in range(nchan):
            out_ref[i, :, h * HD : (h + 1) * HD] = block


def stream(weight, buffer, sems, starts):
    depth = buffer.shape[0] // len(starts)
    copies = []
    for i, start in enumerate(starts):
        rows = pl.ds(pl.multiple_of(start, depth), depth)
        copies.append(pltpu.make_async_copy(weight.at[rows, :], buffer.at[pl.ds(i * depth, depth), :], sems.at[i]))
        copies[-1].start()
    return copies


def out_kernel(lhs, residual, cross, weight, hidden_out, out_ref, buffer, sems):
    blocks = sems.shape[0]
    depth = buffer.shape[0] // blocks
    copies = stream(weight, buffer, sems, [i * depth for i in range(blocks)])
    rows = residual.shape[0]
    for i in range(out_ref.shape[0]):
        out_ref[i, rows : rows + NS, :] = cross[i]
    total = residual[...].astype(F32)
    share = lhs.shape[2] // depth
    product = None
    for i, copy in enumerate(copies):
        at = (i % share) * depth
        copy.wait()
        part = jnp.dot(
            lhs[i // share, :, at : at + depth], buffer[i * depth : (i + 1) * depth, :], preferred_element_type=F32
        )
        product = part if product is None else product + part
    hidden = (total + product).astype(BF16)
    hidden_out[...] = hidden
    for i in range(out_ref.shape[0]):
        out_ref[i, 0:rows, :] = hidden


def half_starts(own):
    c = lax.axis_index("src")
    nchan, depth = own.shape[0], own.shape[2]
    return [(half * nchan + i) * depth for half in (c, 1 - c) for i in range(nchan)]


def halves_dot(copies, own, other, buffer, count):
    nchan, depth = own.shape[0], own.shape[2]
    total = None
    for i, copy in enumerate(copies):
        ref = own if i < nchan else other
        copy.wait()
        part = jnp.dot(ref[i % nchan, 0:count, :], buffer[i * depth : (i + 1) * depth, :], preferred_element_type=F32)
        total = part if total is None else total + part
    return total


def values_kernel(
    lay, own, other, arrived, other_conv, taps, offset, state_proj, same, weight, conv_out, act_out, rms_out, proj_out,
    buffer, sems,
):
    copies = stream(weight, buffer, sems, half_starts(own))
    c = lax.axis_index("src")
    nchan = own.shape[0]
    rows, cols = act_out.shape
    squares = jnp.zeros((rows, own.shape[2]), F32)
    for ref in (own, other):
        for i in range(nchan):
            wide = ref[i, 0:rows, :].astype(F32)
            squares = squares + wide * wide
    inverse = lax.rsqrt(jnp.sum(squares, axis=1, keepdims=True) / D + 1e-06)
    rms_out[...] = jnp.broadcast_to(inverse, rms_out.shape)
    steps = conv_out.shape[0]
    blocks = cols // LANES
    tails = (arrived[:, lay.conv : lay.conv + lay.conv_rows, :].astype(F32), other_conv[...].astype(F32))
    window = []
    for w in range(steps):
        sides = [jnp.concatenate([t[:, b * steps + w, :] for b in range(blocks)], axis=1) for t in tails]
        window.append(in_order(sides[0], sides[1], c))
    window.append(halves_dot(copies, own, other, buffer, rows) * inverse)
    mixed = jnp.zeros((rows, cols), F32)
    for w in range(steps + 1):
        mixed = mixed + window[w] * taps[w : w + 1, :]
        if w > 0:
            conv_out[w - 1] = window[w]
    mixed = mixed + offset[...]
    act = mixed / (1.0 + jnp.exp(-mixed))
    act_out[...] = act
    part = lax.dot_general(act.astype(BF16), state_proj[...], (((1,), (1,)), ((), ())), preferred_element_type=F32)
    spare = round_up(part.shape[1], LANES) - part.shape[1]
    part = jnp.concatenate([part, jnp.zeros((rows, spare), F32)], axis=1).astype(BF16)
    base = blocks * NS
    for i in range(nchan):
        for b in range(blocks):
            proj_out[i, b * NS : (b + 1) * NS, :] = same[i, :, b * LANES : (b + 1) * LANES]
        for b in range(part.shape[1] // LANES):
            proj_out[i, base + b * rows : base + (b + 1) * rows, :] = part[:, b * LANES : (b + 1) * LANES]


def gates_kernel(own, other, rms, weight, out_ref, buffer, sems):
    copies = stream(weight, buffer, sems, half_starts(own))
    gate = halves_dot(copies, own, other, buffer, out_ref.shape[0]) * rms[:, 0:1]
    out_ref[...] = gate / (1.0 + jnp.exp(-gate))


def down_stream(weight, buffer, sems, half):
    width = buffer.shape[1]
    step = width // sems.shape[0]
    copies = []
    for i in range(sems.shape[0]):
        columns = pl.ds(pl.multiple_of(half * width + i * step, step), step)
        copies.append(pltpu.make_async_copy(weight.at[:, columns], buffer.at[:, pl.ds(i * step, step)], sems.at[i]))
        copies[-1].start()
    return copies


def down_product(copies, gated, buffer, out_ref):
    cols = out_ref.shape[2]
    step = buffer.shape[1] // len(copies)
    for i, copy in enumerate(copies):
        copy.wait()
        part = jnp.dot(gated, buffer[:, i * step : (i + 1) * step], preferred_element_type=F32).astype(out_ref.dtype)
        for j in range(step // cols):
            out_ref[i * (step // cols) + j] = part[:, j * cols : (j + 1) * cols]


def scan_kernel(
    own,
    other,
    hid_other,
    act_ref,
    gate_ref,
    step_proj,
    step_bias,
    decay_log,
    skip_gain,
    weight,
    next_out,
    gated_out,
    send_out,
    turned,
    mixed,
    buffer,
    sems,
):
    c = lax.axis_index("src")
    copies = down_stream(weight, buffer, sems, 1 - c)
    nchan = own.shape[0]
    rows, cols = act_ref.shape
    blocks = cols // LANES
    base = blocks * NS
    summed = jnp.zeros((own.shape[1] - base, LANES), F32)
    for ref in (own, other):
        for i in range(nchan):
            summed = summed + ref[i, base:, :].astype(F32)
    parts = [summed[b * rows : (b + 1) * rows, :] for b in range(summed.shape[0] // rows)]
    low = jnp.concatenate(parts[: DTR // LANES], axis=1).astype(BF16)
    act = act_ref[...]
    raw = jnp.dot(low, step_proj[...], preferred_element_type=F32) + step_bias[...]
    step = jnp.maximum(raw, 0.0) + jnp.log1p(jnp.exp(-jnp.abs(raw)))
    turned[...] = jnp.zeros_like(turned)
    turned[0:rows, :] = own_first(parts[DTR // LANES], c)
    mats = turned[...].T
    rate = -jnp.exp(decay_log[...])
    fed = own_first(step * act, c)
    step = own_first(step, c)
    for side in range(2):
        for s in range(nchan):
            q = side * nchan + s
            place = (c if side == 0 else 1 - c) * nchan + s
            b_col = mats[0:NS, q : q + 1]
            c_col = mats[NS : 2 * NS, q : q + 1]
            for b in range(blocks):
                lanes = slice(b * LANES, (b + 1) * LANES)
                if side == 0:
                    state = own[s, b * NS : (b + 1) * NS, :].astype(F32)
                else:
                    state = hid_other[s, rows : rows + NS, lanes].astype(F32)
                after = jnp.exp(step[q : q + 1, lanes] * rate[:, lanes]) * state + fed[q : q + 1, lanes] * b_col
                next_out[place, :, lanes] = after
                mixed[q : q + 1, lanes] = jnp.sum(after * c_col, axis=0, keepdims=True)
    gated = ((own_first(mixed[...], c) + skip_gain[...] * act) * gate_ref[...]).astype(BF16)
    gated_out[...] = gated
    down_product(copies, gated, buffer, send_out)


def down_kernel(gated, weight, out_ref, buffer, sems):
    copies = down_stream(weight, buffer, sems, lax.axis_index("src"))
    down_product(copies, gated[...], buffer, out_ref)


def finish_kernel(final, hidden, out_ref):
    total = None
    for i in range(final.shape[0]):
        part = final[i].astype(F32)
        total = part if total is None else total + part
    out_ref[...] = (hidden[...].astype(F32) + total).astype(BF16)


def on_device(
    residual_input,
    query_heads,
    new_keyval,
    cache_pages,
    prompt_lengths,
    page_owner,
    page_index,
    mamba_state,
    conv_state,
    out_heads,
    in_values,
    in_gates,
    conv_taps,
    conv_offset,
    state_proj,
    step_proj,
    step_bias,
    decay_log,
    skip_gain,
    mamba_down,
):
    nchan = lax.axis_size("chan")
    rows, cols = residual_input.shape
    steps = conv_state.shape[1]
    held, page_tokens = cache_pages.shape[0], cache_pages.shape[1]
    lay = Chunk(nchan, held * page_tokens, cols // LANES, steps)
    call = pl.pallas_call
    shape = jax.ShapeDtypeStruct

    other_query = swap(query_heads)
    conv_rows = jnp.transpose(conv_state, (1, 0, 2))
    packed = call(
        functools.partial(pack_kernel, nchan, lay),
        out_shape=shape((nchan, lay.rows, LANES), BF16),
        in_specs=hbm(8),
        out_specs=vmem(1)[0],
        scratch_shapes=[
            VM(query_heads.shape, BF16),
            VM(query_heads.shape, BF16),
            VM(new_keyval.shape, BF16),
            VM(cache_pages.shape, BF16),
            VM(conv_rows.shape, F32),
            pltpu.SMEM(page_owner.shape, jnp.int32),
            pltpu.SMEM(page_index.shape, jnp.int32),
            pltpu.SMEM(prompt_lengths.shape, jnp.int32),
            pltpu.SemaphoreType.DMA((8,)),
        ],
        compiler_params=pltpu.CompilerParams(vmem_limit_bytes=64 * 2**20 - 2**18),
        name="pack",
    )(query_heads, other_query, new_keyval, cache_pages, conv_rows, page_owner, page_index, prompt_lengths)
    packed, residual_input, mamba_state = lax.optimization_barrier((packed, residual_input, mamba_state))
    arrived = exchange(packed)
    cut = shape((nchan, NS, cols), BF16)
    residual, same, cross = call(
        load_kernel,
        out_shape=(shape((rows, cols), BF16), cut, cut),
        in_specs=vmem(2),
        out_specs=tuple(vmem(3)),
        compiler_params=params(16),
        cost_estimate=cost(SHORT, 0),
        name="load",
    )(residual_input, mamba_state)
    arrived, residual, same, cross = lax.optimization_barrier((arrived, residual, same, cross))

    pairs = rows * lay.per
    partial, conv_send = call(
        functools.partial(attend_kernel, lay),
        out_shape=(shape((pairs, HD + LANES), F32), shape((nchan, lay.conv_rows, LANES), BF16)),
        in_specs=vmem(1),
        out_specs=tuple(vmem(2)),
        scratch_shapes=[VM((pairs, HD), F32), VM((pairs, nchan * lay.tokens), F32)],
        compiler_params=params(4 if held < 16 else 40),
        name="attend",
    )(arrived)
    other_partial = swap(partial)
    other_conv = swap(conv_send)
    attended = call(
        functools.partial(merge_kernel, lay),
        out_shape=shape((nchan, rows, lay.per * HD), BF16),
        in_specs=vmem(2),
        out_specs=vmem(1)[0],
        scratch_shapes=[VM((pairs, HD), F32)],
        compiler_params=params(4),
        name="merge",
    )(partial, other_partial)
    features = exchange(attended)

    streamed = [VM((D, cols), BF16), pltpu.SemaphoreType.DMA((2 * nchan,))]
    hidden, hid_send = call(
        out_kernel,
        out_shape=(shape((rows, cols), BF16), shape((nchan, rows + NS, cols), BF16)),
        in_specs=vmem(3) + hbm(1),
        out_specs=tuple(vmem(2)),
        scratch_shapes=streamed,
        compiler_params=params(STREAM_MIB),
        name="out",
    )(features, residual, cross, out_heads)
    hid_own = exchange(hid_send)
    hid_other = swap(hid_own)

    sent_rows = (cols // LANES) * NS + (round_up(state_proj.shape[1], LANES) // LANES) * rows
    conv_next, act, rms, part = call(
        functools.partial(values_kernel, lay),
        out_shape=(
            shape((steps, rows, cols), F32),
            shape((rows, cols), F32),
            shape((rows, LANES), F32),
            shape((nchan, sent_rows, LANES), BF16),
        ),
        in_specs=vmem(8) + hbm(1),
        out_specs=tuple(vmem(4)),
        scratch_shapes=streamed,
        compiler_params=params(STREAM_MIB),
        name="values",
    )(hid_own, hid_other, arrived, other_conv, conv_taps, conv_offset[None, :], state_proj.T, same, in_values)
    proj_own = exchange(part)
    gate = call(
        gates_kernel,
        out_shape=shape((rows, cols), F32),
        in_specs=vmem(3) + hbm(1),
        out_specs=vmem(1)[0],
        scratch_shapes=streamed,
        compiler_params=params(STREAM_MIB),
        cost_estimate=cost(SHORT, 0),
        name="gates",
    )(hid_own, hid_other, rms, in_gates)
    proj_own, gate = lax.optimization_barrier((proj_own, gate))
    proj_other = swap(proj_own)

    down_streamed = [VM((cols, D // 2), BF16), pltpu.SemaphoreType.DMA((4,))]
    mamba_next, gated, send = call(
        scan_kernel,
        out_shape=(
            shape((rows, NS, cols), F32),
            shape((rows, cols), BF16),
            shape((nchan, rows, cols), BF16),
        ),
        in_specs=vmem(9) + hbm(1),
        out_specs=tuple(vmem(3)),
        scratch_shapes=[VM((LANES, LANES), F32), VM((rows, cols), F32)] + down_streamed,
        compiler_params=params(STREAM_MIB),
        name="scan",
    )(
        proj_own,
        proj_other,
        hid_other,
        act,
        gate,
        step_proj,
        step_bias[None, :],
        decay_log,
        skip_gain[None, :],
        mamba_down,
    )
    taken = swap(send)
    keep = call(
        down_kernel,
        out_shape=shape((nchan, rows, cols), F32),
        in_specs=vmem(1) + hbm(1),
        out_specs=vmem(1)[0],
        scratch_shapes=down_streamed,
        compiler_params=params(STREAM_MIB),
        cost_estimate=cost(SHORT, 0),
        name="down",
    )(gated, mamba_down)
    summed = (keep + taken.astype(F32)).astype(BF16)
    hidden_out = call(
        finish_kernel,
        out_shape=shape((rows, cols), BF16),
        in_specs=vmem(2),
        out_specs=vmem(1)[0],
        compiler_params=params(4),
        name="finish",
    )(exchange(summed), hidden)
    return (hidden_out, mamba_next, jnp.transpose(conv_next, (1, 0, 2)))


def solution(mesh):
    owners = ("groups", "src", "chan")
    channels = ("src", "chan")
    placed = (
        P("groups", channels),
        P(owners, None),
        P(owners, None),
        P(owners, None, None),
        P("groups"),
        P(owners),
        P(owners),
        P(owners, None, None),
        P(owners, None, None),
        P(None, channels),
        P(None, channels),
        P(None, channels),
        P(None, channels),
        P(channels),
        P(channels, None),
        P(None, channels),
        P(channels),
        P(None, channels),
        P(channels),
        P(channels, None),
    )
    return jax.shard_map(
        on_device,
        mesh=mesh,
        in_specs=placed,
        out_specs=(P("groups", channels), P("groups", None, channels), P("groups", None, channels)),
        check_vma=False,
    )
```

```python
import functools
import math

import jax
import jax.numpy as jnp
from jax import lax
from jax.experimental import pallas as pl
from jax.experimental.pallas import tpu as pltpu
from jax.sharding import PartitionSpec as P

D = 8192
NS = 16
DTR = 512
QH = 64
KVH = 8
HD = 128
G = QH // KVH
LANES = 128
NEGATIVE = -1e30
LOWEST = -1e20
STREAM_MIB = 50
SHORT = 3 * 10**9
F32 = jnp.float32
BF16 = jnp.bfloat16
VM = pltpu.VMEM


def round_up(value, step):
    return -(-value // step) * step


def vmem(count):
    return [pl.BlockSpec(memory_space=pltpu.VMEM)] * count


def smem(count):
    return [pl.BlockSpec(memory_space=pltpu.SMEM)] * count


def hbm(count):
    return [pl.BlockSpec(memory_space=pltpu.HBM)] * count


def params(mib):
    return pltpu.CompilerParams(vmem_limit_bytes=mib * 2**20)


def cost(flops, nbytes):
    return pl.CostEstimate(flops=flops, bytes_accessed=nbytes, transcendentals=0)


def swap(x):
    return lax.ppermute(x, "src", [(0, 1), (1, 0)])


def exchange(x):
    return lax.all_to_all(x, "chan", split_axis=0, concat_axis=0, tiled=True)


class Chunk:
    def __init__(self, nchan, held_tokens, blocks, steps):
        self.per = QH // nchan
        self.tokens = held_tokens
        self.owner_rows = held_tokens // LANES
        self.value = held_tokens
        self.misc = 2 * held_tokens
        self.query = self.misc + round_up(2 + self.owner_rows, 16)
        self.conv = self.query + round_up(2 * self.per, 16)
        self.conv_rows = round_up(steps * blocks, 16)
        self.rows = self.conv + 2 * self.conv_rows


def pack_kernel(
    nchan,
    lay,
    query_hbm,
    other_hbm,
    newkv_hbm,
    pages_hbm,
    conv_hbm,
    owner_hbm,
    index_hbm,
    lengths_hbm,
    out_ref,
    query,
    other_query,
    newkv,
    pages,
    conv,
    owners,
    indexes,
    lengths,
    sems,
):
    moves = (
        (pages_hbm, pages),
        (conv_hbm, conv),
        (query_hbm, query),
        (other_hbm, other_query),
        (newkv_hbm, newkv),
        (owner_hbm, owners),
        (index_hbm, indexes),
        (lengths_hbm, lengths),
    )
    copies = [pltpu.make_async_copy(src, dst, sems.at[i]) for i, (src, dst) in enumerate(moves)]
    for copy in copies:
        copy.start()
    c = lax.axis_index("src")
    page_tokens = pages.shape[1]
    cols = conv.shape[2] // (2 * nchan)
    blocks = cols // LANES
    steps = conv.shape[0]
    rep = nchan // KVH
    for copy in copies[1:]:
        copy.wait()
    lane = lax.broadcasted_iota(jnp.int32, (1, LANES), 1)
    per_row = LANES // page_tokens
    owner_rows = []
    for i in range(lay.owner_rows):
        found = jnp.full((1, LANES), -1, jnp.int32)
        for j in range(per_row):
            owner = owners[i * per_row + j]
            left = lengths[owner] - indexes[i * per_row + j] * page_tokens
            found = jnp.where((lane // page_tokens == j) & (lane % page_tokens < left), owner, found)
        owner_rows.append(found.astype(F32))
    fill = lay.query - lay.misc - 2 - lay.owner_rows
    owner_rows.append(jnp.zeros((fill, LANES), F32))
    for d in range(nchan):
        at = (d // rep) * HD
        fresh = [newkv[0:1, x : x + HD].astype(F32) for x in (at, KVH * HD + at)]
        out_ref[d, lay.misc : lay.query, :] = jnp.concatenate(fresh + owner_rows, axis=0).astype(BF16)
        heads = []
        for ref in (query, other_query):
            for h in range(lay.per):
                place = (d * lay.per + h) * HD
                heads.append(ref[0:1, place : place + HD].astype(F32))
        spare = lay.conv - lay.query - len(heads)
        if spare:
            heads.append(jnp.zeros((spare, LANES), F32))
        out_ref[d, lay.query : lay.conv, :] = jnp.concatenate(heads, axis=0).astype(BF16)
    for side in range(2):
        first = (c if side == 0 else 1 - c) * (nchan * cols)
        for d in range(nchan):
            rows = []
            for b in range(blocks):
                lanes = pl.ds(pl.multiple_of(first + d * cols + b * LANES, LANES), LANES)
                for w in range(steps):
                    rows.append(conv[w, 0:1, lanes])
            rows.append(jnp.zeros((lay.conv_rows - len(rows), LANES), F32))
            base = lay.conv + side * lay.conv_rows
            out_ref[d, base : base + lay.conv_rows, :] = jnp.concatenate(rows, axis=0).astype(BF16)
    copies[0].wait()
    for d in range(nchan):
        at = (d // rep) * HD
        out_ref[d, 0 : lay.tokens, :] = pages[:, :, at : at + HD].reshape(lay.tokens, HD)
        at = KVH * HD + at
        out_ref[d, lay.value : lay.misc, :] = pages[:, :, at : at + HD].reshape(lay.tokens, HD)


def load_kernel(residual, state, residual_out, same, cross):
    c = lax.axis_index("src")
    nchan, _, cols = same.shape
    residual_out[...] = residual[...]
    for ref, half in ((same, c), (cross, 1 - c)):
        for d in range(nchan):
            lanes = pl.ds(pl.multiple_of((half * nchan + d) * cols, cols), cols)
            ref[d] = state[0, :, lanes].astype(BF16)


def attend_kernel(lay, recv, out_ref, conv_out, queries, scores):
    nchan = recv.shape[0]
    per, tokens = lay.per, lay.tokens
    c = lax.axis_index("src")
    count = nchan * per
    scale = 1.0 / math.sqrt(HD)
    contract = (((1,), (1,)), ((), ()))
    new_keys, new_values, owners = [], [], []
    for s in range(nchan):
        conv_out[s] = recv[s, lay.conv + lay.conv_rows : lay.rows, :]
        heads = recv[s, lay.query : lay.conv, :].astype(F32)
        queries[s * per : (s + 1) * per, :] = heads[0:per, :]
        queries[count + s * per : count + (s + 1) * per, :] = heads[per : 2 * per, :]
        misc = recv[s, lay.misc : lay.query, :].astype(F32)
        new_keys.append(misc[0:1, :])
        new_values.append(misc[1:2, :])
        owners.append(jnp.concatenate([misc[2 + i : 3 + i, :] for i in range(lay.owner_rows)], axis=1))
    fill = round_up(nchan, 16) - nchan
    if fill:
        new_keys.append(jnp.zeros((fill, HD), F32))
        new_values.append(jnp.zeros((fill, HD), F32))
    new_keys = jnp.concatenate(new_keys, axis=0).astype(BF16)
    new_values = jnp.concatenate(new_values, axis=0).astype(BF16)
    row = lax.broadcasted_iota(jnp.int32, (2 * count, 1), 0)
    side = jnp.where(row < count, c, 1 - c)
    request = side * nchan + (row % count) // per
    lane = lax.broadcasted_iota(jnp.int32, (1, nchan + fill), 1)
    new_owner = jnp.where(lane < nchan, c * nchan + lane, -1)
    q = queries[...].astype(BF16)
    new_scores = lax.dot_general(q, new_keys, contract, preferred_element_type=F32) * scale
    new_scores = jnp.where(request == new_owner, new_scores, NEGATIVE)
    wide = request.astype(F32)
    highest = None
    for s in range(nchan):
        part = lax.dot_general(q, recv[s, 0:tokens, :], contract, preferred_element_type=F32) * scale
        part = jnp.where(wide == owners[s], part, NEGATIVE)
        scores[:, s * tokens : (s + 1) * tokens] = part
        highest = part if highest is None else jnp.maximum(highest, part)
    peak = jnp.maximum(jnp.max(highest, axis=1, keepdims=True), jnp.max(new_scores, axis=1, keepdims=True))
    peak = jnp.maximum(peak, LOWEST)
    new_weight = jnp.exp(new_scores - peak)
    numer = jnp.dot(new_weight.astype(BF16), new_values, preferred_element_type=F32)
    summed = None
    for s in range(nchan):
        weight = jnp.exp(scores[:, s * tokens : (s + 1) * tokens] - peak)
        summed = weight if summed is None else summed + weight
        numer = numer + jnp.dot(weight.astype(BF16), recv[s, lay.value : lay.misc, :], preferred_element_type=F32)
    total = jnp.sum(summed, axis=1, keepdims=True) + jnp.sum(new_weight, axis=1, keepdims=True)
    out_ref[:, 0:HD] = numer
    lane = lax.broadcasted_iota(jnp.int32, (1, LANES), 1)
    out_ref[:, HD : HD + LANES] = jnp.where(lane == 0, peak, total)


def in_order(own, other, c):
    return jnp.where(c == 0, jnp.concatenate([own, other], axis=0), jnp.concatenate([other, own], axis=0))


def own_first(x, c):
    half = x.shape[0] // 2
    return in_order(x[:half], x[half:], c)


def merge_kernel(lay, own, other, out_ref, result):
    nchan = out_ref.shape[0]
    c = lax.axis_index("src")
    count = nchan * lay.per
    theirs = jnp.concatenate([other[count:, :], other[:count, :]], axis=0)
    ours = own[...]
    top = jnp.maximum(ours[:, HD : HD + 1], theirs[:, HD : HD + 1])
    numer, denom = 0.0, 0.0
    for part in (ours, theirs):
        factor = jnp.exp(part[:, HD : HD + 1] - top)
        numer = numer + factor * part[:, 0:HD]
        denom = denom + factor * part[:, HD + 1 : HD + 2]
    result[...] = numer / denom
    share = lay.per // 2
    for h in range(share):
        head = c * share + h
        mine = result[pl.ds(head, nchan, stride=lay.per), :]
        rest = result[pl.ds(count + head, nchan, stride=lay.per), :]
        block = in_order(mine, rest, c).astype(BF16)
        for i in range(nchan):
            out_ref[i, :, h * HD : (h + 1) * HD] = block


def stream(weight, buffer, sems, starts):
    depth = buffer.shape[0] // len(starts)
    copies = []
    for i, start in enumerate(starts):
        rows = pl.ds(pl.multiple_of(start, depth), depth)
        copies.append(pltpu.make_async_copy(weight.at[rows, :], buffer.at[pl.ds(i * depth, depth), :], sems.at[i]))
        copies[-1].start()
    return copies


def half_starts(own):
    c = lax.axis_index("src")
    nchan, depth = own.shape[0], own.shape[2]
    return [(half * nchan + i) * depth for half in (c, 1 - c) for i in range(nchan)]


def halves_dot(copies, own, other, buffer, count):
    nchan, depth = own.shape[0], own.shape[2]
    total = None
    for i, copy in enumerate(copies):
        ref = own if i < nchan else other
        copy.wait()
        part = jnp.dot(ref[i % nchan, 0:count, :], buffer[i * depth : (i + 1) * depth, :], preferred_element_type=F32)
        total = part if total is None else total + part
    return total


def out_kernel(own, other, residual, cross, weight, hidden_out, out_ref, buffer, sems):
    c = lax.axis_index("src")
    nchan, rows, depth = own.shape
    starts = [(2 * i + half) * depth for half in (c, 1 - c) for i in range(nchan)]
    copies = stream(weight, buffer, sems, starts)
    for i in range(nchan):
        out_ref[i, rows : rows + NS, :] = cross[i]
    product = halves_dot(copies, own, other, buffer, rows)
    hidden = (residual[...].astype(F32) + product).astype(BF16)
    hidden_out[...] = hidden
    for i in range(nchan):
        out_ref[i, 0:rows, :] = hidden


def values_kernel(
    lay, own, other, arrived, other_conv, taps, offset, state_proj, same, weight, conv_out, act_out, rms_out, proj_out,
    buffer, sems,
):
    copies = stream(weight, buffer, sems, half_starts(own))
    c = lax.axis_index("src")
    nchan = own.shape[0]
    rows, cols = act_out.shape
    squares = jnp.zeros((rows, own.shape[2]), F32)
    for ref in (own, other):
        for i in range(nchan):
            wide = ref[i, 0:rows, :].astype(F32)
            squares = squares + wide * wide
    inverse = lax.rsqrt(jnp.sum(squares, axis=1, keepdims=True) / D + 1e-06)
    rms_out[...] = jnp.broadcast_to(inverse, rms_out.shape)
    steps = conv_out.shape[0]
    blocks = cols // LANES
    for i in range(nchan):
        for b in range(blocks):
            proj_out[i, b * NS : (b + 1) * NS, :] = same[i, :, b * LANES : (b + 1) * LANES]
    tails = (arrived[:, lay.conv : lay.conv + lay.conv_rows, :].astype(F32), other_conv[...].astype(F32))
    window = []
    for w in range(steps):
        sides = [jnp.concatenate([t[:, b * steps + w, :] for b in range(blocks)], axis=1) for t in tails]
        window.append(in_order(sides[0], sides[1], c))
    window.append(halves_dot(copies, own, other, buffer, rows) * inverse)
    mixed = jnp.zeros((rows, cols), F32)
    for w in range(steps + 1):
        mixed = mixed + window[w] * taps[w : w + 1, :]
        if w > 0:
            conv_out[w - 1] = window[w]
    mixed = mixed + offset[...]
    act = mixed / (1.0 + jnp.exp(-mixed))
    act_out[...] = act
    part = lax.dot_general(act.astype(BF16), state_proj[...], (((1,), (1,)), ((), ())), preferred_element_type=F32)
    spare = round_up(part.shape[1], LANES) - part.shape[1]
    part = jnp.concatenate([part, jnp.zeros((rows, spare), F32)], axis=1).astype(BF16)
    base = blocks * NS
    for i in range(nchan):
        for b in range(part.shape[1] // LANES):
            proj_out[i, base + b * rows : base + (b + 1) * rows, :] = part[:, b * LANES : (b + 1) * LANES]


def gates_kernel(own, other, rms, weight, out_ref, buffer, sems):
    copies = stream(weight, buffer, sems, half_starts(own))
    gate = halves_dot(copies, own, other, buffer, out_ref.shape[0]) * rms[:, 0:1]
    out_ref[...] = gate / (1.0 + jnp.exp(-gate))


def down_stream(weight, buffer, sems, halves):
    width = weight.shape[1] // 2
    pieces = sems.shape[0] // 2
    step = width // pieces
    copies = []
    for half in halves:
        for i in range(pieces):
            slot = len(copies)
            columns = pl.ds(pl.multiple_of(half * width + i * step, step), step)
            target = buffer.at[:, pl.ds(slot * step, step)]
            copies.append(pltpu.make_async_copy(weight.at[:, columns], target, sems.at[slot]))
            copies[-1].start()
    return copies


def down_product(copies, gated, buffer, outs):
    cols = outs[0].shape[2]
    step = buffer.shape[1] // len(copies)
    pieces = len(copies) // len(outs)
    for slot, copy in enumerate(copies):
        copy.wait()
        out_ref, i = outs[slot // pieces], slot % pieces
        part = jnp.dot(gated, buffer[:, slot * step : (slot + 1) * step], preferred_element_type=F32)
        part = part.astype(out_ref.dtype)
        for j in range(step // cols):
            out_ref[i * (step // cols) + j] = part[:, j * cols : (j + 1) * cols]


def scan_kernel(
    own,
    other,
    hid_other,
    act_ref,
    gate_ref,
    step_proj,
    step_bias,
    decay_log,
    skip_gain,
    weight,
    next_out,
    send_out,
    keep_out,
    turned,
    mixed,
    buffer,
    sems,
):
    c = lax.axis_index("src")
    copies = down_stream(weight, buffer, sems, (1 - c, c))
    nchan = own.shape[0]
    rows, cols = act_ref.shape
    blocks = cols // LANES
    base = blocks * NS
    summed = jnp.zeros((own.shape[1] - base, LANES), F32)
    for ref in (own, other):
        for i in range(nchan):
            summed = summed + ref[i, base:, :].astype(F32)
    parts = [summed[b * rows : (b + 1) * rows, :] for b in range(summed.shape[0] // rows)]
    low = jnp.concatenate(parts[: DTR // LANES], axis=1).astype(BF16)
    act = act_ref[...]
    raw = jnp.dot(low, step_proj[...], preferred_element_type=F32) + step_bias[...]
    step = jnp.maximum(raw, 0.0) + jnp.log1p(jnp.exp(-jnp.abs(raw)))
    turned[...] = jnp.zeros_like(turned)
    turned[0:rows, :] = own_first(parts[DTR // LANES], c)
    mats = turned[...].T
    rate = -jnp.exp(decay_log[...])
    fed = own_first(step * act, c)
    step = own_first(step, c)
    for side in range(2):
        for s in range(nchan):
            q = side * nchan + s
            place = (c if side == 0 else 1 - c) * nchan + s
            b_col = mats[0:NS, q : q + 1]
            c_col = mats[NS : 2 * NS, q : q + 1]
            for b in range(blocks):
                lanes = slice(b * LANES, (b + 1) * LANES)
                if side == 0:
                    state = own[s, b * NS : (b + 1) * NS, :].astype(F32)
                else:
                    state = hid_other[s, rows : rows + NS, lanes].astype(F32)
                after = jnp.exp(step[q : q + 1, lanes] * rate[:, lanes]) * state + fed[q : q + 1, lanes] * b_col
                next_out[place, :, lanes] = after
                mixed[q : q + 1, lanes] = jnp.sum(after * c_col, axis=0, keepdims=True)
    gated = ((own_first(mixed[...], c) + skip_gain[...] * act) * gate_ref[...]).astype(BF16)
    down_product(copies, gated, buffer, (send_out, keep_out))


def finish_kernel(final, hidden, out_ref):
    total = None
    for i in range(final.shape[0]):
        part = final[i].astype(F32)
        total = part if total is None else total + part
    out_ref[...] = (hidden[...].astype(F32) + total).astype(BF16)


def on_device(
    residual_input,
    query_heads,
    new_keyval,
    cache_pages,
    prompt_lengths,
    page_owner,
    page_index,
    mamba_state,
    conv_state,
    out_heads,
    in_values,
    in_gates,
    conv_taps,
    conv_offset,
    state_proj,
    step_proj,
    step_bias,
    decay_log,
    skip_gain,
    mamba_down,
):
    nchan = lax.axis_size("chan")
    rows, cols = residual_input.shape
    steps = conv_state.shape[1]
    held, page_tokens = cache_pages.shape[0], cache_pages.shape[1]
    lay = Chunk(nchan, held * page_tokens, cols // LANES, steps)
    call = pl.pallas_call
    shape = jax.ShapeDtypeStruct

    other_query = swap(query_heads)
    conv_rows = jnp.transpose(conv_state, (1, 0, 2))
    packed = call(
        functools.partial(pack_kernel, nchan, lay),
        out_shape=shape((nchan, lay.rows, LANES), BF16),
        in_specs=hbm(8),
        out_specs=vmem(1)[0],
        scratch_shapes=[
            VM(query_heads.shape, BF16),
            VM(query_heads.shape, BF16),
            VM(new_keyval.shape, BF16),
            VM(cache_pages.shape, BF16),
            VM(conv_rows.shape, F32),
            pltpu.SMEM(page_owner.shape, jnp.int32),
            pltpu.SMEM(page_index.shape, jnp.int32),
            pltpu.SMEM(prompt_lengths.shape, jnp.int32),
            pltpu.SemaphoreType.DMA((8,)),
        ],
        compiler_params=pltpu.CompilerParams(vmem_limit_bytes=64 * 2**20 - 2**18),
        name="pack",
    )(query_heads, other_query, new_keyval, cache_pages, conv_rows, page_owner, page_index, prompt_lengths)
    packed, residual_input, mamba_state = lax.optimization_barrier((packed, residual_input, mamba_state))
    arrived = exchange(packed)
    cut = shape((nchan, NS, cols), BF16)
    residual, same, cross = call(
        load_kernel,
        out_shape=(shape((rows, cols), BF16), cut, cut),
        in_specs=vmem(2),
        out_specs=tuple(vmem(3)),
        compiler_params=params(16),
        cost_estimate=cost(SHORT, 0),
        name="load",
    )(residual_input, mamba_state)
    arrived, residual, same, cross = lax.optimization_barrier((arrived, residual, same, cross))

    pairs = rows * lay.per
    partial, conv_send = call(
        functools.partial(attend_kernel, lay),
        out_shape=(shape((pairs, HD + LANES), F32), shape((nchan, lay.conv_rows, LANES), BF16)),
        in_specs=vmem(1),
        out_specs=tuple(vmem(2)),
        scratch_shapes=[VM((pairs, HD), F32), VM((pairs, nchan * lay.tokens), F32)],
        compiler_params=params(4 if held < 16 else 40),
        name="attend",
    )(arrived)
    other_partial = swap(partial)
    other_conv = swap(conv_send)
    other_partial, other_conv = lax.optimization_barrier((other_partial, other_conv))
    attended = call(
        functools.partial(merge_kernel, lay),
        out_shape=shape((nchan, rows, cols), BF16),
        in_specs=vmem(2),
        out_specs=vmem(1)[0],
        scratch_shapes=[VM((pairs, HD), F32)],
        compiler_params=params(4),
        name="merge",
    )(partial, other_partial)
    att_own = exchange(attended)
    att_other = swap(att_own)

    streamed = [VM((D, cols), BF16), pltpu.SemaphoreType.DMA((2 * nchan,))]
    hidden, hid_send = call(
        out_kernel,
        out_shape=(shape((rows, cols), BF16), shape((nchan, rows + NS, cols), BF16)),
        in_specs=vmem(4) + hbm(1),
        out_specs=tuple(vmem(2)),
        scratch_shapes=streamed,
        compiler_params=params(STREAM_MIB),
        name="out",
    )(att_own, att_other, residual, cross, out_heads)
    hid_own = exchange(hid_send)
    hid_other = swap(hid_own)

    sent_rows = (cols // LANES) * NS + (round_up(state_proj.shape[1], LANES) // LANES) * rows
    conv_next, act, rms, part = call(
        functools.partial(values_kernel, lay),
        out_shape=(
            shape((steps, rows, cols), F32),
            shape((rows, cols), F32),
            shape((rows, LANES), F32),
            shape((nchan, sent_rows, LANES), BF16),
        ),
        in_specs=vmem(8) + hbm(1),
        out_specs=tuple(vmem(4)),
        scratch_shapes=streamed,
        compiler_params=params(STREAM_MIB),
        name="values",
    )(hid_own, hid_other, arrived, other_conv, conv_taps, conv_offset[None, :], state_proj.T, same, in_values)
    proj_own = exchange(part)
    gate = call(
        gates_kernel,
        out_shape=shape((rows, cols), F32),
        in_specs=vmem(3) + hbm(1),
        out_specs=vmem(1)[0],
        scratch_shapes=streamed,
        compiler_params=params(STREAM_MIB),
        cost_estimate=cost(SHORT, 0),
        name="gates",
    )(hid_own, hid_other, rms, in_gates)
    proj_own, gate = lax.optimization_barrier((proj_own, gate))
    proj_other = swap(proj_own)

    down_streamed = [VM((cols, D), BF16), pltpu.SemaphoreType.DMA((8,))]
    mamba_next, send, keep = call(
        scan_kernel,
        out_shape=(
            shape((rows, NS, cols), F32),
            shape((nchan, rows, cols), BF16),
            shape((nchan, rows, cols), F32),
        ),
        in_specs=vmem(9) + hbm(1),
        out_specs=tuple(vmem(3)),
        scratch_shapes=[VM((LANES, LANES), F32), VM((rows, cols), F32)] + down_streamed,
        compiler_params=params(STREAM_MIB),
        name="scan",
    )(
        proj_own,
        proj_other,
        hid_other,
        act,
        gate,
        step_proj,
        step_bias[None, :],
        decay_log,
        skip_gain[None, :],
        mamba_down,
    )
    taken = swap(send)
    summed = (keep + taken.astype(F32)).astype(BF16)
    hidden_out = call(
        finish_kernel,
        out_shape=shape((rows, cols), BF16),
        in_specs=vmem(2),
        out_specs=vmem(1)[0],
        compiler_params=params(4),
        name="finish",
    )(exchange(summed), hidden)
    return (hidden_out, mamba_next, jnp.transpose(conv_next, (1, 0, 2)))


def solution(mesh):
    owners = ("groups", "src", "chan")
    channels = ("src", "chan")
    placed = (
        P("groups", channels),
        P(owners, None),
        P(owners, None),
        P(owners, None, None),
        P("groups"),
        P(owners),
        P(owners),
        P(owners, None, None),
        P(owners, None, None),
        P(None, channels),
        P(None, channels),
        P(None, channels),
        P(None, channels),
        P(channels),
        P(channels, None),
        P(None, channels),
        P(channels),
        P(None, channels),
        P(channels),
        P(channels, None),
    )
    return jax.shard_map(
        on_device,
        mesh=mesh,
        in_specs=placed,
        out_specs=(P("groups", channels), P("groups", None, channels), P("groups", None, channels)),
        check_vma=False,
    )
```

```python
import functools
import math

import jax
import jax.numpy as jnp
from jax import lax
from jax.experimental import pallas as pl
from jax.experimental.pallas import tpu as pltpu
from jax.sharding import PartitionSpec as P

D = 8192
NS = 16
DTR = 512
QH = 64
KVH = 8
HD = 128
G = QH // KVH
LANES = 128
NEGATIVE = -1e30
LOWEST = -1e20
STREAM_MIB = 50
DOWN_READY = 1
SHORT = 3 * 10**9
F32 = jnp.float32
BF16 = jnp.bfloat16
VM = pltpu.VMEM


def round_up(value, step):
    return -(-value // step) * step


def vmem(count):
    return [pl.BlockSpec(memory_space=pltpu.VMEM)] * count


def smem(count):
    return [pl.BlockSpec(memory_space=pltpu.SMEM)] * count


def hbm(count):
    return [pl.BlockSpec(memory_space=pltpu.HBM)] * count


def params(mib):
    return pltpu.CompilerParams(vmem_limit_bytes=mib * 2**20)


def cost(flops, nbytes):
    return pl.CostEstimate(flops=flops, bytes_accessed=nbytes, transcendentals=0)


def swap(x):
    return lax.ppermute(x, "src", [(0, 1), (1, 0)])


def exchange(x):
    return lax.all_to_all(x, "chan", split_axis=0, concat_axis=0, tiled=True)


class Chunk:
    def __init__(self, nchan, held_tokens, blocks, steps):
        self.per = QH // nchan
        self.tokens = held_tokens
        self.owner_rows = held_tokens // LANES
        self.value = held_tokens
        self.misc = 2 * held_tokens
        self.query = self.misc + round_up(2 + self.owner_rows, 16)
        self.conv = self.query + round_up(2 * self.per, 16)
        self.conv_rows = round_up(steps * blocks, 16)
        self.rows = self.conv + 2 * self.conv_rows


def pack_kernel(
    nchan,
    lay,
    query_hbm,
    other_hbm,
    newkv_hbm,
    pages_hbm,
    conv_hbm,
    owner_hbm,
    index_hbm,
    lengths_hbm,
    out_ref,
    query,
    other_query,
    newkv,
    pages,
    conv,
    owners,
    indexes,
    lengths,
    sems,
):
    moves = (
        (pages_hbm, pages),
        (conv_hbm, conv),
        (query_hbm, query),
        (other_hbm, other_query),
        (newkv_hbm, newkv),
        (owner_hbm, owners),
        (index_hbm, indexes),
        (lengths_hbm, lengths),
    )
    copies = [pltpu.make_async_copy(src, dst, sems.at[i]) for i, (src, dst) in enumerate(moves)]
    for copy in copies:
        copy.start()
    c = lax.axis_index("src")
    page_tokens = pages.shape[1]
    cols = conv.shape[2] // (2 * nchan)
    blocks = cols // LANES
    steps = conv.shape[0]
    rep = nchan // KVH
    for copy in copies[1:]:
        copy.wait()
    lane = lax.broadcasted_iota(jnp.int32, (1, LANES), 1)
    per_row = LANES // page_tokens
    owner_rows = []
    for i in range(lay.owner_rows):
        found = jnp.full((1, LANES), -1, jnp.int32)
        for j in range(per_row):
            owner = owners[i * per_row + j]
            left = lengths[owner] - indexes[i * per_row + j] * page_tokens
            found = jnp.where((lane // page_tokens == j) & (lane % page_tokens < left), owner, found)
        owner_rows.append(found.astype(F32))
    fill = lay.query - lay.misc - 2 - lay.owner_rows
    owner_rows.append(jnp.zeros((fill, LANES), F32))
    for d in range(nchan):
        at = (d // rep) * HD
        fresh = [newkv[0:1, x : x + HD].astype(F32) for x in (at, KVH * HD + at)]
        out_ref[d, lay.misc : lay.query, :] = jnp.concatenate(fresh + owner_rows, axis=0).astype(BF16)
        heads = []
        for ref in (query, other_query):
            for h in range(lay.per):
                place = (d * lay.per + h) * HD
                heads.append(ref[0:1, place : place + HD].astype(F32))
        spare = lay.conv - lay.query - len(heads)
        if spare:
            heads.append(jnp.zeros((spare, LANES), F32))
        out_ref[d, lay.query : lay.conv, :] = jnp.concatenate(heads, axis=0).astype(BF16)
    for side in range(2):
        first = (c if side == 0 else 1 - c) * (nchan * cols)
        for d in range(nchan):
            rows = []
            for b in range(blocks):
                lanes = pl.ds(pl.multiple_of(first + d * cols + b * LANES, LANES), LANES)
                for w in range(steps):
                    rows.append(conv[w, 0:1, lanes])
            rows.append(jnp.zeros((lay.conv_rows - len(rows), LANES), F32))
            base = lay.conv + side * lay.conv_rows
            out_ref[d, base : base + lay.conv_rows, :] = jnp.concatenate(rows, axis=0).astype(BF16)
    copies[0].wait()
    for d in range(nchan):
        at = (d // rep) * HD
        out_ref[d, 0 : lay.tokens, :] = pages[:, :, at : at + HD].reshape(lay.tokens, HD)
        at = KVH * HD + at
        out_ref[d, lay.value : lay.misc, :] = pages[:, :, at : at + HD].reshape(lay.tokens, HD)


def load_kernel(residual, state, residual_out, same, cross):
    c = lax.axis_index("src")
    nchan, _, cols = same.shape
    residual_out[...] = residual[...]
    for ref, half in ((same, c), (cross, 1 - c)):
        for d in range(nchan):
            lanes = pl.ds(pl.multiple_of((half * nchan + d) * cols, cols), cols)
            ref[d] = state[0, :, lanes].astype(BF16)


def attend_kernel(lay, recv, out_ref, conv_own, conv_out, queries, scores):
    nchan = recv.shape[0]
    per, tokens = lay.per, lay.tokens
    c = lax.axis_index("src")
    count = nchan * per
    scale = 1.0 / math.sqrt(HD)
    contract = (((1,), (1,)), ((), ()))
    new_keys, new_values, owners = [], [], []
    for s in range(nchan):
        conv_own[s] = recv[s, lay.conv : lay.conv + lay.conv_rows, :]
        conv_out[s] = recv[s, lay.conv + lay.conv_rows : lay.rows, :]
        heads = recv[s, lay.query : lay.conv, :].astype(F32)
        queries[s * per : (s + 1) * per, :] = heads[0:per, :]
        queries[count + s * per : count + (s + 1) * per, :] = heads[per : 2 * per, :]
        misc = recv[s, lay.misc : lay.query, :].astype(F32)
        new_keys.append(misc[0:1, :])
        new_values.append(misc[1:2, :])
        owners.append(jnp.concatenate([misc[2 + i : 3 + i, :] for i in range(lay.owner_rows)], axis=1))
    fill = round_up(nchan, 16) - nchan
    if fill:
        new_keys.append(jnp.zeros((fill, HD), F32))
        new_values.append(jnp.zeros((fill, HD), F32))
    new_keys = jnp.concatenate(new_keys, axis=0).astype(BF16)
    new_values = jnp.concatenate(new_values, axis=0).astype(BF16)
    row = lax.broadcasted_iota(jnp.int32, (2 * count, 1), 0)
    side = jnp.where(row < count, c, 1 - c)
    request = side * nchan + (row % count) // per
    lane = lax.broadcasted_iota(jnp.int32, (1, nchan + fill), 1)
    new_owner = jnp.where(lane < nchan, c * nchan + lane, -1)
    q = queries[...].astype(BF16)
    new_scores = lax.dot_general(q, new_keys, contract, preferred_element_type=F32) * scale
    new_scores = jnp.where(request == new_owner, new_scores, NEGATIVE)
    wide = request.astype(F32)
    highest = None
    for s in range(nchan):
        part = lax.dot_general(q, recv[s, 0:tokens, :], contract, preferred_element_type=F32) * scale
        part = jnp.where(wide == owners[s], part, NEGATIVE)
        scores[:, s * tokens : (s + 1) * tokens] = part
        highest = part if highest is None else jnp.maximum(highest, part)
    peak = jnp.maximum(jnp.max(highest, axis=1, keepdims=True), jnp.max(new_scores, axis=1, keepdims=True))
    peak = jnp.maximum(peak, LOWEST)
    new_weight = jnp.exp(new_scores - peak)
    numer = jnp.dot(new_weight.astype(BF16), new_values, preferred_element_type=F32)
    summed = None
    for s in range(nchan):
        weight = jnp.exp(scores[:, s * tokens : (s + 1) * tokens] - peak)
        summed = weight if summed is None else summed + weight
        numer = numer + jnp.dot(weight.astype(BF16), recv[s, lay.value : lay.misc, :], preferred_element_type=F32)
    total = jnp.sum(summed, axis=1, keepdims=True) + jnp.sum(new_weight, axis=1, keepdims=True)
    out_ref[:, 0:HD] = numer
    lane = lax.broadcasted_iota(jnp.int32, (1, LANES), 1)
    out_ref[:, HD : HD + LANES] = jnp.where(lane == 0, peak, total)


def in_order(own, other, c):
    return jnp.where(c == 0, jnp.concatenate([own, other], axis=0), jnp.concatenate([other, own], axis=0))


def own_first(x, c):
    half = x.shape[0] // 2
    return in_order(x[:half], x[half:], c)


def merge_kernel(lay, own, other, out_ref, result):
    nchan = out_ref.shape[0]
    c = lax.axis_index("src")
    count = nchan * lay.per
    theirs = jnp.concatenate([other[count:, :], other[:count, :]], axis=0)
    ours = own[...]
    top = jnp.maximum(ours[:, HD : HD + 1], theirs[:, HD : HD + 1])
    numer, denom = 0.0, 0.0
    for part in (ours, theirs):
        factor = jnp.exp(part[:, HD : HD + 1] - top)
        numer = numer + factor * part[:, 0:HD]
        denom = denom + factor * part[:, HD + 1 : HD + 2]
    result[...] = numer / denom
    share = lay.per // 2
    for h in range(share):
        head = c * share + h
        mine = result[pl.ds(head, nchan, stride=lay.per), :]
        rest = result[pl.ds(count + head, nchan, stride=lay.per), :]
        block = in_order(mine, rest, c).astype(BF16)
        for i in range(nchan):
            out_ref[i, :, h * HD : (h + 1) * HD] = block


def stream(weight, buffer, sems, starts):
    depth = buffer.shape[0] // len(starts)
    copies = []
    for i, start in enumerate(starts):
        rows = pl.ds(pl.multiple_of(start, depth), depth)
        copies.append(pltpu.make_async_copy(weight.at[rows, :], buffer.at[pl.ds(i * depth, depth), :], sems.at[i]))
        copies[-1].start()
    return copies


def row_starts(nchan, depth, by_chip, own):
    c = lax.axis_index("src")
    half = c if own else 1 - c
    return [((2 * i + half) if by_chip else (half * nchan + i)) * depth for i in range(nchan)]


def fetch_kernel(nchan, by_chip, weight, out_ref, sems):
    depth = weight.shape[0] // (2 * nchan)
    starts = row_starts(nchan, depth, by_chip, False)[: out_ref.shape[0] // depth]
    for copy in stream(weight, out_ref, sems, starts):
        copy.wait()


def exchange_and_fetch(x, weight, by_chip, share, name):
    x, weight = lax.optimization_barrier((x, weight))
    received = exchange(x)
    nchan = x.shape[0]
    fetched = pl.pallas_call(
        functools.partial(fetch_kernel, nchan, by_chip),
        out_shape=jax.ShapeDtypeStruct((weight.shape[0] // share, weight.shape[1]), weight.dtype),
        in_specs=hbm(1),
        out_specs=vmem(1)[0],
        scratch_shapes=[pltpu.SemaphoreType.DMA((2 * nchan // share,))],
        compiler_params=params(STREAM_MIB),
        cost_estimate=cost(SHORT, 0),
        name=name,
    )(weight)
    return lax.optimization_barrier((received, fetched))


def own_kernel(by_chip, lhs, weight, out_ref, buffer, sems):
    nchan, depth = lhs.shape[0], lhs.shape[2]
    copies = stream(weight, buffer, sems, row_starts(nchan, depth, by_chip, True))
    total = None
    for i, copy in enumerate(copies):
        copy.wait()
        part = jnp.dot(
            lhs[i, 0 : out_ref.shape[0], :], buffer[i * depth : (i + 1) * depth, :], preferred_element_type=F32
        )
        total = part if total is None else total + part
    out_ref[...] = total


def rest_start(by_chip, lhs, fetched, weight, buffer, sems):
    nchan, depth = lhs.shape[0], lhs.shape[2]
    ready = fetched.shape[0] // depth
    return stream(weight, buffer, sems, row_starts(nchan, depth, by_chip, False)[ready:])


def rest_dot(copies, lhs, total, fetched, buffer):
    depth, rows = lhs.shape[2], total.shape[0]
    ready = fetched.shape[0] // depth
    for i in range(lhs.shape[0]):
        if i < ready:
            block = fetched[i * depth : (i + 1) * depth, :]
        else:
            copies[i - ready].wait()
            block = buffer[(i - ready) * depth : (i - ready + 1) * depth, :]
        total = total + jnp.dot(lhs[i, 0:rows, :], block, preferred_element_type=F32)
    return total


def halves_dot(copies, own, other, buffer, count):
    nchan, depth = own.shape[0], own.shape[2]
    total = None
    for i, copy in enumerate(copies):
        ref = own if i < nchan else other
        copy.wait()
        part = jnp.dot(ref[i % nchan, 0:count, :], buffer[i * depth : (i + 1) * depth, :], preferred_element_type=F32)
        total = part if total is None else total + part
    return total


def out_kernel(lhs, partial, residual, cross, fetched, weight, hidden_out, out_ref, buffer, sems):
    copies = rest_start(True, lhs, fetched, weight, buffer, sems)
    nchan, rows, _ = lhs.shape
    for i in range(nchan):
        out_ref[i, rows : rows + NS, :] = cross[i]
    product = rest_dot(copies, lhs, partial[...], fetched, buffer)
    hidden = (residual[...].astype(F32) + product).astype(BF16)
    hidden_out[...] = hidden
    for i in range(nchan):
        out_ref[i, 0:rows, :] = hidden


def values_kernel(
    lay, own, other, own_conv, other_conv, taps, offset, state_proj, same, partial, fetched, weight,
    conv_out, act_out, rms_out, proj_out, buffer, sems,
):
    copies = rest_start(False, other, fetched, weight, buffer, sems)
    c = lax.axis_index("src")
    nchan = own.shape[0]
    rows, cols = act_out.shape
    squares = jnp.zeros((rows, own.shape[2]), F32)
    for ref in (own, other):
        for i in range(nchan):
            wide = ref[i, 0:rows, :].astype(F32)
            squares = squares + wide * wide
    inverse = lax.rsqrt(jnp.sum(squares, axis=1, keepdims=True) / D + 1e-06)
    rms_out[...] = jnp.broadcast_to(inverse, rms_out.shape)
    steps = conv_out.shape[0]
    blocks = cols // LANES
    for i in range(nchan):
        for b in range(blocks):
            proj_out[i, b * NS : (b + 1) * NS, :] = same[i, :, b * LANES : (b + 1) * LANES]
    tails = (own_conv[...].astype(F32), other_conv[...].astype(F32))
    window = []
    for w in range(steps):
        sides = [jnp.concatenate([t[:, b * steps + w, :] for b in range(blocks)], axis=1) for t in tails]
        window.append(in_order(sides[0], sides[1], c))
    window.append(rest_dot(copies, other, partial[...], fetched, buffer) * inverse)
    mixed = jnp.zeros((rows, cols), F32)
    for w in range(steps + 1):
        mixed = mixed + window[w] * taps[w : w + 1, :]
        if w > 0:
            conv_out[w - 1] = window[w]
    mixed = mixed + offset[...]
    act = mixed / (1.0 + jnp.exp(-mixed))
    act_out[...] = act
    part = lax.dot_general(act.astype(BF16), state_proj[...], (((1,), (1,)), ((), ())), preferred_element_type=F32)
    spare = round_up(part.shape[1], LANES) - part.shape[1]
    part = jnp.concatenate([part, jnp.zeros((rows, spare), F32)], axis=1).astype(BF16)
    base = blocks * NS
    for i in range(nchan):
        for b in range(part.shape[1] // LANES):
            proj_out[i, base + b * rows : base + (b + 1) * rows, :] = part[:, b * LANES : (b + 1) * LANES]


def gates_kernel(own, other, rms, weight, down_hbm, out_ref, down_out, buffer, sems, down_sems):
    nchan, depth = own.shape[0], own.shape[2]
    copies = stream(
        weight,
        buffer,
        sems,
        row_starts(nchan, depth, False, True) + row_starts(nchan, depth, False, False),
    )
    part_down = down_stream(down_hbm, down_out, down_sems, (1 - lax.axis_index("src"),), 0)
    gate = halves_dot(copies, own, other, buffer, out_ref.shape[0]) * rms[:, 0:1]
    out_ref[...] = gate / (1.0 + jnp.exp(-gate))
    for copy in part_down:
        copy.wait()


def down_stream(weight, buffer, sems, halves, first):
    width = weight.shape[1] // 2
    step = buffer.shape[1] // sems.shape[0]
    blocks = [(half, i) for half in halves for i in range(width // step)]
    copies = []
    for half, i in blocks[first : first + sems.shape[0]]:
        slot = len(copies)
        columns = pl.ds(pl.multiple_of(half * width + i * step, step), step)
        target = buffer.at[:, pl.ds(slot * step, step)]
        copies.append(pltpu.make_async_copy(weight.at[:, columns], target, sems.at[slot]))
        copies[-1].start()
    return copies


def down_product(copies, gated, fetched, buffer, outs):
    cols = outs[0].shape[2]
    step = buffer.shape[1] // len(copies)
    ready = fetched.shape[1] // step
    pieces = (ready + len(copies)) // len(outs)
    for slot in range(ready + len(copies)):
        if slot < ready:
            block = fetched[:, slot * step : (slot + 1) * step]
        else:
            copies[slot - ready].wait()
            block = buffer[:, (slot - ready) * step : (slot - ready + 1) * step]
        out_ref, i = outs[slot // pieces], slot % pieces
        part = jnp.dot(gated, block, preferred_element_type=F32).astype(out_ref.dtype)
        for j in range(step // cols):
            out_ref[i * (step // cols) + j] = part[:, j * cols : (j + 1) * cols]


def scan_kernel(
    own,
    other,
    hid_other,
    act_ref,
    gate_ref,
    step_proj,
    step_bias,
    decay_log,
    skip_gain,
    fetched,
    weight,
    next_hbm,
    send_out,
    keep_out,
    turned,
    mixed,
    next_out,
    buffer,
    sems,
    save_sem,
):
    c = lax.axis_index("src")
    copies = down_stream(weight, buffer, sems, (1 - c, c), DOWN_READY)
    nchan = own.shape[0]
    rows, cols = act_ref.shape
    blocks = cols // LANES
    base = blocks * NS
    summed = jnp.zeros((own.shape[1] - base, LANES), F32)
    for ref in (own, other):
        for i in range(nchan):
            summed = summed + ref[i, base:, :].astype(F32)
    parts = [summed[b * rows : (b + 1) * rows, :] for b in range(summed.shape[0] // rows)]
    low = jnp.concatenate(parts[: DTR // LANES], axis=1).astype(BF16)
    act = act_ref[...]
    raw = jnp.dot(low, step_proj[...], preferred_element_type=F32) + step_bias[...]
    step = jnp.maximum(raw, 0.0) + jnp.log1p(jnp.exp(-jnp.abs(raw)))
    turned[...] = jnp.zeros_like(turned)
    turned[0:rows, :] = own_first(parts[DTR // LANES], c)
    mats = turned[...].T
    rate = -jnp.exp(decay_log[...])
    fed = own_first(step * act, c)
    step = own_first(step, c)
    for side in range(2):
        for s in range(nchan):
            q = side * nchan + s
            place = (c if side == 0 else 1 - c) * nchan + s
            b_col = mats[0:NS, q : q + 1]
            c_col = mats[NS : 2 * NS, q : q + 1]
            for b in range(blocks):
                lanes = slice(b * LANES, (b + 1) * LANES)
                if side == 0:
                    state = own[s, b * NS : (b + 1) * NS, :].astype(F32)
                else:
                    state = hid_other[s, rows : rows + NS, lanes].astype(F32)
                after = jnp.exp(step[q : q + 1, lanes] * rate[:, lanes]) * state + fed[q : q + 1, lanes] * b_col
                next_out[place, :, lanes] = after
                mixed[q : q + 1, lanes] = jnp.sum(after * c_col, axis=0, keepdims=True)
    save = pltpu.make_async_copy(next_out, next_hbm, save_sem)
    save.start()
    gated = ((own_first(mixed[...], c) + skip_gain[...] * act) * gate_ref[...]).astype(BF16)
    down_product(copies, gated, fetched, buffer, (send_out, keep_out))
    save.wait()


def finish_kernel(final, hidden, out_ref):
    total = None
    for i in range(final.shape[0]):
        part = final[i].astype(F32)
        total = part if total is None else total + part
    out_ref[...] = (hidden[...].astype(F32) + total).astype(BF16)


def on_device(
    residual_input,
    query_heads,
    new_keyval,
    cache_pages,
    prompt_lengths,
    page_owner,
    page_index,
    mamba_state,
    conv_state,
    out_heads,
    in_values,
    in_gates,
    conv_taps,
    conv_offset,
    state_proj,
    step_proj,
    step_bias,
    decay_log,
    skip_gain,
    mamba_down,
):
    nchan = lax.axis_size("chan")
    rows, cols = residual_input.shape
    steps = conv_state.shape[1]
    held, page_tokens = cache_pages.shape[0], cache_pages.shape[1]
    lay = Chunk(nchan, held * page_tokens, cols // LANES, steps)
    call = pl.pallas_call
    shape = jax.ShapeDtypeStruct

    other_query = swap(query_heads)
    conv_rows = jnp.transpose(conv_state, (1, 0, 2))
    packed = call(
        functools.partial(pack_kernel, nchan, lay),
        out_shape=shape((nchan, lay.rows, LANES), BF16),
        in_specs=hbm(8),
        out_specs=vmem(1)[0],
        scratch_shapes=[
            VM(query_heads.shape, BF16),
            VM(query_heads.shape, BF16),
            VM(new_keyval.shape, BF16),
            VM(cache_pages.shape, BF16),
            VM(conv_rows.shape, F32),
            pltpu.SMEM(page_owner.shape, jnp.int32),
            pltpu.SMEM(page_index.shape, jnp.int32),
            pltpu.SMEM(prompt_lengths.shape, jnp.int32),
            pltpu.SemaphoreType.DMA((8,)),
        ],
        compiler_params=pltpu.CompilerParams(vmem_limit_bytes=64 * 2**20 - 2**18),
        name="pack",
    )(query_heads, other_query, new_keyval, cache_pages, conv_rows, page_owner, page_index, prompt_lengths)
    packed, residual_input, mamba_state = lax.optimization_barrier((packed, residual_input, mamba_state))
    arrived = exchange(packed)
    cut = shape((nchan, NS, cols), BF16)
    residual, same, cross = call(
        load_kernel,
        out_shape=(shape((rows, cols), BF16), cut, cut),
        in_specs=vmem(2),
        out_specs=tuple(vmem(3)),
        compiler_params=params(16),
        cost_estimate=cost(SHORT, 0),
        name="load",
    )(residual_input, mamba_state)
    arrived, residual, same, cross = lax.optimization_barrier((arrived, residual, same, cross))

    pairs = rows * lay.per
    conv_cut = shape((nchan, lay.conv_rows, LANES), BF16)
    partial, conv_own, conv_send = call(
        functools.partial(attend_kernel, lay),
        out_shape=(shape((pairs, HD + LANES), F32), conv_cut, conv_cut),
        in_specs=vmem(1),
        out_specs=tuple(vmem(3)),
        scratch_shapes=[VM((pairs, HD), F32), VM((pairs, nchan * lay.tokens), F32)],
        compiler_params=params(4 if held < 16 else 40),
        name="attend",
    )(arrived)
    other_partial = swap(partial)
    other_conv = swap(conv_send)
    other_partial, other_conv = lax.optimization_barrier((other_partial, other_conv))
    attended = call(
        functools.partial(merge_kernel, lay),
        out_shape=shape((nchan, rows, cols), BF16),
        in_specs=vmem(2),
        out_specs=vmem(1)[0],
        scratch_shapes=[VM((pairs, HD), F32)],
        compiler_params=params(4),
        name="merge",
    )(partial, other_partial)
    att_own, out_fetched = exchange_and_fetch(attended, out_heads, True, 4, "fetch_out")
    att_other = swap(att_own)
    half_streamed = [VM((D // 2, cols), BF16), pltpu.SemaphoreType.DMA((nchan,))]
    rest_streamed = [VM((D // 4, cols), BF16), pltpu.SemaphoreType.DMA((nchan // 2,))]

    def own_product(x, weight, by_chip, name):
        return call(
            functools.partial(own_kernel, by_chip),
            out_shape=shape((rows, cols), F32),
            in_specs=vmem(1) + hbm(1),
            out_specs=vmem(1)[0],
            scratch_shapes=half_streamed,
            compiler_params=params(STREAM_MIB),
            cost_estimate=cost(SHORT, 0),
            name=name,
        )(x, weight)

    out_partial = own_product(att_own, out_heads, True, "out_own")

    streamed = [VM((D, cols), BF16), pltpu.SemaphoreType.DMA((2 * nchan,))]
    hidden, hid_send = call(
        out_kernel,
        out_shape=(shape((rows, cols), BF16), shape((nchan, rows + NS, cols), BF16)),
        in_specs=vmem(5) + hbm(1),
        out_specs=tuple(vmem(2)),
        scratch_shapes=rest_streamed,
        compiler_params=params(STREAM_MIB),
        name="out",
    )(att_other, out_partial, residual, cross, out_fetched, out_heads)
    hid_own, values_fetched = exchange_and_fetch(hid_send, in_values, False, 4, "fetch_values")
    hid_other = swap(hid_own)
    values_partial = own_product(hid_own, in_values, False, "values_own")

    sent_rows = (cols // LANES) * NS + (round_up(state_proj.shape[1], LANES) // LANES) * rows
    conv_next, act, rms, part = call(
        functools.partial(values_kernel, lay),
        out_shape=(
            shape((steps, rows, cols), F32),
            shape((rows, cols), F32),
            shape((rows, LANES), F32),
            shape((nchan, sent_rows, LANES), BF16),
        ),
        in_specs=vmem(10) + hbm(1),
        out_specs=tuple(vmem(4)),
        scratch_shapes=[VM((D // 2 - D // 4, cols), BF16), pltpu.SemaphoreType.DMA((nchan - 2 * nchan // 4,))],
        compiler_params=params(STREAM_MIB),
        name="values",
    )(hid_own, hid_other, conv_own, other_conv, conv_taps, conv_offset[None, :], state_proj.T, same, values_partial, values_fetched, in_values)
    part, down_weight = lax.optimization_barrier((part, mamba_down))
    proj_own = exchange(part)
    pieces = 8
    piece = D // pieces
    gate, down_fetched = call(
        gates_kernel,
        out_shape=(shape((rows, cols), F32), shape((cols, DOWN_READY * piece), BF16)),
        in_specs=vmem(3) + hbm(2),
        out_specs=tuple(vmem(2)),
        scratch_shapes=streamed + [pltpu.SemaphoreType.DMA((DOWN_READY,))],
        compiler_params=params(STREAM_MIB),
        cost_estimate=cost(SHORT, 0),
        name="gates",
    )(hid_own, hid_other, rms, in_gates, down_weight)
    proj_own, gate, down_fetched = lax.optimization_barrier((proj_own, gate, down_fetched))
    proj_other = swap(proj_own)

    down_streamed = [
        VM((rows, NS, cols), F32),
        VM((cols, D - DOWN_READY * piece), BF16),
        pltpu.SemaphoreType.DMA((pieces - DOWN_READY,)),
        pltpu.SemaphoreType.DMA,
    ]
    mamba_next, send, keep = call(
        scan_kernel,
        out_shape=(
            shape((rows, NS, cols), F32),
            shape((nchan, rows, cols), BF16),
            shape((nchan, rows, cols), F32),
        ),
        in_specs=vmem(10) + hbm(1),
        out_specs=tuple(hbm(1) + vmem(2)),
        scratch_shapes=[VM((LANES, LANES), F32), VM((rows, cols), F32)] + down_streamed,
        compiler_params=params(STREAM_MIB),
        name="scan",
    )(
        proj_own,
        proj_other,
        hid_other,
        act,
        gate,
        step_proj,
        step_bias[None, :],
        decay_log,
        skip_gain[None, :],
        down_fetched,
        mamba_down,
    )
    taken = swap(send)
    summed = (keep + taken.astype(F32)).astype(BF16)
    hidden_out = call(
        finish_kernel,
        out_shape=shape((rows, cols), BF16),
        in_specs=vmem(2),
        out_specs=vmem(1)[0],
        compiler_params=params(4),
        name="finish",
    )(exchange(summed), hidden)
    return (hidden_out, mamba_next, jnp.transpose(conv_next, (1, 0, 2)))


def solution(mesh):
    owners = ("groups", "src", "chan")
    channels = ("src", "chan")
    placed = (
        P("groups", channels),
        P(owners, None),
        P(owners, None),
        P(owners, None, None),
        P("groups"),
        P(owners),
        P(owners),
        P(owners, None, None),
        P(owners, None, None),
        P(None, channels),
        P(None, channels),
        P(None, channels),
        P(None, channels),
        P(channels),
        P(channels, None),
        P(None, channels),
        P(channels),
        P(None, channels),
        P(channels),
        P(channels, None),
    )
    return jax.shard_map(
        on_device,
        mesh=mesh,
        in_specs=placed,
        out_specs=(P("groups", channels), P("groups", None, channels), P("groups", None, channels)),
        check_vma=False,
    )
```

```python
import functools
import math

import jax
import jax.numpy as jnp
from jax import lax
from jax.experimental import pallas as pl
from jax.experimental.pallas import tpu as pltpu
from jax.sharding import PartitionSpec as P

D = 8192
NS = 16
DTR = 512
QH = 64
KVH = 8
HD = 128
G = QH // KVH
LANES = 128
NEGATIVE = -1e30
LOWEST = -1e20
STREAM_MIB = 50
DOWN_READY = 1
SHORT = 3 * 10**9
F32 = jnp.float32
BF16 = jnp.bfloat16
VM = pltpu.VMEM


def round_up(value, step):
    return -(-value // step) * step


def vmem(count):
    return [pl.BlockSpec(memory_space=pltpu.VMEM)] * count


def smem(count):
    return [pl.BlockSpec(memory_space=pltpu.SMEM)] * count


def hbm(count):
    return [pl.BlockSpec(memory_space=pltpu.HBM)] * count


def params(mib):
    return pltpu.CompilerParams(vmem_limit_bytes=mib * 2**20)


def cost(flops, nbytes):
    return pl.CostEstimate(flops=flops, bytes_accessed=nbytes, transcendentals=0)


def swap(x):
    return lax.ppermute(x, "src", [(0, 1), (1, 0)])


def exchange(x):
    return lax.all_to_all(x, "chan", split_axis=0, concat_axis=0, tiled=True)


class Chunk:
    def __init__(self, nchan, held_tokens, blocks, steps):
        self.per = QH // nchan
        self.tokens = held_tokens
        self.owner_rows = held_tokens // LANES
        self.value = held_tokens
        self.misc = 2 * held_tokens
        self.query = self.misc + round_up(2 + self.owner_rows, 16)
        self.conv = self.query + round_up(2 * self.per, 16)
        self.conv_rows = round_up(steps * blocks, 16)
        self.rows = self.conv + 2 * self.conv_rows


def pack_kernel(
    nchan,
    lay,
    query_hbm,
    other_hbm,
    newkv_hbm,
    pages_hbm,
    conv_hbm,
    owner_hbm,
    index_hbm,
    lengths_hbm,
    out_ref,
    query,
    other_query,
    newkv,
    pages,
    conv,
    owners,
    indexes,
    lengths,
    sems,
):
    moves = (
        (pages_hbm, pages),
        (conv_hbm, conv),
        (query_hbm, query),
        (other_hbm, other_query),
        (newkv_hbm, newkv),
        (owner_hbm, owners),
        (index_hbm, indexes),
        (lengths_hbm, lengths),
    )
    copies = [pltpu.make_async_copy(src, dst, sems.at[i]) for i, (src, dst) in enumerate(moves)]
    for copy in copies:
        copy.start()
    c = lax.axis_index("src")
    page_tokens = pages.shape[1]
    cols = conv.shape[2] // (2 * nchan)
    blocks = cols // LANES
    steps = conv.shape[0]
    rep = nchan // KVH
    for copy in copies[1:]:
        copy.wait()
    lane = lax.broadcasted_iota(jnp.int32, (1, LANES), 1)
    per_row = LANES // page_tokens
    owner_rows = []
    for i in range(lay.owner_rows):
        found = jnp.full((1, LANES), -1, jnp.int32)
        for j in range(per_row):
            owner = owners[i * per_row + j]
            left = lengths[owner] - indexes[i * per_row + j] * page_tokens
            found = jnp.where((lane // page_tokens == j) & (lane % page_tokens < left), owner, found)
        owner_rows.append(found.astype(F32))
    fill = lay.query - lay.misc - 2 - lay.owner_rows
    owner_rows.append(jnp.zeros((fill, LANES), F32))
    for d in range(nchan):
        at = (d // rep) * HD
        fresh = [newkv[0:1, x : x + HD].astype(F32) for x in (at, KVH * HD + at)]
        out_ref[d, lay.misc : lay.query, :] = jnp.concatenate(fresh + owner_rows, axis=0).astype(BF16)
        heads = []
        for ref in (query, other_query):
            for h in range(lay.per):
                place = (d * lay.per + h) * HD
                heads.append(ref[0:1, place : place + HD].astype(F32))
        spare = lay.conv - lay.query - len(heads)
        if spare:
            heads.append(jnp.zeros((spare, LANES), F32))
        out_ref[d, lay.query : lay.conv, :] = jnp.concatenate(heads, axis=0).astype(BF16)
    for side in range(2):
        first = (c if side == 0 else 1 - c) * (nchan * cols)
        for d in range(nchan):
            rows = []
            for b in range(blocks):
                lanes = pl.ds(pl.multiple_of(first + d * cols + b * LANES, LANES), LANES)
                for w in range(steps):
                    rows.append(conv[w, 0:1, lanes])
            rows.append(jnp.zeros((lay.conv_rows - len(rows), LANES), F32))
            base = lay.conv + side * lay.conv_rows
            out_ref[d, base : base + lay.conv_rows, :] = jnp.concatenate(rows, axis=0).astype(BF16)
    copies[0].wait()
    for d in range(nchan):
        at = (d // rep) * HD
        out_ref[d, 0 : lay.tokens, :] = pages[:, :, at : at + HD].reshape(lay.tokens, HD)
        at = KVH * HD + at
        out_ref[d, lay.value : lay.misc, :] = pages[:, :, at : at + HD].reshape(lay.tokens, HD)


def load_kernel(residual, state, residual_out, same, cross):
    c = lax.axis_index("src")
    nchan, _, cols = same.shape
    residual_out[...] = residual[...]
    for ref, half in ((same, c), (cross, 1 - c)):
        for d in range(nchan):
            lanes = pl.ds(pl.multiple_of((half * nchan + d) * cols, cols), cols)
            ref[d] = state[0, :, lanes].astype(BF16)


def attend_kernel(lay, recv, out_ref, conv_own, conv_out, queries, scores):
    nchan = recv.shape[0]
    per, tokens = lay.per, lay.tokens
    c = lax.axis_index("src")
    count = nchan * per
    scale = 1.0 / math.sqrt(HD)
    contract = (((1,), (1,)), ((), ()))
    new_keys, new_values, owners = [], [], []
    for s in range(nchan):
        conv_own[s] = recv[s, lay.conv : lay.conv + lay.conv_rows, :]
        conv_out[s] = recv[s, lay.conv + lay.conv_rows : lay.rows, :]
        heads = recv[s, lay.query : lay.conv, :].astype(F32)
        queries[s * per : (s + 1) * per, :] = heads[0:per, :]
        queries[count + s * per : count + (s + 1) * per, :] = heads[per : 2 * per, :]
        misc = recv[s, lay.misc : lay.query, :].astype(F32)
        new_keys.append(misc[0:1, :])
        new_values.append(misc[1:2, :])
        owners.append(jnp.concatenate([misc[2 + i : 3 + i, :] for i in range(lay.owner_rows)], axis=1))
    fill = round_up(nchan, 16) - nchan
    if fill:
        new_keys.append(jnp.zeros((fill, HD), F32))
        new_values.append(jnp.zeros((fill, HD), F32))
    new_keys = jnp.concatenate(new_keys, axis=0).astype(BF16)
    new_values = jnp.concatenate(new_values, axis=0).astype(BF16)
    row = lax.broadcasted_iota(jnp.int32, (2 * count, 1), 0)
    side = jnp.where(row < count, c, 1 - c)
    request = side * nchan + (row % count) // per
    lane = lax.broadcasted_iota(jnp.int32, (1, nchan + fill), 1)
    new_owner = jnp.where(lane < nchan, c * nchan + lane, -1)
    q = queries[...].astype(BF16)
    new_scores = lax.dot_general(q, new_keys, contract, preferred_element_type=F32) * scale
    new_scores = jnp.where(request == new_owner, new_scores, NEGATIVE)
    wide = request.astype(F32)
    highest = None
    for s in range(nchan):
        part = lax.dot_general(q, recv[s, 0:tokens, :], contract, preferred_element_type=F32) * scale
        part = jnp.where(wide == owners[s], part, NEGATIVE)
        scores[:, s * tokens : (s + 1) * tokens] = part
        highest = part if highest is None else jnp.maximum(highest, part)
    peak = jnp.maximum(jnp.max(highest, axis=1, keepdims=True), jnp.max(new_scores, axis=1, keepdims=True))
    peak = jnp.maximum(peak, LOWEST)
    new_weight = jnp.exp(new_scores - peak)
    numer = jnp.dot(new_weight.astype(BF16), new_values, preferred_element_type=F32)
    summed = None
    for s in range(nchan):
        weight = jnp.exp(scores[:, s * tokens : (s + 1) * tokens] - peak)
        summed = weight if summed is None else summed + weight
        numer = numer + jnp.dot(weight.astype(BF16), recv[s, lay.value : lay.misc, :], preferred_element_type=F32)
    total = jnp.sum(summed, axis=1, keepdims=True) + jnp.sum(new_weight, axis=1, keepdims=True)
    out_ref[:, 0:HD] = numer
    lane = lax.broadcasted_iota(jnp.int32, (1, LANES), 1)
    out_ref[:, HD : HD + LANES] = jnp.where(lane == 0, peak, total)


def in_order(own, other, c):
    return jnp.where(c == 0, jnp.concatenate([own, other], axis=0), jnp.concatenate([other, own], axis=0))


def own_first(x, c):
    half = x.shape[0] // 2
    return in_order(x[:half], x[half:], c)


def merge_kernel(lay, own, other, out_ref, result):
    nchan = out_ref.shape[0]
    c = lax.axis_index("src")
    count = nchan * lay.per
    theirs = jnp.concatenate([other[count:, :], other[:count, :]], axis=0)
    ours = own[...]
    top = jnp.maximum(ours[:, HD : HD + 1], theirs[:, HD : HD + 1])
    numer, denom = 0.0, 0.0
    for part in (ours, theirs):
        factor = jnp.exp(part[:, HD : HD + 1] - top)
        numer = numer + factor * part[:, 0:HD]
        denom = denom + factor * part[:, HD + 1 : HD + 2]
    result[...] = numer / denom
    share = lay.per // 2
    for h in range(share):
        head = c * share + h
        mine = result[pl.ds(head, nchan, stride=lay.per), :]
        rest = result[pl.ds(count + head, nchan, stride=lay.per), :]
        block = in_order(mine, rest, c).astype(BF16)
        for i in range(nchan):
            out_ref[i, :, h * HD : (h + 1) * HD] = block


def stream(weight, buffer, sems, starts):
    depth = buffer.shape[0] // len(starts)
    copies = []
    for i, start in enumerate(starts):
        rows = pl.ds(pl.multiple_of(start, depth), depth)
        copies.append(pltpu.make_async_copy(weight.at[rows, :], buffer.at[pl.ds(i * depth, depth), :], sems.at[i]))
        copies[-1].start()
    return copies


def row_starts(nchan, depth, by_chip, own):
    c = lax.axis_index("src")
    half = c if own else 1 - c
    return [((2 * i + half) if by_chip else (half * nchan + i)) * depth for i in range(nchan)]


def half_dot(copies, lhs, total, buffer, rows):
    depth = lhs.shape[2]
    for i, copy in enumerate(copies):
        copy.wait()
        block = buffer[i * depth : (i + 1) * depth, :]
        part = jnp.dot(lhs[i, 0:rows, :], block, preferred_element_type=F32)
        total = part if total is None else total + part
    return total


def own_kernel(by_chip, lhs, weight, out_ref, buffer, sems):
    nchan, depth = lhs.shape[0], lhs.shape[2]
    copies = stream(weight, buffer, sems, row_starts(nchan, depth, by_chip, True))
    out_ref[...] = half_dot(copies, lhs, None, buffer, out_ref.shape[0])


def halves_dot(copies, own, other, buffer, count):
    nchan, depth = own.shape[0], own.shape[2]
    total = None
    for i, copy in enumerate(copies):
        ref = own if i < nchan else other
        copy.wait()
        part = jnp.dot(ref[i % nchan, 0:count, :], buffer[i * depth : (i + 1) * depth, :], preferred_element_type=F32)
        total = part if total is None else total + part
    return total


def out_kernel(lhs, partial, residual, cross, weight, hidden_out, out_ref, buffer, sems):
    nchan, rows, depth = lhs.shape
    copies = stream(weight, buffer, sems, row_starts(nchan, depth, True, False))
    for i in range(nchan):
        out_ref[i, rows : rows + NS, :] = cross[i]
    product = half_dot(copies, lhs, partial[...], buffer, rows)
    hidden = (residual[...].astype(F32) + product).astype(BF16)
    hidden_out[...] = hidden
    for i in range(nchan):
        out_ref[i, 0:rows, :] = hidden


def values_kernel(
    lay, own, other, own_conv, other_conv, taps, offset, state_proj, same, partial, weight,
    conv_out, act_out, rms_out, proj_out, buffer, sems,
):
    copies = stream(weight, buffer, sems, row_starts(own.shape[0], own.shape[2], False, False))
    c = lax.axis_index("src")
    nchan = own.shape[0]
    rows, cols = act_out.shape
    squares = jnp.zeros((rows, own.shape[2]), F32)
    for ref in (own, other):
        for i in range(nchan):
            wide = ref[i, 0:rows, :].astype(F32)
            squares = squares + wide * wide
    inverse = lax.rsqrt(jnp.sum(squares, axis=1, keepdims=True) / D + 1e-06)
    rms_out[...] = jnp.broadcast_to(inverse, rms_out.shape)
    steps = conv_out.shape[0]
    blocks = cols // LANES
    for i in range(nchan):
        for b in range(blocks):
            proj_out[i, b * NS : (b + 1) * NS, :] = same[i, :, b * LANES : (b + 1) * LANES]
    tails = (own_conv[...].astype(F32), other_conv[...].astype(F32))
    window = []
    for w in range(steps):
        sides = [jnp.concatenate([t[:, b * steps + w, :] for b in range(blocks)], axis=1) for t in tails]
        window.append(in_order(sides[0], sides[1], c))
    window.append(half_dot(copies, other, partial[...], buffer, rows) * inverse)
    mixed = jnp.zeros((rows, cols), F32)
    for w in range(steps + 1):
        mixed = mixed + window[w] * taps[w : w + 1, :]
        if w > 0:
            conv_out[w - 1] = window[w]
    mixed = mixed + offset[...]
    act = mixed / (1.0 + jnp.exp(-mixed))
    act_out[...] = act
    part = lax.dot_general(act.astype(BF16), state_proj[...], (((1,), (1,)), ((), ())), preferred_element_type=F32)
    spare = round_up(part.shape[1], LANES) - part.shape[1]
    part = jnp.concatenate([part, jnp.zeros((rows, spare), F32)], axis=1).astype(BF16)
    base = blocks * NS
    for i in range(nchan):
        for b in range(part.shape[1] // LANES):
            proj_out[i, base + b * rows : base + (b + 1) * rows, :] = part[:, b * LANES : (b + 1) * LANES]


def gates_kernel(own, other, rms, weight, down_hbm, out_ref, down_out, buffer, sems, down_sems):
    nchan, depth = own.shape[0], own.shape[2]
    copies = stream(
        weight,
        buffer,
        sems,
        row_starts(nchan, depth, False, True) + row_starts(nchan, depth, False, False),
    )
    part_down = down_stream(down_hbm, down_out, down_sems, (1 - lax.axis_index("src"),), 0)
    gate = halves_dot(copies, own, other, buffer, out_ref.shape[0]) * rms[:, 0:1]
    out_ref[...] = gate / (1.0 + jnp.exp(-gate))
    for copy in part_down:
        copy.wait()


def down_stream(weight, buffer, sems, halves, first):
    width = weight.shape[1] // 2
    step = buffer.shape[1] // sems.shape[0]
    blocks = [(half, i) for half in halves for i in range(width // step)]
    copies = []
    for half, i in blocks[first : first + sems.shape[0]]:
        slot = len(copies)
        columns = pl.ds(pl.multiple_of(half * width + i * step, step), step)
        target = buffer.at[:, pl.ds(slot * step, step)]
        copies.append(pltpu.make_async_copy(weight.at[:, columns], target, sems.at[slot]))
        copies[-1].start()
    return copies


def down_product(copies, gated, fetched, buffer, out_ref):
    cols = out_ref.shape[2]
    step = buffer.shape[1] // len(copies)
    ready = 0 if fetched is None else fetched.shape[1] // step
    each = step // cols
    for slot in range(ready + len(copies)):
        if slot < ready:
            block = fetched[:, slot * step : (slot + 1) * step]
        else:
            copies[slot - ready].wait()
            block = buffer[:, (slot - ready) * step : (slot - ready + 1) * step]
        part = jnp.dot(gated, block, preferred_element_type=F32).astype(out_ref.dtype)
        for j in range(each):
            out_ref[slot * each + j] = part[:, j * cols : (j + 1) * cols]


def scan_kernel(
    own,
    other,
    hid_other,
    act_ref,
    gate_ref,
    step_proj,
    step_bias,
    decay_log,
    skip_gain,
    fetched,
    weight,
    next_hbm,
    gated_out,
    send_out,
    turned,
    mixed,
    next_out,
    buffer,
    sems,
    save_sem,
):
    c = lax.axis_index("src")
    copies = down_stream(weight, buffer, sems, (1 - c,), DOWN_READY)
    nchan = own.shape[0]
    rows, cols = act_ref.shape
    blocks = cols // LANES
    base = blocks * NS
    summed = jnp.zeros((own.shape[1] - base, LANES), F32)
    for ref in (own, other):
        for i in range(nchan):
            summed = summed + ref[i, base:, :].astype(F32)
    parts = [summed[b * rows : (b + 1) * rows, :] for b in range(summed.shape[0] // rows)]
    low = jnp.concatenate(parts[: DTR // LANES], axis=1).astype(BF16)
    act = act_ref[...]
    raw = jnp.dot(low, step_proj[...], preferred_element_type=F32) + step_bias[...]
    step = jnp.maximum(raw, 0.0) + jnp.log1p(jnp.exp(-jnp.abs(raw)))
    turned[...] = jnp.zeros_like(turned)
    turned[0:rows, :] = own_first(parts[DTR // LANES], c)
    mats = turned[...].T
    rate = -jnp.exp(decay_log[...])
    fed = own_first(step * act, c)
    step = own_first(step, c)
    for side in range(2):
        for s in range(nchan):
            q = side * nchan + s
            place = (c if side == 0 else 1 - c) * nchan + s
            b_col = mats[0:NS, q : q + 1]
            c_col = mats[NS : 2 * NS, q : q + 1]
            for b in range(blocks):
                lanes = slice(b * LANES, (b + 1) * LANES)
                if side == 0:
                    state = own[s, b * NS : (b + 1) * NS, :].astype(F32)
                else:
                    state = hid_other[s, rows : rows + NS, lanes].astype(F32)
                after = jnp.exp(step[q : q + 1, lanes] * rate[:, lanes]) * state + fed[q : q + 1, lanes] * b_col
                next_out[place, :, lanes] = after
                mixed[q : q + 1, lanes] = jnp.sum(after * c_col, axis=0, keepdims=True)
    save = pltpu.make_async_copy(next_out, next_hbm, save_sem)
    save.start()
    gated = ((own_first(mixed[...], c) + skip_gain[...] * act) * gate_ref[...]).astype(BF16)
    gated_out[...] = gated
    down_product(copies, gated, fetched, buffer, send_out)
    save.wait()


def down_kernel(gated, weight, out_ref, buffer, sems):
    copies = down_stream(weight, buffer, sems, (lax.axis_index("src"),), 0)
    down_product(copies, gated[...], None, buffer, out_ref)


def finish_kernel(final, hidden, out_ref):
    total = None
    for i in range(final.shape[0]):
        part = final[i].astype(F32)
        total = part if total is None else total + part
    out_ref[...] = (hidden[...].astype(F32) + total).astype(BF16)


def on_device(
    residual_input,
    query_heads,
    new_keyval,
    cache_pages,
    prompt_lengths,
    page_owner,
    page_index,
    mamba_state,
    conv_state,
    out_heads,
    in_values,
    in_gates,
    conv_taps,
    conv_offset,
    state_proj,
    step_proj,
    step_bias,
    decay_log,
    skip_gain,
    mamba_down,
):
    nchan = lax.axis_size("chan")
    rows, cols = residual_input.shape
    steps = conv_state.shape[1]
    held, page_tokens = cache_pages.shape[0], cache_pages.shape[1]
    lay = Chunk(nchan, held * page_tokens, cols // LANES, steps)
    call = pl.pallas_call
    shape = jax.ShapeDtypeStruct

    other_query = swap(query_heads)
    conv_rows = jnp.transpose(conv_state, (1, 0, 2))
    packed = call(
        functools.partial(pack_kernel, nchan, lay),
        out_shape=shape((nchan, lay.rows, LANES), BF16),
        in_specs=hbm(8),
        out_specs=vmem(1)[0],
        scratch_shapes=[
            VM(query_heads.shape, BF16),
            VM(query_heads.shape, BF16),
            VM(new_keyval.shape, BF16),
            VM(cache_pages.shape, BF16),
            VM(conv_rows.shape, F32),
            pltpu.SMEM(page_owner.shape, jnp.int32),
            pltpu.SMEM(page_index.shape, jnp.int32),
            pltpu.SMEM(prompt_lengths.shape, jnp.int32),
            pltpu.SemaphoreType.DMA((8,)),
        ],
        compiler_params=pltpu.CompilerParams(vmem_limit_bytes=64 * 2**20 - 2**18),
        name="pack",
    )(query_heads, other_query, new_keyval, cache_pages, conv_rows, page_owner, page_index, prompt_lengths)
    packed, residual_input, mamba_state = lax.optimization_barrier((packed, residual_input, mamba_state))
    arrived = exchange(packed)
    cut = shape((nchan, NS, cols), BF16)
    residual, same, cross = call(
        load_kernel,
        out_shape=(shape((rows, cols), BF16), cut, cut),
        in_specs=vmem(2),
        out_specs=tuple(vmem(3)),
        compiler_params=params(16),
        cost_estimate=cost(SHORT, 0),
        name="load",
    )(residual_input, mamba_state)
    arrived, residual, same, cross = lax.optimization_barrier((arrived, residual, same, cross))

    pairs = rows * lay.per
    conv_cut = shape((nchan, lay.conv_rows, LANES), BF16)
    partial, conv_own, conv_send = call(
        functools.partial(attend_kernel, lay),
        out_shape=(shape((pairs, HD + LANES), F32), conv_cut, conv_cut),
        in_specs=vmem(1),
        out_specs=tuple(vmem(3)),
        scratch_shapes=[VM((pairs, HD), F32), VM((pairs, nchan * lay.tokens), F32)],
        compiler_params=params(4 if held < 16 else 40),
        name="attend",
    )(arrived)
    other_partial = swap(partial)
    other_conv = swap(conv_send)
    other_partial, other_conv = lax.optimization_barrier((other_partial, other_conv))
    attended = call(
        functools.partial(merge_kernel, lay),
        out_shape=shape((nchan, rows, cols), BF16),
        in_specs=vmem(2),
        out_specs=vmem(1)[0],
        scratch_shapes=[VM((pairs, HD), F32)],
        compiler_params=params(4),
        name="merge",
    )(partial, other_partial)
    att_own = exchange(attended)
    att_other = swap(att_own)
    half_streamed = [VM((D // 2, cols), BF16), pltpu.SemaphoreType.DMA((nchan,))]

    def own_product(x, weight, by_chip, name):
        return call(
            functools.partial(own_kernel, by_chip),
            out_shape=shape((rows, cols), F32),
            in_specs=vmem(1) + hbm(1),
            out_specs=vmem(1)[0],
            scratch_shapes=half_streamed,
            compiler_params=params(STREAM_MIB),
            cost_estimate=cost(SHORT, 0),
            name=name,
        )(x, weight)

    out_partial = own_product(att_own, out_heads, True, "out_own")

    streamed = [VM((D, cols), BF16), pltpu.SemaphoreType.DMA((2 * nchan,))]
    hidden, hid_send = call(
        out_kernel,
        out_shape=(shape((rows, cols), BF16), shape((nchan, rows + NS, cols), BF16)),
        in_specs=vmem(4) + hbm(1),
        out_specs=tuple(vmem(2)),
        scratch_shapes=half_streamed,
        compiler_params=params(STREAM_MIB),
        name="out",
    )(att_other, out_partial, residual, cross, out_heads)
    hid_own = exchange(hid_send)
    hid_other = swap(hid_own)
    values_partial = own_product(hid_own, in_values, False, "values_own")

    sent_rows = (cols // LANES) * NS + (round_up(state_proj.shape[1], LANES) // LANES) * rows
    conv_next, act, rms, part = call(
        functools.partial(values_kernel, lay),
        out_shape=(
            shape((steps, rows, cols), F32),
            shape((rows, cols), F32),
            shape((rows, LANES), F32),
            shape((nchan, sent_rows, LANES), BF16),
        ),
        in_specs=vmem(9) + hbm(1),
        out_specs=tuple(vmem(4)),
        scratch_shapes=half_streamed,
        compiler_params=params(STREAM_MIB),
        name="values",
    )(hid_own, hid_other, conv_own, other_conv, conv_taps, conv_offset[None, :], state_proj.T, same, values_partial, in_values)
    part, down_weight = lax.optimization_barrier((part, mamba_down))
    proj_own = exchange(part)
    pieces = 8
    piece = D // pieces
    gate, down_fetched = call(
        gates_kernel,
        out_shape=(shape((rows, cols), F32), shape((cols, DOWN_READY * piece), BF16)),
        in_specs=vmem(3) + hbm(2),
        out_specs=tuple(vmem(2)),
        scratch_shapes=streamed + [pltpu.SemaphoreType.DMA((DOWN_READY,))],
        compiler_params=params(STREAM_MIB),
        cost_estimate=cost(SHORT, 0),
        name="gates",
    )(hid_own, hid_other, rms, in_gates, down_weight)
    proj_own, gate, down_fetched = lax.optimization_barrier((proj_own, gate, down_fetched))
    proj_other = swap(proj_own)

    down_streamed = [
        VM((rows, NS, cols), F32),
        VM((cols, D // 2 - DOWN_READY * piece), BF16),
        pltpu.SemaphoreType.DMA((pieces // 2 - DOWN_READY,)),
        pltpu.SemaphoreType.DMA,
    ]
    mamba_next, gated, send = call(
        scan_kernel,
        out_shape=(
            shape((rows, NS, cols), F32),
            shape((rows, cols), BF16),
            shape((nchan, rows, cols), BF16),
        ),
        in_specs=vmem(10) + hbm(1),
        out_specs=tuple(hbm(1) + vmem(2)),
        scratch_shapes=[VM((LANES, LANES), F32), VM((rows, cols), F32)] + down_streamed,
        compiler_params=params(STREAM_MIB),
        name="scan",
    )(
        proj_own,
        proj_other,
        hid_other,
        act,
        gate,
        step_proj,
        step_bias[None, :],
        decay_log,
        skip_gain[None, :],
        down_fetched,
        mamba_down,
    )
    taken = swap(send)
    keep = call(
        down_kernel,
        out_shape=shape((nchan, rows, cols), F32),
        in_specs=vmem(1) + hbm(1),
        out_specs=vmem(1)[0],
        scratch_shapes=[VM((cols, D // 2), BF16), pltpu.SemaphoreType.DMA((pieces // 2,))],
        compiler_params=params(STREAM_MIB),
        cost_estimate=cost(SHORT, 0),
        name="down",
    )(gated, mamba_down)
    summed = (keep + taken.astype(F32)).astype(BF16)
    hidden_out = call(
        finish_kernel,
        out_shape=shape((rows, cols), BF16),
        in_specs=vmem(2),
        out_specs=vmem(1)[0],
        compiler_params=params(4),
        name="finish",
    )(exchange(summed), hidden)
    return (hidden_out, mamba_next, jnp.transpose(conv_next, (1, 0, 2)))


def solution(mesh):
    owners = ("groups", "src", "chan")
    channels = ("src", "chan")
    placed = (
        P("groups", channels),
        P(owners, None),
        P(owners, None),
        P(owners, None, None),
        P("groups"),
        P(owners),
        P(owners),
        P(owners, None, None),
        P(owners, None, None),
        P(None, channels),
        P(None, channels),
        P(None, channels),
        P(None, channels),
        P(channels),
        P(channels, None),
        P(None, channels),
        P(channels),
        P(None, channels),
        P(channels),
        P(channels, None),
    )
    return jax.shard_map(
        on_device,
        mesh=mesh,
        in_specs=placed,
        out_specs=(P("groups", channels), P("groups", None, channels), P("groups", None, channels)),
        check_vma=False,
    )
```

```python
import functools
import math

import jax
import jax.numpy as jnp
from jax import lax
from jax.experimental import pallas as pl
from jax.experimental.pallas import tpu as pltpu
from jax.sharding import PartitionSpec as P

D = 8192
NS = 16
DTR = 512
QH = 64
KVH = 8
HD = 128
G = QH // KVH
LANES = 128
NEGATIVE = -1e30
STREAM_MIB = 50
DOWN_READY = 1
SHORT = 3 * 10**9
F32 = jnp.float32
BF16 = jnp.bfloat16
VM = pltpu.VMEM


def round_up(value, step):
    return -(-value // step) * step


def vmem(count):
    return [pl.BlockSpec(memory_space=pltpu.VMEM)] * count


def smem(count):
    return [pl.BlockSpec(memory_space=pltpu.SMEM)] * count


def hbm(count):
    return [pl.BlockSpec(memory_space=pltpu.HBM)] * count


def params(mib):
    return pltpu.CompilerParams(vmem_limit_bytes=mib * 2**20)


def cost(flops, nbytes):
    return pl.CostEstimate(flops=flops, bytes_accessed=nbytes, transcendentals=0)


def swap(x):
    return lax.ppermute(x, "src", [(0, 1), (1, 0)])


def exchange(x):
    return lax.all_to_all(x, "chan", split_axis=0, concat_axis=0, tiled=True)


class Chunk:
    def __init__(self, nchan, held_tokens, blocks, steps):
        self.per = QH // nchan
        self.tokens = held_tokens
        self.owner_rows = held_tokens // LANES
        self.value = held_tokens
        self.small = 2 * held_tokens
        self.query = 2 + self.owner_rows
        self.conv = self.query + self.per
        self.conv_rows = steps * blocks
        self.small_rows = round_up(self.conv + 2 * self.conv_rows, 16)
        self.rows = self.small + self.small_rows


def pack_kernel(
    nchan,
    lay,
    query_hbm,
    newkv_hbm,
    pages_hbm,
    conv_hbm,
    owner_hbm,
    index_hbm,
    lengths_hbm,
    out_ref,
    query,
    newkv,
    pages,
    conv,
    owners,
    indexes,
    lengths,
    sems,
):
    moves = (
        (pages_hbm, pages),
        (conv_hbm, conv),
        (query_hbm, query),
        (newkv_hbm, newkv),
        (owner_hbm, owners),
        (index_hbm, indexes),
        (lengths_hbm, lengths),
    )
    copies = [pltpu.make_async_copy(src, dst, sems.at[i]) for i, (src, dst) in enumerate(moves)]
    for copy in copies:
        copy.start()
    c = lax.axis_index("src")
    page_tokens = pages.shape[1]
    cols = conv.shape[2] // (2 * nchan)
    blocks = cols // LANES
    steps = conv.shape[0]
    rep = nchan // KVH
    for copy in copies[1:]:
        copy.wait()
    lane = lax.broadcasted_iota(jnp.int32, (1, LANES), 1)
    per_row = LANES // page_tokens
    owner_rows = []
    for i in range(lay.owner_rows):
        found = jnp.full((1, LANES), -1, jnp.int32)
        for j in range(per_row):
            owner = owners[i * per_row + j]
            left = lengths[owner] - indexes[i * per_row + j] * page_tokens
            found = jnp.where((lane // page_tokens == j) & (lane % page_tokens < left), owner, found)
        owner_rows.append(found.astype(F32))
    for d in range(nchan):
        at = (d // rep) * HD
        small = [newkv[0:1, x : x + HD].astype(F32) for x in (at, KVH * HD + at)] + owner_rows
        for h in range(lay.per):
            place = (d * lay.per + h) * HD
            small.append(query[0:1, place : place + HD].astype(F32))
        for half in (c, 1 - c):
            first = (half * nchan + d) * cols
            for b in range(blocks):
                lanes = pl.ds(pl.multiple_of(first + b * LANES, LANES), LANES)
                for w in range(steps):
                    small.append(conv[w, 0:1, lanes])
        if lay.small_rows > len(small):
            small.append(jnp.zeros((lay.small_rows - len(small), LANES), F32))
        out_ref[d, lay.small : lay.rows, :] = jnp.concatenate(small, axis=0).astype(BF16)
    copies[0].wait()
    for d in range(nchan):
        at = (d // rep) * HD
        out_ref[d, 0 : lay.tokens, :] = pages[:, :, at : at + HD].reshape(lay.tokens, HD)
        at = KVH * HD + at
        out_ref[d, lay.value : lay.small, :] = pages[:, :, at : at + HD].reshape(lay.tokens, HD)


def load_kernel(residual, state, residual_out, same, cross):
    c = lax.axis_index("src")
    nchan, _, cols = same.shape
    residual_out[...] = residual[...]
    for ref, half in ((same, c), (cross, 1 - c)):
        for d in range(nchan):
            lanes = pl.ds(pl.multiple_of((half * nchan + d) * cols, cols), cols)
            ref[d] = state[0, :, lanes].astype(BF16)


def attend_kernel(lay, recv, other, out_ref, conv_own, conv_other, queries, scores, result):
    nchan = recv.shape[0]
    per, tokens = lay.per, lay.tokens
    c = lax.axis_index("src")
    count = nchan * per
    scale = 1.0 / math.sqrt(HD)
    contract = (((1,), (1,)), ((), ()))
    new_keys, new_values, owners = [], [], []
    spare = conv_own.shape[1] - lay.conv_rows
    for ref, conv_out, at in ((recv, conv_own, lay.conv), (other, conv_other, lay.conv + lay.conv_rows)):
        for s in range(nchan):
            small = ref[s, lay.small : lay.rows, :].astype(F32)
            conv = small[at : at + lay.conv_rows, :]
            conv_out[s] = jnp.concatenate([conv, jnp.zeros((spare, LANES), F32)], axis=0) if spare else conv
            owners.append(jnp.concatenate([small[2 + i : 3 + i, :] for i in range(lay.owner_rows)], axis=1))
            if ref is recv:
                queries[s * per : (s + 1) * per, :] = small[lay.query : lay.query + per, :]
                new_keys.append(small[0:1, :])
                new_values.append(small[1:2, :])
    fill = round_up(nchan, 16) - nchan
    if fill:
        new_keys.append(jnp.zeros((fill, HD), F32))
        new_values.append(jnp.zeros((fill, HD), F32))
    new_keys = jnp.concatenate(new_keys, axis=0).astype(BF16)
    new_values = jnp.concatenate(new_values, axis=0).astype(BF16)
    place = lax.broadcasted_iota(jnp.int32, (count, 1), 0) // per
    lane = lax.broadcasted_iota(jnp.int32, (1, nchan + fill), 1)
    q = queries[...].astype(BF16)
    new_scores = lax.dot_general(q, new_keys, contract, preferred_element_type=F32) * scale
    new_scores = jnp.where(place == lane, new_scores, NEGATIVE)
    wide = (c * nchan + place).astype(F32)
    sources = [(ref, s) for ref in (recv, other) for s in range(nchan)]
    highest = None
    for i, (ref, s) in enumerate(sources):
        part = lax.dot_general(q, ref[s, 0:tokens, :], contract, preferred_element_type=F32) * scale
        part = jnp.where(wide == owners[i], part, NEGATIVE)
        scores[:, i * tokens : (i + 1) * tokens] = part
        highest = part if highest is None else jnp.maximum(highest, part)
    peak = jnp.maximum(jnp.max(highest, axis=1, keepdims=True), jnp.max(new_scores, axis=1, keepdims=True))
    new_weight = jnp.exp(new_scores - peak)
    numer = jnp.dot(new_weight.astype(BF16), new_values, preferred_element_type=F32)
    summed = None
    for i, (ref, s) in enumerate(sources):
        weight = jnp.exp(scores[:, i * tokens : (i + 1) * tokens] - peak)
        summed = weight if summed is None else summed + weight
        numer = numer + jnp.dot(weight.astype(BF16), ref[s, lay.value : lay.small, :], preferred_element_type=F32)
    total = jnp.sum(summed, axis=1, keepdims=True) + jnp.sum(new_weight, axis=1, keepdims=True)
    result[...] = numer / total
    heads = [result[pl.ds(h, nchan, stride=per), :] for h in range(per)]
    block = jnp.concatenate(heads, axis=0).astype(BF16)
    for i in range(nchan):
        out_ref[i] = block


def in_order(own, other, c):
    return jnp.where(c == 0, jnp.concatenate([own, other], axis=0), jnp.concatenate([other, own], axis=0))


def own_first(x, c):
    half = x.shape[0] // 2
    return in_order(x[:half], x[half:], c)


def stream(weight, buffer, sems, starts):
    depth = buffer.shape[0] // len(starts)
    copies = []
    for i, start in enumerate(starts):
        rows = pl.ds(pl.multiple_of(start, depth), depth)
        copies.append(pltpu.make_async_copy(weight.at[rows, :], buffer.at[pl.ds(i * depth, depth), :], sems.at[i]))
        copies[-1].start()
    return copies


def row_starts(nchan, depth, own):
    c = lax.axis_index("src")
    half = c if own else 1 - c
    return [(half * nchan + i) * depth for i in range(nchan)]


def half_dot(copies, lhs, total, buffer, rows):
    depth = lhs.shape[2]
    for i, copy in enumerate(copies):
        copy.wait()
        block = buffer[i * depth : (i + 1) * depth, :]
        part = jnp.dot(lhs[i, 0:rows, :], block, preferred_element_type=F32)
        total = part if total is None else total + part
    return total


def own_kernel(lhs, weight, out_ref, buffer, sems):
    nchan, depth = lhs.shape[0], lhs.shape[2]
    copies = stream(weight, buffer, sems, row_starts(nchan, depth, True))
    out_ref[...] = half_dot(copies, lhs, None, buffer, out_ref.shape[0])


def halves_dot(copies, own, other, buffer, count):
    nchan, depth = own.shape[0], own.shape[2]
    total = None
    for i, copy in enumerate(copies):
        ref = own if i < nchan else other
        copy.wait()
        part = jnp.dot(ref[i % nchan, 0:count, :], buffer[i * depth : (i + 1) * depth, :], preferred_element_type=F32)
        total = part if total is None else total + part
    return total


def fetch_kernel(weight, out_ref, sems):
    depth = out_ref.shape[0] // sems.shape[0]
    for copy in stream(weight, out_ref, sems, [i * depth for i in range(sems.shape[0])]):
        copy.wait()


def out_kernel(lay, own, other, residual, cross, fetched, weight, hidden_out, out_ref, buffer, sems):
    c = lax.axis_index("src")
    nchan, rows = own.shape[0], residual.shape[0]
    depth = lay.per * HD
    ready = fetched.shape[0] // depth
    copies = stream(weight, buffer, sems, [i * depth for i in range(ready, nchan)])
    for i in range(nchan):
        out_ref[i, rows : rows + NS, :] = cross[i]
    product = residual[...].astype(F32)
    for i in range(nchan):
        mine, rest = own[i].astype(F32), other[i].astype(F32)
        heads = [slice(h * nchan, (h + 1) * nchan) for h in range(lay.per)]
        lhs = jnp.concatenate([in_order(mine[h], rest[h], c) for h in heads], axis=1).astype(BF16)
        if i < ready:
            block = fetched[i * depth : (i + 1) * depth, :]
        else:
            copies[i - ready].wait()
            block = buffer[(i - ready) * depth : (i - ready + 1) * depth, :]
        product = product + jnp.dot(lhs, block, preferred_element_type=F32)
    hidden = product.astype(BF16)
    hidden_out[...] = hidden
    for i in range(nchan):
        out_ref[i, 0:rows, :] = hidden


def values_kernel(
    lay, own, other, own_conv, other_conv, taps, offset, state_proj, same, partial, weight,
    conv_out, act_out, rms_out, proj_out, buffer, sems,
):
    copies = stream(weight, buffer, sems, row_starts(own.shape[0], own.shape[2], False))
    c = lax.axis_index("src")
    nchan = own.shape[0]
    rows, cols = act_out.shape
    squares = jnp.zeros((rows, own.shape[2]), F32)
    for ref in (own, other):
        for i in range(nchan):
            wide = ref[i, 0:rows, :].astype(F32)
            squares = squares + wide * wide
    inverse = lax.rsqrt(jnp.sum(squares, axis=1, keepdims=True) / D + 1e-06)
    rms_out[...] = jnp.broadcast_to(inverse, rms_out.shape)
    steps = conv_out.shape[0]
    blocks = cols // LANES
    for i in range(nchan):
        for b in range(blocks):
            proj_out[i, b * NS : (b + 1) * NS, :] = same[i, :, b * LANES : (b + 1) * LANES]
    tails = (own_conv[...], other_conv[...])
    window = []
    for w in range(steps):
        sides = [jnp.concatenate([t[:, b * steps + w, :] for b in range(blocks)], axis=1) for t in tails]
        window.append(in_order(sides[0], sides[1], c))
    window.append(half_dot(copies, other, partial[...], buffer, rows) * inverse)
    mixed = jnp.zeros((rows, cols), F32)
    for w in range(steps + 1):
        mixed = mixed + window[w] * taps[w : w + 1, :]
        if w > 0:
            conv_out[w - 1] = window[w]
    mixed = mixed + offset[...]
    act = mixed / (1.0 + jnp.exp(-mixed))
    act_out[...] = act
    part = lax.dot_general(act.astype(BF16), state_proj[...], (((1,), (1,)), ((), ())), preferred_element_type=F32)
    spare = round_up(part.shape[1], LANES) - part.shape[1]
    part = jnp.concatenate([part, jnp.zeros((rows, spare), F32)], axis=1).astype(BF16)
    base = blocks * NS
    for i in range(nchan):
        for b in range(part.shape[1] // LANES):
            proj_out[i, base + b * rows : base + (b + 1) * rows, :] = part[:, b * LANES : (b + 1) * LANES]


def gates_kernel(own, other, rms, weight, down_hbm, out_ref, down_out, buffer, sems, down_sems):
    nchan, depth = own.shape[0], own.shape[2]
    copies = stream(
        weight,
        buffer,
        sems,
        row_starts(nchan, depth, True) + row_starts(nchan, depth, False),
    )
    part_down = down_stream(down_hbm, down_out, down_sems, (1 - lax.axis_index("src"),), 0)
    gate = halves_dot(copies, own, other, buffer, out_ref.shape[0]) * rms[:, 0:1]
    out_ref[...] = gate / (1.0 + jnp.exp(-gate))
    for copy in part_down:
        copy.wait()


def down_stream(weight, buffer, sems, halves, first):
    width = weight.shape[1] // 2
    step = buffer.shape[1] // sems.shape[0]
    blocks = [(half, i) for half in halves for i in range(width // step)]
    copies = []
    for half, i in blocks[first : first + sems.shape[0]]:
        slot = len(copies)
        columns = pl.ds(pl.multiple_of(half * width + i * step, step), step)
        target = buffer.at[:, pl.ds(slot * step, step)]
        copies.append(pltpu.make_async_copy(weight.at[:, columns], target, sems.at[slot]))
        copies[-1].start()
    return copies


def down_product(copies, gated, fetched, buffer, out_ref):
    cols = out_ref.shape[2]
    step = buffer.shape[1] // len(copies)
    ready = 0 if fetched is None else fetched.shape[1] // step
    each = step // cols
    for slot in range(ready + len(copies)):
        if slot < ready:
            block = fetched[:, slot * step : (slot + 1) * step]
        else:
            copies[slot - ready].wait()
            block = buffer[:, (slot - ready) * step : (slot - ready + 1) * step]
        part = jnp.dot(gated, block, preferred_element_type=F32).astype(out_ref.dtype)
        for j in range(each):
            out_ref[slot * each + j] = part[:, j * cols : (j + 1) * cols]


def scan_kernel(
    own,
    other,
    hid_other,
    act_ref,
    gate_ref,
    step_proj,
    step_bias,
    decay_log,
    skip_gain,
    fetched,
    weight,
    next_hbm,
    gated_out,
    send_out,
    turned,
    mixed,
    next_out,
    buffer,
    sems,
    save_sem,
):
    c = lax.axis_index("src")
    copies = down_stream(weight, buffer, sems, (1 - c,), DOWN_READY)
    nchan = own.shape[0]
    rows, cols = act_ref.shape
    blocks = cols // LANES
    base = blocks * NS
    summed = jnp.zeros((own.shape[1] - base, LANES), F32)
    for ref in (own, other):
        for i in range(nchan):
            summed = summed + ref[i, base:, :].astype(F32)
    parts = [summed[b * rows : (b + 1) * rows, :] for b in range(summed.shape[0] // rows)]
    low = jnp.concatenate(parts[: DTR // LANES], axis=1).astype(BF16)
    act = act_ref[...]
    raw = jnp.dot(low, step_proj[...], preferred_element_type=F32) + step_bias[...]
    step = jnp.maximum(raw, 0.0) + jnp.log1p(jnp.exp(-jnp.abs(raw)))
    turned[...] = jnp.zeros_like(turned)
    turned[0:rows, :] = own_first(parts[DTR // LANES], c)
    mats = turned[...].T
    rate = -jnp.exp(decay_log[...])
    fed = own_first(step * act, c)
    step = own_first(step, c)
    for side in range(2):
        for s in range(nchan):
            q = side * nchan + s
            place = (c if side == 0 else 1 - c) * nchan + s
            b_col = mats[0:NS, q : q + 1]
            c_col = mats[NS : 2 * NS, q : q + 1]
            for b in range(blocks):
                lanes = slice(b * LANES, (b + 1) * LANES)
                if side == 0:
                    state = own[s, b * NS : (b + 1) * NS, :].astype(F32)
                else:
                    state = hid_other[s, rows : rows + NS, lanes].astype(F32)
                after = jnp.exp(step[q : q + 1, lanes] * rate[:, lanes]) * state + fed[q : q + 1, lanes] * b_col
                next_out[place, :, lanes] = after
                mixed[q : q + 1, lanes] = jnp.sum(after * c_col, axis=0, keepdims=True)
    save = pltpu.make_async_copy(next_out, next_hbm, save_sem)
    save.start()
    gated = ((own_first(mixed[...], c) + skip_gain[...] * act) * gate_ref[...]).astype(BF16)
    gated_out[...] = gated
    down_product(copies, gated, fetched, buffer, send_out)
    save.wait()


def down_kernel(gated, weight, out_ref, buffer, sems):
    copies = down_stream(weight, buffer, sems, (lax.axis_index("src"),), 0)
    down_product(copies, gated[...], None, buffer, out_ref)


def finish_kernel(final, hidden, out_ref):
    total = None
    for i in range(final.shape[0]):
        part = final[i].astype(F32)
        total = part if total is None else total + part
    out_ref[...] = (hidden[...].astype(F32) + total).astype(BF16)


def on_device(
    residual_input,
    query_heads,
    new_keyval,
    cache_pages,
    prompt_lengths,
    page_owner,
    page_index,
    mamba_state,
    conv_state,
    out_heads,
    in_values,
    in_gates,
    conv_taps,
    conv_offset,
    state_proj,
    step_proj,
    step_bias,
    decay_log,
    skip_gain,
    mamba_down,
):
    nchan = lax.axis_size("chan")
    rows, cols = residual_input.shape
    steps = conv_state.shape[1]
    held, page_tokens = cache_pages.shape[0], cache_pages.shape[1]
    lay = Chunk(nchan, held * page_tokens, cols // LANES, steps)
    call = pl.pallas_call
    shape = jax.ShapeDtypeStruct

    conv_rows = jnp.transpose(conv_state, (1, 0, 2))
    packed = call(
        functools.partial(pack_kernel, nchan, lay),
        out_shape=shape((nchan, lay.rows, LANES), BF16),
        in_specs=hbm(7),
        out_specs=vmem(1)[0],
        scratch_shapes=[
            VM(query_heads.shape, BF16),
            VM(new_keyval.shape, BF16),
            VM(cache_pages.shape, BF16),
            VM(conv_rows.shape, F32),
            pltpu.SMEM(page_owner.shape, jnp.int32),
            pltpu.SMEM(page_index.shape, jnp.int32),
            pltpu.SMEM(prompt_lengths.shape, jnp.int32),
            pltpu.SemaphoreType.DMA((7,)),
        ],
        compiler_params=pltpu.CompilerParams(vmem_limit_bytes=64 * 2**20 - 2**18),
        name="pack",
    )(query_heads, new_keyval, cache_pages, conv_rows, page_owner, page_index, prompt_lengths)
    packed, residual_input, mamba_state = lax.optimization_barrier((packed, residual_input, mamba_state))
    arrived = exchange(packed)
    cut = shape((nchan, NS, cols), BF16)
    residual, same, cross = call(
        load_kernel,
        out_shape=(shape((rows, cols), BF16), cut, cut),
        in_specs=vmem(2),
        out_specs=tuple(vmem(3)),
        compiler_params=params(16),
        cost_estimate=cost(SHORT, 0),
        name="load",
    )(residual_input, mamba_state)
    arrived, residual, same, cross = lax.optimization_barrier((arrived, residual, same, cross))

    other_arrived = swap(arrived)
    pairs = nchan * lay.per
    conv_cut = shape((nchan, round_up(lay.conv_rows, 8), LANES), F32)
    attended, conv_own, conv_other = call(
        functools.partial(attend_kernel, lay),
        out_shape=(shape((nchan, pairs, LANES), BF16), conv_cut, conv_cut),
        in_specs=vmem(2),
        out_specs=tuple(vmem(3)),
        scratch_shapes=[VM((pairs, HD), F32), VM((pairs, 2 * nchan * lay.tokens), F32), VM((pairs, HD), F32)],
        compiler_params=params(4 if held < 16 else 44),
        name="attend",
    )(arrived, other_arrived)
    att_own, out_weight = lax.optimization_barrier((exchange(attended), out_heads))
    att_other = swap(att_own)
    fetched_rows = D // 4
    out_fetched = call(
        fetch_kernel,
        out_shape=shape((fetched_rows, cols), BF16),
        in_specs=hbm(1),
        out_specs=vmem(1)[0],
        scratch_shapes=[pltpu.SemaphoreType.DMA((4,))],
        compiler_params=params(STREAM_MIB),
        cost_estimate=cost(SHORT, 0),
        name="fetch",
    )(out_weight)
    hidden, hid_send = call(
        functools.partial(out_kernel, lay),
        out_shape=(shape((rows, cols), BF16), shape((nchan, rows + NS, cols), BF16)),
        in_specs=vmem(5) + hbm(1),
        out_specs=tuple(vmem(2)),
        scratch_shapes=[
            VM((D - fetched_rows, cols), BF16),
            pltpu.SemaphoreType.DMA(((D - fetched_rows) // (lay.per * HD),)),
        ],
        compiler_params=params(STREAM_MIB),
        name="out",
    )(att_own, att_other, residual, cross, out_fetched, out_heads)
    half_streamed = [VM((D // 2, cols), BF16), pltpu.SemaphoreType.DMA((nchan,))]
    streamed = [VM((D, cols), BF16), pltpu.SemaphoreType.DMA((2 * nchan,))]
    hid_own = exchange(hid_send)
    hid_other = swap(hid_own)
    values_partial = call(
        own_kernel,
        out_shape=shape((rows, cols), F32),
        in_specs=vmem(1) + hbm(1),
        out_specs=vmem(1)[0],
        scratch_shapes=half_streamed,
        compiler_params=params(STREAM_MIB),
        cost_estimate=cost(SHORT, 0),
        name="values_own",
    )(hid_own, in_values)

    sent_rows = (cols // LANES) * NS + (round_up(state_proj.shape[1], LANES) // LANES) * rows
    conv_next, act, rms, part = call(
        functools.partial(values_kernel, lay),
        out_shape=(
            shape((steps, rows, cols), F32),
            shape((rows, cols), F32),
            shape((rows, LANES), F32),
            shape((nchan, sent_rows, LANES), BF16),
        ),
        in_specs=vmem(9) + hbm(1),
        out_specs=tuple(vmem(4)),
        scratch_shapes=half_streamed,
        compiler_params=params(STREAM_MIB),
        name="values",
    )(hid_own, hid_other, conv_own, conv_other, conv_taps, conv_offset[None, :], state_proj.T, same, values_partial, in_values)
    part, down_weight = lax.optimization_barrier((part, mamba_down))
    proj_own = exchange(part)
    pieces = 8
    piece = D // pieces
    gate, down_fetched = call(
        gates_kernel,
        out_shape=(shape((rows, cols), F32), shape((cols, DOWN_READY * piece), BF16)),
        in_specs=vmem(3) + hbm(2),
        out_specs=tuple(vmem(2)),
        scratch_shapes=streamed + [pltpu.SemaphoreType.DMA((DOWN_READY,))],
        compiler_params=params(STREAM_MIB),
        cost_estimate=cost(SHORT, 0),
        name="gates",
    )(hid_own, hid_other, rms, in_gates, down_weight)
    proj_own, gate, down_fetched = lax.optimization_barrier((proj_own, gate, down_fetched))
    proj_other = swap(proj_own)

    down_streamed = [
        VM((rows, NS, cols), F32),
        VM((cols, D // 2 - DOWN_READY * piece), BF16),
        pltpu.SemaphoreType.DMA((pieces // 2 - DOWN_READY,)),
        pltpu.SemaphoreType.DMA,
    ]
    mamba_next, gated, send = call(
        scan_kernel,
        out_shape=(
            shape((rows, NS, cols), F32),
            shape((rows, cols), BF16),
            shape((nchan, rows, cols), BF16),
        ),
        in_specs=vmem(10) + hbm(1),
        out_specs=tuple(hbm(1) + vmem(2)),
        scratch_shapes=[VM((LANES, LANES), F32), VM((rows, cols), F32)] + down_streamed,
        compiler_params=params(STREAM_MIB),
        name="scan",
    )(
        proj_own,
        proj_other,
        hid_other,
        act,
        gate,
        step_proj,
        step_bias[None, :],
        decay_log,
        skip_gain[None, :],
        down_fetched,
        mamba_down,
    )
    taken = swap(send)
    keep = call(
        down_kernel,
        out_shape=shape((nchan, rows, cols), F32),
        in_specs=vmem(1) + hbm(1),
        out_specs=vmem(1)[0],
        scratch_shapes=[VM((cols, D // 2), BF16), pltpu.SemaphoreType.DMA((pieces // 2,))],
        compiler_params=params(STREAM_MIB),
        cost_estimate=cost(SHORT, 0),
        name="down",
    )(gated, mamba_down)
    summed = (keep + taken.astype(F32)).astype(BF16)
    hidden_out = call(
        finish_kernel,
        out_shape=shape((rows, cols), BF16),
        in_specs=vmem(2),
        out_specs=vmem(1)[0],
        compiler_params=params(4),
        name="finish",
    )(exchange(summed), hidden)
    return (hidden_out, mamba_next, jnp.transpose(conv_next, (1, 0, 2)))


def solution(mesh):
    owners = ("groups", "src", "chan")
    channels = ("src", "chan")
    placed = (
        P("groups", channels),
        P(owners, None),
        P(owners, None),
        P(owners, None, None),
        P("groups"),
        P(owners),
        P(owners),
        P(owners, None, None),
        P(owners, None, None),
        P(None, channels),
        P(None, channels),
        P(None, channels),
        P(None, channels),
        P(channels),
        P(channels, None),
        P(None, channels),
        P(channels),
        P(None, channels),
        P(channels),
        P(channels, None),
    )
    return jax.shard_map(
        on_device,
        mesh=mesh,
        in_specs=placed,
        out_specs=(P("groups", channels), P("groups", None, channels), P("groups", None, channels)),
        check_vma=False,
    )
```

```python
import functools
import math

import jax
import jax.numpy as jnp
from jax import lax
from jax.experimental import pallas as pl
from jax.experimental.pallas import tpu as pltpu
from jax.sharding import PartitionSpec as P

D = 8192
NS = 16
DTR = 512
QH = 64
KVH = 8
HD = 128
G = QH // KVH
LANES = 128
NEGATIVE = -1e30
STREAM_MIB = 50
DOWN_READY = 1
SHORT = 3 * 10**9
F32 = jnp.float32
BF16 = jnp.bfloat16
VM = pltpu.VMEM


def round_up(value, step):
    return -(-value // step) * step


def vmem(count):
    return [pl.BlockSpec(memory_space=pltpu.VMEM)] * count


def smem(count):
    return [pl.BlockSpec(memory_space=pltpu.SMEM)] * count


def hbm(count):
    return [pl.BlockSpec(memory_space=pltpu.HBM)] * count


def params(mib):
    return pltpu.CompilerParams(vmem_limit_bytes=mib * 2**20)


def cost(flops, nbytes):
    return pl.CostEstimate(flops=flops, bytes_accessed=nbytes, transcendentals=0)


def swap(x):
    return lax.ppermute(x, "src", [(0, 1), (1, 0)])


def exchange(x):
    return lax.all_to_all(x, "chan", split_axis=0, concat_axis=0, tiled=True)


class Chunk:
    def __init__(self, nchan, held_tokens, blocks, steps):
        self.per = QH // nchan
        self.tokens = held_tokens
        self.owner_rows = held_tokens // LANES
        self.value = held_tokens
        self.small = 2 * held_tokens
        self.query = 2 + self.owner_rows
        self.conv = self.query + self.per
        self.conv_rows = steps * blocks
        self.small_rows = round_up(self.conv + 2 * self.conv_rows, 16)
        self.rows = self.small + self.small_rows


def pack_kernel(
    nchan,
    lay,
    query_hbm,
    newkv_hbm,
    pages_hbm,
    conv_hbm,
    owner_hbm,
    index_hbm,
    lengths_hbm,
    *refs,
):
    outs, (query, newkv, pages, conv, owners, indexes, lengths, sems) = refs[:nchan], refs[nchan:]
    moves = (
        (pages_hbm, pages),
        (conv_hbm, conv),
        (query_hbm, query),
        (newkv_hbm, newkv),
        (owner_hbm, owners),
        (index_hbm, indexes),
        (lengths_hbm, lengths),
    )
    copies = [pltpu.make_async_copy(src, dst, sems.at[i]) for i, (src, dst) in enumerate(moves)]
    for copy in copies:
        copy.start()
    c = lax.axis_index("src")
    page_tokens = pages.shape[1]
    cols = conv.shape[2] // (2 * nchan)
    blocks = cols // LANES
    steps = conv.shape[0]
    rep = nchan // KVH
    for copy in copies[1:]:
        copy.wait()
    lane = lax.broadcasted_iota(jnp.int32, (1, LANES), 1)
    per_row = LANES // page_tokens
    owner_rows = []
    for i in range(lay.owner_rows):
        found = jnp.full((1, LANES), -1, jnp.int32)
        for j in range(per_row):
            owner = owners[i * per_row + j]
            left = lengths[owner] - indexes[i * per_row + j] * page_tokens
            found = jnp.where((lane // page_tokens == j) & (lane % page_tokens < left), owner, found)
        owner_rows.append(found.astype(F32))
    targets = [jnp.bitwise_xor(lax.axis_index("chan"), k) for k in range(nchan)]
    for d, out_ref in zip(targets, outs):
        at = lax.div(d, rep) * HD
        small = [newkv[0:1, pl.ds(pl.multiple_of(x, HD), HD)].astype(F32) for x in (at, KVH * HD + at)] + owner_rows
        for h in range(lay.per):
            place = pl.multiple_of((d * lay.per + h) * HD, HD)
            small.append(query[0:1, pl.ds(place, HD)].astype(F32))
        for half in (c, 1 - c):
            first = (half * nchan + d) * cols
            for b in range(blocks):
                lanes = pl.ds(pl.multiple_of(first + b * LANES, LANES), LANES)
                for w in range(steps):
                    small.append(conv[w, 0:1, lanes])
        if lay.small_rows > len(small):
            small.append(jnp.zeros((lay.small_rows - len(small), LANES), F32))
        out_ref[lay.small : lay.rows, :] = jnp.concatenate(small, axis=0).astype(BF16)
    copies[0].wait()
    for d, out_ref in zip(targets, outs):
        at = lax.div(d, rep) * HD
        keys = pl.ds(pl.multiple_of(at, HD), HD)
        values = pl.ds(pl.multiple_of(KVH * HD + at, HD), HD)
        out_ref[0 : lay.tokens, :] = pages[:, :, keys].reshape(lay.tokens, HD)
        out_ref[lay.value : lay.small, :] = pages[:, :, values].reshape(lay.tokens, HD)


def load_kernel(residual, state, residual_out, same, cross):
    c = lax.axis_index("src")
    nchan, _, cols = same.shape
    residual_out[...] = residual[...]
    for ref, half in ((same, c), (cross, 1 - c)):
        for d in range(nchan):
            lanes = pl.ds(pl.multiple_of((half * nchan + d) * cols, cols), cols)
            ref[d] = state[0, :, lanes].astype(BF16)


def attend_kernel(lay, nchan, *refs):
    recv, other = refs[:nchan], refs[nchan : 2 * nchan]
    out_ref, conv_own, conv_other, queries, scores, result = refs[2 * nchan :]
    d = lax.axis_index("chan")
    per, tokens = lay.per, lay.tokens
    c = lax.axis_index("src")
    count = nchan * per
    scale = 1.0 / math.sqrt(HD)
    contract = (((1,), (1,)), ((), ()))
    new_keys, new_values, owners = [], [], []
    spare = conv_own.shape[1] - lay.conv_rows
    for blocks, conv_out, at in ((recv, conv_own, lay.conv), (other, conv_other, lay.conv + lay.conv_rows)):
        for k, ref in enumerate(blocks):
            s = jnp.bitwise_xor(d, k)
            small = ref[lay.small : lay.rows, :].astype(F32)
            conv = small[at : at + lay.conv_rows, :]
            conv_out[s] = jnp.concatenate([conv, jnp.zeros((spare, LANES), F32)], axis=0) if spare else conv
            owners.append(jnp.concatenate([small[2 + i : 3 + i, :] for i in range(lay.owner_rows)], axis=1))
            if blocks is recv:
                queries[pl.ds(pl.multiple_of(s * per, per), per), :] = small[lay.query : lay.query + per, :]
                new_keys.append(small[0:1, :])
                new_values.append(small[1:2, :])
    fill = round_up(nchan, 16) - nchan
    if fill:
        new_keys.append(jnp.zeros((fill, HD), F32))
        new_values.append(jnp.zeros((fill, HD), F32))
    new_keys = jnp.concatenate(new_keys, axis=0).astype(BF16)
    new_values = jnp.concatenate(new_values, axis=0).astype(BF16)
    place = lax.broadcasted_iota(jnp.int32, (count, 1), 0) // per
    lane = lax.broadcasted_iota(jnp.int32, (1, nchan + fill), 1)
    q = queries[...].astype(BF16)
    new_scores = lax.dot_general(q, new_keys, contract, preferred_element_type=F32) * scale
    new_scores = jnp.where(jnp.bitwise_xor(place, d) == lane, new_scores, NEGATIVE)
    wide = (c * nchan + place).astype(F32)
    sources = list(recv) + list(other)
    highest = None
    for i, ref in enumerate(sources):
        part = lax.dot_general(q, ref[0:tokens, :], contract, preferred_element_type=F32) * scale
        part = jnp.where(wide == owners[i], part, NEGATIVE)
        scores[:, i * tokens : (i + 1) * tokens] = part
        highest = part if highest is None else jnp.maximum(highest, part)
    peak = jnp.maximum(jnp.max(highest, axis=1, keepdims=True), jnp.max(new_scores, axis=1, keepdims=True))
    new_weight = jnp.exp(new_scores - peak)
    numer = jnp.dot(new_weight.astype(BF16), new_values, preferred_element_type=F32)
    summed = None
    for i, ref in enumerate(sources):
        weight = jnp.exp(scores[:, i * tokens : (i + 1) * tokens] - peak)
        summed = weight if summed is None else summed + weight
        numer = numer + jnp.dot(weight.astype(BF16), ref[lay.value : lay.small, :], preferred_element_type=F32)
    total = jnp.sum(summed, axis=1, keepdims=True) + jnp.sum(new_weight, axis=1, keepdims=True)
    result[...] = numer / total
    heads = [result[pl.ds(h, nchan, stride=per), :] for h in range(per)]
    block = jnp.concatenate(heads, axis=0).astype(BF16)
    for i in range(nchan):
        out_ref[i] = block


def in_order(own, other, c):
    return jnp.where(c == 0, jnp.concatenate([own, other], axis=0), jnp.concatenate([other, own], axis=0))


def own_first(x, c):
    half = x.shape[0] // 2
    return in_order(x[:half], x[half:], c)


def stream(weight, buffer, sems, starts):
    depth = buffer.shape[0] // len(starts)
    copies = []
    for i, start in enumerate(starts):
        rows = pl.ds(pl.multiple_of(start, depth), depth)
        copies.append(pltpu.make_async_copy(weight.at[rows, :], buffer.at[pl.ds(i * depth, depth), :], sems.at[i]))
        copies[-1].start()
    return copies


def row_starts(nchan, depth, own):
    c = lax.axis_index("src")
    half = c if own else 1 - c
    return [(half * nchan + i) * depth for i in range(nchan)]


def half_dot(copies, lhs, total, buffer, rows):
    depth = lhs.shape[2]
    for i, copy in enumerate(copies):
        copy.wait()
        block = buffer[i * depth : (i + 1) * depth, :]
        part = jnp.dot(lhs[i, 0:rows, :], block, preferred_element_type=F32)
        total = part if total is None else total + part
    return total


def own_kernel(lhs, weight, out_ref, buffer, sems):
    nchan, depth = lhs.shape[0], lhs.shape[2]
    copies = stream(weight, buffer, sems, row_starts(nchan, depth, True))
    out_ref[...] = half_dot(copies, lhs, None, buffer, out_ref.shape[0])


def halves_dot(copies, own, other, buffer, count):
    nchan, depth = own.shape[0], own.shape[2]
    total = None
    for i, copy in enumerate(copies):
        ref = own if i < nchan else other
        copy.wait()
        part = jnp.dot(ref[i % nchan, 0:count, :], buffer[i * depth : (i + 1) * depth, :], preferred_element_type=F32)
        total = part if total is None else total + part
    return total


def fetch_kernel(weight, out_ref, sems):
    depth = out_ref.shape[0] // sems.shape[0]
    for copy in stream(weight, out_ref, sems, [i * depth for i in range(sems.shape[0])]):
        copy.wait()


def out_kernel(lay, own, other, residual, cross, fetched, weight, hidden_out, out_ref, buffer, sems):
    c = lax.axis_index("src")
    nchan, rows = own.shape[0], residual.shape[0]
    depth = lay.per * HD
    ready = fetched.shape[0] // depth
    copies = stream(weight, buffer, sems, [i * depth for i in range(ready, nchan)])
    for i in range(nchan):
        out_ref[i, rows : rows + NS, :] = cross[i]
    product = residual[...].astype(F32)
    for i in range(nchan):
        mine, rest = own[i].astype(F32), other[i].astype(F32)
        heads = [slice(h * nchan, (h + 1) * nchan) for h in range(lay.per)]
        lhs = jnp.concatenate([in_order(mine[h], rest[h], c) for h in heads], axis=1).astype(BF16)
        if i < ready:
            block = fetched[i * depth : (i + 1) * depth, :]
        else:
            copies[i - ready].wait()
            block = buffer[(i - ready) * depth : (i - ready + 1) * depth, :]
        product = product + jnp.dot(lhs, block, preferred_element_type=F32)
    hidden = product.astype(BF16)
    hidden_out[...] = hidden
    for i in range(nchan):
        out_ref[i, 0:rows, :] = hidden


def values_kernel(
    lay, own, other, own_conv, other_conv, taps, offset, state_proj, same, partial, weight,
    conv_out, act_out, rms_out, proj_out, buffer, sems,
):
    copies = stream(weight, buffer, sems, row_starts(own.shape[0], own.shape[2], False))
    c = lax.axis_index("src")
    nchan = own.shape[0]
    rows, cols = act_out.shape
    squares = jnp.zeros((rows, own.shape[2]), F32)
    for ref in (own, other):
        for i in range(nchan):
            wide = ref[i, 0:rows, :].astype(F32)
            squares = squares + wide * wide
    inverse = lax.rsqrt(jnp.sum(squares, axis=1, keepdims=True) / D + 1e-06)
    rms_out[...] = jnp.broadcast_to(inverse, rms_out.shape)
    steps = conv_out.shape[0]
    blocks = cols // LANES
    for i in range(nchan):
        for b in range(blocks):
            proj_out[i, b * NS : (b + 1) * NS, :] = same[i, :, b * LANES : (b + 1) * LANES]
    tails = (own_conv[...], other_conv[...])
    window = []
    for w in range(steps):
        sides = [jnp.concatenate([t[:, b * steps + w, :] for b in range(blocks)], axis=1) for t in tails]
        window.append(in_order(sides[0], sides[1], c))
    window.append(half_dot(copies, other, partial[...], buffer, rows) * inverse)
    mixed = jnp.zeros((rows, cols), F32)
    for w in range(steps + 1):
        mixed = mixed + window[w] * taps[w : w + 1, :]
        if w > 0:
            conv_out[w - 1] = window[w]
    mixed = mixed + offset[...]
    act = mixed / (1.0 + jnp.exp(-mixed))
    act_out[...] = act
    part = lax.dot_general(act.astype(BF16), state_proj[...], (((1,), (1,)), ((), ())), preferred_element_type=F32)
    spare = round_up(part.shape[1], LANES) - part.shape[1]
    part = jnp.concatenate([part, jnp.zeros((rows, spare), F32)], axis=1).astype(BF16)
    base = blocks * NS
    for i in range(nchan):
        for b in range(part.shape[1] // LANES):
            proj_out[i, base + b * rows : base + (b + 1) * rows, :] = part[:, b * LANES : (b + 1) * LANES]


def gates_kernel(own, other, rms, weight, down_hbm, out_ref, down_out, buffer, sems, down_sems):
    nchan, depth = own.shape[0], own.shape[2]
    copies = stream(
        weight,
        buffer,
        sems,
        row_starts(nchan, depth, True) + row_starts(nchan, depth, False),
    )
    part_down = down_stream(down_hbm, down_out, down_sems, (1 - lax.axis_index("src"),), 0)
    gate = halves_dot(copies, own, other, buffer, out_ref.shape[0]) * rms[:, 0:1]
    out_ref[...] = gate / (1.0 + jnp.exp(-gate))
    for copy in part_down:
        copy.wait()


def down_stream(weight, buffer, sems, halves, first):
    width = weight.shape[1] // 2
    step = buffer.shape[1] // sems.shape[0]
    blocks = [(half, i) for half in halves for i in range(width // step)]
    copies = []
    for half, i in blocks[first : first + sems.shape[0]]:
        slot = len(copies)
        columns = pl.ds(pl.multiple_of(half * width + i * step, step), step)
        target = buffer.at[:, pl.ds(slot * step, step)]
        copies.append(pltpu.make_async_copy(weight.at[:, columns], target, sems.at[slot]))
        copies[-1].start()
    return copies


def down_product(copies, gated, fetched, buffer, out_ref):
    cols = out_ref.shape[2]
    step = buffer.shape[1] // len(copies)
    ready = 0 if fetched is None else fetched.shape[1] // step
    each = step // cols
    for slot in range(ready + len(copies)):
        if slot < ready:
            block = fetched[:, slot * step : (slot + 1) * step]
        else:
            copies[slot - ready].wait()
            block = buffer[:, (slot - ready) * step : (slot - ready + 1) * step]
        part = jnp.dot(gated, block, preferred_element_type=F32).astype(out_ref.dtype)
        for j in range(each):
            out_ref[slot * each + j] = part[:, j * cols : (j + 1) * cols]


def scan_kernel(
    own,
    other,
    hid_other,
    act_ref,
    gate_ref,
    step_proj,
    step_bias,
    decay_log,
    skip_gain,
    fetched,
    weight,
    next_hbm,
    gated_out,
    send_out,
    turned,
    mixed,
    next_out,
    buffer,
    sems,
    save_sem,
):
    c = lax.axis_index("src")
    copies = down_stream(weight, buffer, sems, (1 - c,), DOWN_READY)
    nchan = own.shape[0]
    rows, cols = act_ref.shape
    blocks = cols // LANES
    base = blocks * NS
    summed = jnp.zeros((own.shape[1] - base, LANES), F32)
    for ref in (own, other):
        for i in range(nchan):
            summed = summed + ref[i, base:, :].astype(F32)
    parts = [summed[b * rows : (b + 1) * rows, :] for b in range(summed.shape[0] // rows)]
    low = jnp.concatenate(parts[: DTR // LANES], axis=1).astype(BF16)
    act = act_ref[...]
    raw = jnp.dot(low, step_proj[...], preferred_element_type=F32) + step_bias[...]
    step = jnp.maximum(raw, 0.0) + jnp.log1p(jnp.exp(-jnp.abs(raw)))
    turned[...] = jnp.zeros_like(turned)
    turned[0:rows, :] = own_first(parts[DTR // LANES], c)
    mats = turned[...].T
    rate = -jnp.exp(decay_log[...])
    fed = own_first(step * act, c)
    step = own_first(step, c)
    for side in range(2):
        for s in range(nchan):
            q = side * nchan + s
            place = (c if side == 0 else 1 - c) * nchan + s
            b_col = mats[0:NS, q : q + 1]
            c_col = mats[NS : 2 * NS, q : q + 1]
            for b in range(blocks):
                lanes = slice(b * LANES, (b + 1) * LANES)
                if side == 0:
                    state = own[s, b * NS : (b + 1) * NS, :].astype(F32)
                else:
                    state = hid_other[s, rows : rows + NS, lanes].astype(F32)
                after = jnp.exp(step[q : q + 1, lanes] * rate[:, lanes]) * state + fed[q : q + 1, lanes] * b_col
                next_out[place, :, lanes] = after
                mixed[q : q + 1, lanes] = jnp.sum(after * c_col, axis=0, keepdims=True)
    save = pltpu.make_async_copy(next_out, next_hbm, save_sem)
    save.start()
    gated = ((own_first(mixed[...], c) + skip_gain[...] * act) * gate_ref[...]).astype(BF16)
    gated_out[...] = gated
    down_product(copies, gated, fetched, buffer, send_out)
    save.wait()


def down_kernel(gated, weight, out_ref, buffer, sems):
    copies = down_stream(weight, buffer, sems, (lax.axis_index("src"),), 0)
    down_product(copies, gated[...], None, buffer, out_ref)


def finish_kernel(final, hidden, out_ref):
    total = None
    for i in range(final.shape[0]):
        part = final[i].astype(F32)
        total = part if total is None else total + part
    out_ref[...] = (hidden[...].astype(F32) + total).astype(BF16)


def on_device(
    residual_input,
    query_heads,
    new_keyval,
    cache_pages,
    prompt_lengths,
    page_owner,
    page_index,
    mamba_state,
    conv_state,
    out_heads,
    in_values,
    in_gates,
    conv_taps,
    conv_offset,
    state_proj,
    step_proj,
    step_bias,
    decay_log,
    skip_gain,
    mamba_down,
):
    nchan = lax.axis_size("chan")
    rows, cols = residual_input.shape
    steps = conv_state.shape[1]
    held, page_tokens = cache_pages.shape[0], cache_pages.shape[1]
    lay = Chunk(nchan, held * page_tokens, cols // LANES, steps)
    call = pl.pallas_call
    shape = jax.ShapeDtypeStruct

    conv_rows = jnp.transpose(conv_state, (1, 0, 2))
    chunk = shape((lay.rows, LANES), BF16)
    packed = call(
        functools.partial(pack_kernel, nchan, lay),
        out_shape=(chunk,) * nchan,
        in_specs=hbm(7),
        out_specs=tuple(vmem(nchan)),
        scratch_shapes=[
            VM(query_heads.shape, BF16),
            VM(new_keyval.shape, BF16),
            VM(cache_pages.shape, BF16),
            VM(conv_rows.shape, F32),
            pltpu.SMEM(page_owner.shape, jnp.int32),
            pltpu.SMEM(page_index.shape, jnp.int32),
            pltpu.SMEM(prompt_lengths.shape, jnp.int32),
            pltpu.SemaphoreType.DMA((7,)),
        ],
        compiler_params=pltpu.CompilerParams(vmem_limit_bytes=64 * 2**20 - 2**18),
        name="pack",
    )(query_heads, new_keyval, cache_pages, conv_rows, page_owner, page_index, prompt_lengths)
    *packed, residual_input, mamba_state = lax.optimization_barrier((*packed, residual_input, mamba_state))
    arrived = [packed[0]]
    for k in range(1, nchan):
        arrived.append(lax.ppermute(packed[k], "chan", [(i, i ^ k) for i in range(nchan)]))
    cut = shape((nchan, NS, cols), BF16)
    residual, same, cross = call(
        load_kernel,
        out_shape=(shape((rows, cols), BF16), cut, cut),
        in_specs=vmem(2),
        out_specs=tuple(vmem(3)),
        compiler_params=params(16),
        cost_estimate=cost(SHORT, 0),
        name="load",
    )(residual_input, mamba_state)

    early = nchan // 4
    arrived[early], residual, same, cross = lax.optimization_barrier((arrived[early], residual, same, cross))
    other_arrived = [swap(block) for block in arrived]
    pairs = nchan * lay.per
    conv_cut = shape((nchan, round_up(lay.conv_rows, 8), LANES), F32)
    attended, conv_own, conv_other = call(
        functools.partial(attend_kernel, lay, nchan),
        out_shape=(shape((nchan, pairs, LANES), BF16), conv_cut, conv_cut),
        in_specs=vmem(2 * nchan),
        out_specs=tuple(vmem(3)),
        scratch_shapes=[VM((pairs, HD), F32), VM((pairs, 2 * nchan * lay.tokens), F32), VM((pairs, HD), F32)],
        compiler_params=params(4 if held < 16 else 44),
        name="attend",
    )(*arrived, *other_arrived)
    att_own, out_weight = lax.optimization_barrier((exchange(attended), out_heads))
    att_other = swap(att_own)
    fetched_rows = D // 4
    out_fetched = call(
        fetch_kernel,
        out_shape=shape((fetched_rows, cols), BF16),
        in_specs=hbm(1),
        out_specs=vmem(1)[0],
        scratch_shapes=[pltpu.SemaphoreType.DMA((4,))],
        compiler_params=params(STREAM_MIB),
        cost_estimate=cost(SHORT, 0),
        name="fetch",
    )(out_weight)
    hidden, hid_send = call(
        functools.partial(out_kernel, lay),
        out_shape=(shape((rows, cols), BF16), shape((nchan, rows + NS, cols), BF16)),
        in_specs=vmem(5) + hbm(1),
        out_specs=tuple(vmem(2)),
        scratch_shapes=[
            VM((D - fetched_rows, cols), BF16),
            pltpu.SemaphoreType.DMA(((D - fetched_rows) // (lay.per * HD),)),
        ],
        compiler_params=params(STREAM_MIB),
        name="out",
    )(att_own, att_other, residual, cross, out_fetched, out_heads)
    half_streamed = [VM((D // 2, cols), BF16), pltpu.SemaphoreType.DMA((nchan,))]
    streamed = [VM((D, cols), BF16), pltpu.SemaphoreType.DMA((2 * nchan,))]
    hid_own = exchange(hid_send)
    hid_other = swap(hid_own)
    values_partial = call(
        own_kernel,
        out_shape=shape((rows, cols), F32),
        in_specs=vmem(1) + hbm(1),
        out_specs=vmem(1)[0],
        scratch_shapes=half_streamed,
        compiler_params=params(STREAM_MIB),
        cost_estimate=cost(SHORT, 0),
        name="values_own",
    )(hid_own, in_values)

    sent_rows = (cols // LANES) * NS + (round_up(state_proj.shape[1], LANES) // LANES) * rows
    conv_next, act, rms, part = call(
        functools.partial(values_kernel, lay),
        out_shape=(
            shape((steps, rows, cols), F32),
            shape((rows, cols), F32),
            shape((rows, LANES), F32),
            shape((nchan, sent_rows, LANES), BF16),
        ),
        in_specs=vmem(9) + hbm(1),
        out_specs=tuple(vmem(4)),
        scratch_shapes=half_streamed,
        compiler_params=params(STREAM_MIB),
        name="values",
    )(hid_own, hid_other, conv_own, conv_other, conv_taps, conv_offset[None, :], state_proj.T, same, values_partial, in_values)
    part, down_weight = lax.optimization_barrier((part, mamba_down))
    proj_own = exchange(part)
    pieces = 8
    piece = D // pieces
    gate, down_fetched = call(
        gates_kernel,
        out_shape=(shape((rows, cols), F32), shape((cols, DOWN_READY * piece), BF16)),
        in_specs=vmem(3) + hbm(2),
        out_specs=tuple(vmem(2)),
        scratch_shapes=streamed + [pltpu.SemaphoreType.DMA((DOWN_READY,))],
        compiler_params=params(STREAM_MIB),
        cost_estimate=cost(SHORT, 0),
        name="gates",
    )(hid_own, hid_other, rms, in_gates, down_weight)
    proj_own, gate, down_fetched = lax.optimization_barrier((proj_own, gate, down_fetched))
    proj_other = swap(proj_own)

    down_streamed = [
        VM((rows, NS, cols), F32),
        VM((cols, D // 2 - DOWN_READY * piece), BF16),
        pltpu.SemaphoreType.DMA((pieces // 2 - DOWN_READY,)),
        pltpu.SemaphoreType.DMA,
    ]
    mamba_next, gated, send = call(
        scan_kernel,
        out_shape=(
            shape((rows, NS, cols), F32),
            shape((rows, cols), BF16),
            shape((nchan, rows, cols), BF16),
        ),
        in_specs=vmem(10) + hbm(1),
        out_specs=tuple(hbm(1) + vmem(2)),
        scratch_shapes=[VM((LANES, LANES), F32), VM((rows, cols), F32)] + down_streamed,
        compiler_params=params(STREAM_MIB),
        name="scan",
    )(
        proj_own,
        proj_other,
        hid_other,
        act,
        gate,
        step_proj,
        step_bias[None, :],
        decay_log,
        skip_gain[None, :],
        down_fetched,
        mamba_down,
    )
    taken = swap(send)
    keep = call(
        down_kernel,
        out_shape=shape((nchan, rows, cols), F32),
        in_specs=vmem(1) + hbm(1),
        out_specs=vmem(1)[0],
        scratch_shapes=[VM((cols, D // 2), BF16), pltpu.SemaphoreType.DMA((pieces // 2,))],
        compiler_params=params(STREAM_MIB),
        cost_estimate=cost(SHORT, 0),
        name="down",
    )(gated, mamba_down)
    summed = (keep + taken.astype(F32)).astype(BF16)
    hidden_out = call(
        finish_kernel,
        out_shape=shape((rows, cols), BF16),
        in_specs=vmem(2),
        out_specs=vmem(1)[0],
        compiler_params=params(4),
        name="finish",
    )(exchange(summed), hidden)
    return (hidden_out, mamba_next, jnp.transpose(conv_next, (1, 0, 2)))


def solution(mesh):
    owners = ("groups", "src", "chan")
    channels = ("src", "chan")
    placed = (
        P("groups", channels),
        P(owners, None),
        P(owners, None),
        P(owners, None, None),
        P("groups"),
        P(owners),
        P(owners),
        P(owners, None, None),
        P(owners, None, None),
        P(None, channels),
        P(None, channels),
        P(None, channels),
        P(None, channels),
        P(channels),
        P(channels, None),
        P(None, channels),
        P(channels),
        P(None, channels),
        P(channels),
        P(channels, None),
    )
    return jax.shard_map(
        on_device,
        mesh=mesh,
        in_specs=placed,
        out_specs=(P("groups", channels), P("groups", None, channels), P("groups", None, channels)),
        check_vma=False,
    )
```

```python
import functools
import math

import jax
import jax.numpy as jnp
from jax import lax
from jax.experimental import pallas as pl
from jax.experimental.pallas import tpu as pltpu
from jax.sharding import PartitionSpec as P

D = 8192
NS = 16
DTR = 512
QH = 64
KVH = 8
HD = 128
G = QH // KVH
LANES = 128
NEGATIVE = -1e30
STREAM_MIB = 50
DOWN_READY = 1
SHORT = 3 * 10**9
F32 = jnp.float32
BF16 = jnp.bfloat16
VM = pltpu.VMEM


def round_up(value, step):
    return -(-value // step) * step


def vmem(count):
    return [pl.BlockSpec(memory_space=pltpu.VMEM)] * count


def smem(count):
    return [pl.BlockSpec(memory_space=pltpu.SMEM)] * count


def hbm(count):
    return [pl.BlockSpec(memory_space=pltpu.HBM)] * count


def params(mib):
    return pltpu.CompilerParams(vmem_limit_bytes=mib * 2**20)


def cost(flops, nbytes):
    return pl.CostEstimate(flops=flops, bytes_accessed=nbytes, transcendentals=0)


def swap(x):
    return lax.ppermute(x, "src", [(0, 1), (1, 0)])


def exchange(x):
    return lax.all_to_all(x, "chan", split_axis=0, concat_axis=0, tiled=True)


class Chunk:
    def __init__(self, nchan, held_tokens, blocks, steps):
        self.per = QH // nchan
        self.tokens = held_tokens
        self.owner_rows = held_tokens // LANES
        self.value = held_tokens
        self.small = 2 * held_tokens
        self.query = 2 + self.owner_rows
        self.conv = self.query + self.per
        self.conv_rows = steps * blocks
        self.small_rows = round_up(self.conv + 2 * self.conv_rows, 16)
        self.rows = self.small + self.small_rows


def pack_kernel(
    nchan,
    lay,
    query_hbm,
    newkv_hbm,
    pages_hbm,
    conv_hbm,
    owner_hbm,
    index_hbm,
    lengths_hbm,
    state_hbm,
    *refs,
):
    outs, (same, cross) = refs[:nchan], refs[nchan : nchan + 2]
    query, newkv, pages, conv, owners, indexes, lengths, state, sems = refs[nchan + 2 :]
    moves = (
        (pages_hbm, pages),
        (conv_hbm, conv),
        (query_hbm, query),
        (newkv_hbm, newkv),
        (owner_hbm, owners),
        (index_hbm, indexes),
        (lengths_hbm, lengths),
        (state_hbm, state),
    )
    copies = [pltpu.make_async_copy(src, dst, sems.at[i]) for i, (src, dst) in enumerate(moves)]
    for copy in copies:
        copy.start()
    c = lax.axis_index("src")
    page_tokens = pages.shape[1]
    cols = conv.shape[2] // (2 * nchan)
    blocks = cols // LANES
    steps = conv.shape[0]
    rep = nchan // KVH
    for copy in copies[1:-1]:
        copy.wait()
    lane = lax.broadcasted_iota(jnp.int32, (1, LANES), 1)
    per_row = LANES // page_tokens
    owner_rows = []
    for i in range(lay.owner_rows):
        found = jnp.full((1, LANES), -1, jnp.int32)
        for j in range(per_row):
            owner = owners[i * per_row + j]
            left = lengths[owner] - indexes[i * per_row + j] * page_tokens
            found = jnp.where((lane // page_tokens == j) & (lane % page_tokens < left), owner, found)
        owner_rows.append(found.astype(F32))
    targets = [jnp.bitwise_xor(lax.axis_index("chan"), k) for k in range(nchan)]
    for d, out_ref in zip(targets, outs):
        at = lax.div(d, rep) * HD
        small = [newkv[0:1, pl.ds(pl.multiple_of(x, HD), HD)].astype(F32) for x in (at, KVH * HD + at)] + owner_rows
        for h in range(lay.per):
            place = pl.multiple_of((d * lay.per + h) * HD, HD)
            small.append(query[0:1, pl.ds(place, HD)].astype(F32))
        for half in (c, 1 - c):
            first = (half * nchan + d) * cols
            for b in range(blocks):
                lanes = pl.ds(pl.multiple_of(first + b * LANES, LANES), LANES)
                for w in range(steps):
                    small.append(conv[w, 0:1, lanes])
        if lay.small_rows > len(small):
            small.append(jnp.zeros((lay.small_rows - len(small), LANES), F32))
        out_ref[lay.small : lay.rows, :] = jnp.concatenate(small, axis=0).astype(BF16)
    copies[0].wait()
    for d, out_ref in zip(targets, outs):
        at = lax.div(d, rep) * HD
        keys = pl.ds(pl.multiple_of(at, HD), HD)
        values = pl.ds(pl.multiple_of(KVH * HD + at, HD), HD)
        out_ref[0 : lay.tokens, :] = pages[:, :, keys].reshape(lay.tokens, HD)
        out_ref[lay.value : lay.small, :] = pages[:, :, values].reshape(lay.tokens, HD)
    copies[-1].wait()
    for ref, half in ((same, c), (cross, 1 - c)):
        for d in range(nchan):
            lanes = pl.ds(pl.multiple_of((half * nchan + d) * cols, cols), cols)
            ref[d] = state[0, :, lanes].astype(BF16)


def attend_kernel(lay, nchan, *refs):
    recv, other = refs[:nchan], refs[nchan : 2 * nchan]
    out_ref, conv_own, conv_other, queries, scores, result = refs[2 * nchan :]
    d = lax.axis_index("chan")
    per, tokens = lay.per, lay.tokens
    c = lax.axis_index("src")
    count = nchan * per
    scale = 1.0 / math.sqrt(HD)
    contract = (((1,), (1,)), ((), ()))
    new_keys, new_values, owners = [], [], []
    spare = conv_own.shape[1] - lay.conv_rows
    for blocks, conv_out, at in ((recv, conv_own, lay.conv), (other, conv_other, lay.conv + lay.conv_rows)):
        for k, ref in enumerate(blocks):
            s = jnp.bitwise_xor(d, k)
            small = ref[lay.small : lay.rows, :].astype(F32)
            conv = small[at : at + lay.conv_rows, :]
            conv_out[s] = jnp.concatenate([conv, jnp.zeros((spare, LANES), F32)], axis=0) if spare else conv
            owners.append(jnp.concatenate([small[2 + i : 3 + i, :] for i in range(lay.owner_rows)], axis=1))
            if blocks is recv:
                queries[pl.ds(pl.multiple_of(s * per, per), per), :] = small[lay.query : lay.query + per, :]
                new_keys.append(small[0:1, :])
                new_values.append(small[1:2, :])
    fill = round_up(nchan, 16) - nchan
    if fill:
        new_keys.append(jnp.zeros((fill, HD), F32))
        new_values.append(jnp.zeros((fill, HD), F32))
    new_keys = jnp.concatenate(new_keys, axis=0).astype(BF16)
    new_values = jnp.concatenate(new_values, axis=0).astype(BF16)
    place = lax.broadcasted_iota(jnp.int32, (count, 1), 0) // per
    lane = lax.broadcasted_iota(jnp.int32, (1, nchan + fill), 1)
    q = queries[...].astype(BF16)
    new_scores = lax.dot_general(q, new_keys, contract, preferred_element_type=F32) * scale
    new_scores = jnp.where(jnp.bitwise_xor(place, d) == lane, new_scores, NEGATIVE)
    wide = (c * nchan + place).astype(F32)
    sources = list(recv) + list(other)
    highest = None
    for i, ref in enumerate(sources):
        part = lax.dot_general(q, ref[0:tokens, :], contract, preferred_element_type=F32) * scale
        part = jnp.where(wide == owners[i], part, NEGATIVE)
        scores[:, i * tokens : (i + 1) * tokens] = part
        highest = part if highest is None else jnp.maximum(highest, part)
    peak = jnp.maximum(jnp.max(highest, axis=1, keepdims=True), jnp.max(new_scores, axis=1, keepdims=True))
    new_weight = jnp.exp(new_scores - peak)
    numer = jnp.dot(new_weight.astype(BF16), new_values, preferred_element_type=F32)
    summed = None
    for i, ref in enumerate(sources):
        weight = jnp.exp(scores[:, i * tokens : (i + 1) * tokens] - peak)
        summed = weight if summed is None else summed + weight
        numer = numer + jnp.dot(weight.astype(BF16), ref[lay.value : lay.small, :], preferred_element_type=F32)
    total = jnp.sum(summed, axis=1, keepdims=True) + jnp.sum(new_weight, axis=1, keepdims=True)
    result[...] = numer / total
    heads = [result[pl.ds(h, nchan, stride=per), :] for h in range(per)]
    block = jnp.concatenate(heads, axis=0).astype(BF16)
    for i in range(nchan):
        out_ref[i] = block


def in_order(own, other, c):
    return jnp.where(c == 0, jnp.concatenate([own, other], axis=0), jnp.concatenate([other, own], axis=0))


def own_first(x, c):
    half = x.shape[0] // 2
    return in_order(x[:half], x[half:], c)


def stream(weight, buffer, sems, starts):
    depth = buffer.shape[0] // len(starts)
    copies = []
    for i, start in enumerate(starts):
        rows = pl.ds(pl.multiple_of(start, depth), depth)
        copies.append(pltpu.make_async_copy(weight.at[rows, :], buffer.at[pl.ds(i * depth, depth), :], sems.at[i]))
        copies[-1].start()
    return copies


def row_starts(nchan, depth, own):
    c = lax.axis_index("src")
    half = c if own else 1 - c
    return [(half * nchan + i) * depth for i in range(nchan)]


def half_dot(copies, lhs, total, buffer, rows):
    depth = lhs.shape[2]
    for i, copy in enumerate(copies):
        copy.wait()
        block = buffer[i * depth : (i + 1) * depth, :]
        part = jnp.dot(lhs[i, 0:rows, :], block, preferred_element_type=F32)
        total = part if total is None else total + part
    return total


def own_kernel(lhs, weight, out_ref, buffer, sems):
    nchan, depth = lhs.shape[0], lhs.shape[2]
    copies = stream(weight, buffer, sems, row_starts(nchan, depth, True))
    out_ref[...] = half_dot(copies, lhs, None, buffer, out_ref.shape[0])


def halves_dot(copies, own, other, buffer, count):
    nchan, depth = own.shape[0], own.shape[2]
    total = None
    for i, copy in enumerate(copies):
        ref = own if i < nchan else other
        copy.wait()
        part = jnp.dot(ref[i % nchan, 0:count, :], buffer[i * depth : (i + 1) * depth, :], preferred_element_type=F32)
        total = part if total is None else total + part
    return total


def fetch_kernel(weight, out_ref, sems):
    depth = out_ref.shape[0] // sems.shape[0]
    for copy in stream(weight, out_ref, sems, [i * depth for i in range(sems.shape[0])]):
        copy.wait()


def out_kernel(lay, own, other, residual, cross, fetched, weight, hidden_out, out_ref, buffer, sems):
    c = lax.axis_index("src")
    nchan, rows = own.shape[0], residual.shape[0]
    depth = lay.per * HD
    ready = fetched.shape[0] // depth
    copies = stream(weight, buffer, sems, [i * depth for i in range(ready, nchan)])
    for i in range(nchan):
        out_ref[i, rows : rows + NS, :] = cross[i]
    product = residual[...].astype(F32)
    for i in range(nchan):
        mine, rest = own[i].astype(F32), other[i].astype(F32)
        heads = [slice(h * nchan, (h + 1) * nchan) for h in range(lay.per)]
        lhs = jnp.concatenate([in_order(mine[h], rest[h], c) for h in heads], axis=1).astype(BF16)
        if i < ready:
            block = fetched[i * depth : (i + 1) * depth, :]
        else:
            copies[i - ready].wait()
            block = buffer[(i - ready) * depth : (i - ready + 1) * depth, :]
        product = product + jnp.dot(lhs, block, preferred_element_type=F32)
    hidden = product.astype(BF16)
    hidden_out[...] = hidden
    for i in range(nchan):
        out_ref[i, 0:rows, :] = hidden


def values_kernel(
    lay, own, other, own_conv, other_conv, taps, offset, state_proj, same, partial, weight,
    conv_out, act_out, rms_out, proj_out, buffer, sems,
):
    copies = stream(weight, buffer, sems, row_starts(own.shape[0], own.shape[2], False))
    c = lax.axis_index("src")
    nchan = own.shape[0]
    rows, cols = act_out.shape
    squares = jnp.zeros((rows, own.shape[2]), F32)
    for ref in (own, other):
        for i in range(nchan):
            wide = ref[i, 0:rows, :].astype(F32)
            squares = squares + wide * wide
    inverse = lax.rsqrt(jnp.sum(squares, axis=1, keepdims=True) / D + 1e-06)
    rms_out[...] = jnp.broadcast_to(inverse, rms_out.shape)
    steps = conv_out.shape[0]
    blocks = cols // LANES
    for i in range(nchan):
        for b in range(blocks):
            proj_out[i, b * NS : (b + 1) * NS, :] = same[i, :, b * LANES : (b + 1) * LANES]
    tails = (own_conv[...], other_conv[...])
    window = []
    for w in range(steps):
        sides = [jnp.concatenate([t[:, b * steps + w, :] for b in range(blocks)], axis=1) for t in tails]
        window.append(in_order(sides[0], sides[1], c))
    window.append(half_dot(copies, other, partial[...], buffer, rows) * inverse)
    mixed = jnp.zeros((rows, cols), F32)
    for w in range(steps + 1):
        mixed = mixed + window[w] * taps[w : w + 1, :]
        if w > 0:
            conv_out[w - 1] = window[w]
    mixed = mixed + offset[...]
    act = mixed / (1.0 + jnp.exp(-mixed))
    act_out[...] = act
    part = lax.dot_general(act.astype(BF16), state_proj[...], (((1,), (1,)), ((), ())), preferred_element_type=F32)
    spare = round_up(part.shape[1], LANES) - part.shape[1]
    part = jnp.concatenate([part, jnp.zeros((rows, spare), F32)], axis=1).astype(BF16)
    base = blocks * NS
    for i in range(nchan):
        for b in range(part.shape[1] // LANES):
            proj_out[i, base + b * rows : base + (b + 1) * rows, :] = part[:, b * LANES : (b + 1) * LANES]


def gates_kernel(own, other, rms, weight, down_hbm, out_ref, down_out, buffer, sems, down_sems):
    nchan, depth = own.shape[0], own.shape[2]
    copies = stream(
        weight,
        buffer,
        sems,
        row_starts(nchan, depth, True) + row_starts(nchan, depth, False),
    )
    part_down = down_stream(down_hbm, down_out, down_sems, (1 - lax.axis_index("src"),), 0)
    gate = halves_dot(copies, own, other, buffer, out_ref.shape[0]) * rms[:, 0:1]
    out_ref[...] = gate / (1.0 + jnp.exp(-gate))
    for copy in part_down:
        copy.wait()


def down_stream(weight, buffer, sems, halves, first):
    width = weight.shape[1] // 2
    step = buffer.shape[1] // sems.shape[0]
    blocks = [(half, i) for half in halves for i in range(width // step)]
    copies = []
    for half, i in blocks[first : first + sems.shape[0]]:
        slot = len(copies)
        columns = pl.ds(pl.multiple_of(half * width + i * step, step), step)
        target = buffer.at[:, pl.ds(slot * step, step)]
        copies.append(pltpu.make_async_copy(weight.at[:, columns], target, sems.at[slot]))
        copies[-1].start()
    return copies


def down_product(copies, gated, fetched, buffer, out_ref):
    cols = out_ref.shape[2]
    step = buffer.shape[1] // len(copies)
    ready = 0 if fetched is None else fetched.shape[1] // step
    each = step // cols
    for slot in range(ready + len(copies)):
        if slot < ready:
            block = fetched[:, slot * step : (slot + 1) * step]
        else:
            copies[slot - ready].wait()
            block = buffer[:, (slot - ready) * step : (slot - ready + 1) * step]
        part = jnp.dot(gated, block, preferred_element_type=F32).astype(out_ref.dtype)
        for j in range(each):
            out_ref[slot * each + j] = part[:, j * cols : (j + 1) * cols]


def scan_kernel(
    own,
    other,
    hid_other,
    act_ref,
    gate_ref,
    step_proj,
    step_bias,
    decay_log,
    skip_gain,
    fetched,
    weight,
    next_hbm,
    gated_out,
    send_out,
    turned,
    mixed,
    next_out,
    buffer,
    sems,
    save_sem,
):
    c = lax.axis_index("src")
    copies = down_stream(weight, buffer, sems, (1 - c,), DOWN_READY)
    nchan = own.shape[0]
    rows, cols = act_ref.shape
    blocks = cols // LANES
    base = blocks * NS
    summed = jnp.zeros((own.shape[1] - base, LANES), F32)
    for ref in (own, other):
        for i in range(nchan):
            summed = summed + ref[i, base:, :].astype(F32)
    parts = [summed[b * rows : (b + 1) * rows, :] for b in range(summed.shape[0] // rows)]
    low = jnp.concatenate(parts[: DTR // LANES], axis=1).astype(BF16)
    act = act_ref[...]
    raw = jnp.dot(low, step_proj[...], preferred_element_type=F32) + step_bias[...]
    step = jnp.maximum(raw, 0.0) + jnp.log1p(jnp.exp(-jnp.abs(raw)))
    turned[...] = jnp.zeros_like(turned)
    turned[0:rows, :] = own_first(parts[DTR // LANES], c)
    mats = turned[...].T
    rate = -jnp.exp(decay_log[...])
    fed = own_first(step * act, c)
    step = own_first(step, c)
    for side in range(2):
        for s in range(nchan):
            q = side * nchan + s
            place = (c if side == 0 else 1 - c) * nchan + s
            b_col = mats[0:NS, q : q + 1]
            c_col = mats[NS : 2 * NS, q : q + 1]
            for b in range(blocks):
                lanes = slice(b * LANES, (b + 1) * LANES)
                if side == 0:
                    state = own[s, b * NS : (b + 1) * NS, :].astype(F32)
                else:
                    state = hid_other[s, rows : rows + NS, lanes].astype(F32)
                after = jnp.exp(step[q : q + 1, lanes] * rate[:, lanes]) * state + fed[q : q + 1, lanes] * b_col
                next_out[place, :, lanes] = after
                mixed[q : q + 1, lanes] = jnp.sum(after * c_col, axis=0, keepdims=True)
    save = pltpu.make_async_copy(next_out, next_hbm, save_sem)
    save.start()
    gated = ((own_first(mixed[...], c) + skip_gain[...] * act) * gate_ref[...]).astype(BF16)
    gated_out[...] = gated
    down_product(copies, gated, fetched, buffer, send_out)
    save.wait()


def down_kernel(gated, weight, out_ref, buffer, sems):
    copies = down_stream(weight, buffer, sems, (lax.axis_index("src"),), 0)
    down_product(copies, gated[...], None, buffer, out_ref)


def finish_kernel(final, hidden, out_ref):
    total = None
    for i in range(final.shape[0]):
        part = final[i].astype(F32)
        total = part if total is None else total + part
    out_ref[...] = (hidden[...].astype(F32) + total).astype(BF16)


def on_device(
    residual_input,
    query_heads,
    new_keyval,
    cache_pages,
    prompt_lengths,
    page_owner,
    page_index,
    mamba_state,
    conv_state,
    out_heads,
    in_values,
    in_gates,
    conv_taps,
    conv_offset,
    state_proj,
    step_proj,
    step_bias,
    decay_log,
    skip_gain,
    mamba_down,
):
    nchan = lax.axis_size("chan")
    rows, cols = residual_input.shape
    steps = conv_state.shape[1]
    held, page_tokens = cache_pages.shape[0], cache_pages.shape[1]
    lay = Chunk(nchan, held * page_tokens, cols // LANES, steps)
    call = pl.pallas_call
    shape = jax.ShapeDtypeStruct

    conv_rows = jnp.transpose(conv_state, (1, 0, 2))
    chunk = shape((lay.rows, LANES), BF16)
    cut = shape((nchan, NS, cols), BF16)
    *packed, same, cross = call(
        functools.partial(pack_kernel, nchan, lay),
        out_shape=(chunk,) * nchan + (cut, cut),
        in_specs=hbm(8),
        out_specs=tuple(vmem(nchan + 2)),
        scratch_shapes=[
            VM(query_heads.shape, BF16),
            VM(new_keyval.shape, BF16),
            VM(cache_pages.shape, BF16),
            VM(conv_rows.shape, F32),
            pltpu.SMEM(page_owner.shape, jnp.int32),
            pltpu.SMEM(page_index.shape, jnp.int32),
            pltpu.SMEM(prompt_lengths.shape, jnp.int32),
            VM(mamba_state.shape, F32),
            pltpu.SemaphoreType.DMA((8,)),
        ],
        compiler_params=pltpu.CompilerParams(vmem_limit_bytes=64 * 2**20 - 2**18),
        name="pack",
    )(query_heads, new_keyval, cache_pages, conv_rows, page_owner, page_index, prompt_lengths, mamba_state)
    arrived = [packed[0]]
    for k in range(1, nchan):
        arrived.append(lax.ppermute(packed[k], "chan", [(i, i ^ k) for i in range(nchan)]))
    other_arrived = [swap(block) for block in arrived]
    pairs = nchan * lay.per
    conv_cut = shape((nchan, round_up(lay.conv_rows, 8), LANES), F32)
    attended, conv_own, conv_other = call(
        functools.partial(attend_kernel, lay, nchan),
        out_shape=(shape((nchan, pairs, LANES), BF16), conv_cut, conv_cut),
        in_specs=vmem(2 * nchan),
        out_specs=tuple(vmem(3)),
        scratch_shapes=[VM((pairs, HD), F32), VM((pairs, 2 * nchan * lay.tokens), F32), VM((pairs, HD), F32)],
        compiler_params=params(4 if held < 16 else 44),
        name="attend",
    )(*arrived, *other_arrived)
    att_own, out_weight = lax.optimization_barrier((exchange(attended), out_heads))
    att_other = swap(att_own)
    fetched_rows = D // 4
    out_fetched = call(
        fetch_kernel,
        out_shape=shape((fetched_rows, cols), BF16),
        in_specs=hbm(1),
        out_specs=vmem(1)[0],
        scratch_shapes=[pltpu.SemaphoreType.DMA((4,))],
        compiler_params=params(STREAM_MIB),
        cost_estimate=cost(SHORT, 0),
        name="fetch",
    )(out_weight)
    hidden, hid_send = call(
        functools.partial(out_kernel, lay),
        out_shape=(shape((rows, cols), BF16), shape((nchan, rows + NS, cols), BF16)),
        in_specs=vmem(5) + hbm(1),
        out_specs=tuple(vmem(2)),
        scratch_shapes=[
            VM((D - fetched_rows, cols), BF16),
            pltpu.SemaphoreType.DMA(((D - fetched_rows) // (lay.per * HD),)),
        ],
        compiler_params=params(STREAM_MIB),
        name="out",
    )(att_own, att_other, residual_input, cross, out_fetched, out_heads)
    half_streamed = [VM((D // 2, cols), BF16), pltpu.SemaphoreType.DMA((nchan,))]
    streamed = [VM((D, cols), BF16), pltpu.SemaphoreType.DMA((2 * nchan,))]
    hid_own = exchange(hid_send)
    hid_other = swap(hid_own)
    values_partial = call(
        own_kernel,
        out_shape=shape((rows, cols), F32),
        in_specs=vmem(1) + hbm(1),
        out_specs=vmem(1)[0],
        scratch_shapes=half_streamed,
        compiler_params=params(STREAM_MIB),
        cost_estimate=cost(SHORT, 0),
        name="values_own",
    )(hid_own, in_values)

    sent_rows = (cols // LANES) * NS + (round_up(state_proj.shape[1], LANES) // LANES) * rows
    conv_next, act, rms, part = call(
        functools.partial(values_kernel, lay),
        out_shape=(
            shape((steps, rows, cols), F32),
            shape((rows, cols), F32),
            shape((rows, LANES), F32),
            shape((nchan, sent_rows, LANES), BF16),
        ),
        in_specs=vmem(9) + hbm(1),
        out_specs=tuple(vmem(4)),
        scratch_shapes=half_streamed,
        compiler_params=params(STREAM_MIB),
        name="values",
    )(hid_own, hid_other, conv_own, conv_other, conv_taps, conv_offset[None, :], state_proj.T, same, values_partial, in_values)
    part, down_weight = lax.optimization_barrier((part, mamba_down))
    proj_own = exchange(part)
    pieces = 8
    piece = D // pieces
    gate, down_fetched = call(
        gates_kernel,
        out_shape=(shape((rows, cols), F32), shape((cols, DOWN_READY * piece), BF16)),
        in_specs=vmem(3) + hbm(2),
        out_specs=tuple(vmem(2)),
        scratch_shapes=streamed + [pltpu.SemaphoreType.DMA((DOWN_READY,))],
        compiler_params=params(STREAM_MIB),
        cost_estimate=cost(SHORT, 0),
        name="gates",
    )(hid_own, hid_other, rms, in_gates, down_weight)
    proj_own, gate, down_fetched = lax.optimization_barrier((proj_own, gate, down_fetched))
    proj_other = swap(proj_own)

    down_streamed = [
        VM((rows, NS, cols), F32),
        VM((cols, D // 2 - DOWN_READY * piece), BF16),
        pltpu.SemaphoreType.DMA((pieces // 2 - DOWN_READY,)),
        pltpu.SemaphoreType.DMA,
    ]
    mamba_next, gated, send = call(
        scan_kernel,
        out_shape=(
            shape((rows, NS, cols), F32),
            shape((rows, cols), BF16),
            shape((nchan, rows, cols), BF16),
        ),
        in_specs=vmem(10) + hbm(1),
        out_specs=tuple(hbm(1) + vmem(2)),
        scratch_shapes=[VM((LANES, LANES), F32), VM((rows, cols), F32)] + down_streamed,
        compiler_params=params(STREAM_MIB),
        name="scan",
    )(
        proj_own,
        proj_other,
        hid_other,
        act,
        gate,
        step_proj,
        step_bias[None, :],
        decay_log,
        skip_gain[None, :],
        down_fetched,
        mamba_down,
    )
    taken = swap(send)
    keep = call(
        down_kernel,
        out_shape=shape((nchan, rows, cols), F32),
        in_specs=vmem(1) + hbm(1),
        out_specs=vmem(1)[0],
        scratch_shapes=[VM((cols, D // 2), BF16), pltpu.SemaphoreType.DMA((pieces // 2,))],
        compiler_params=params(STREAM_MIB),
        cost_estimate=cost(SHORT, 0),
        name="down",
    )(gated, mamba_down)
    summed = (keep + taken.astype(F32)).astype(BF16)
    hidden_out = call(
        finish_kernel,
        out_shape=shape((rows, cols), BF16),
        in_specs=vmem(2),
        out_specs=vmem(1)[0],
        compiler_params=params(4),
        name="finish",
    )(exchange(summed), hidden)
    return (hidden_out, mamba_next, jnp.transpose(conv_next, (1, 0, 2)))


def solution(mesh):
    owners = ("groups", "src", "chan")
    channels = ("src", "chan")
    placed = (
        P("groups", channels),
        P(owners, None),
        P(owners, None),
        P(owners, None, None),
        P("groups"),
        P(owners),
        P(owners),
        P(owners, None, None),
        P(owners, None, None),
        P(None, channels),
        P(None, channels),
        P(None, channels),
        P(None, channels),
        P(channels),
        P(channels, None),
        P(None, channels),
        P(channels),
        P(None, channels),
        P(channels),
        P(channels, None),
    )
    return jax.shard_map(
        on_device,
        mesh=mesh,
        in_specs=placed,
        out_specs=(P("groups", channels), P("groups", None, channels), P("groups", None, channels)),
        check_vma=False,
    )
```

```python
import functools
import math

import jax
import jax.numpy as jnp
from jax import lax
from jax.experimental import pallas as pl
from jax.experimental.pallas import tpu as pltpu
from jax.sharding import PartitionSpec as P

D = 8192
NS = 16
DTR = 512
QH = 64
KVH = 8
HD = 128
G = QH // KVH
LANES = 128
NEGATIVE = -1e30
STREAM_MIB = 50
DOWN_READY = 1
SHORT = 3 * 10**9
F32 = jnp.float32
BF16 = jnp.bfloat16
VM = pltpu.VMEM


def round_up(value, step):
    return -(-value // step) * step


def vmem(count):
    return [pl.BlockSpec(memory_space=pltpu.VMEM)] * count


def smem(count):
    return [pl.BlockSpec(memory_space=pltpu.SMEM)] * count


def hbm(count):
    return [pl.BlockSpec(memory_space=pltpu.HBM)] * count


def params(mib):
    return pltpu.CompilerParams(vmem_limit_bytes=mib * 2**20)


def cost(flops, nbytes):
    return pl.CostEstimate(flops=flops, bytes_accessed=nbytes, transcendentals=0)


def swap(x):
    return lax.ppermute(x, "src", [(0, 1), (1, 0)])


def exchange(x):
    return lax.all_to_all(x, "chan", split_axis=0, concat_axis=0, tiled=True)


class Chunk:
    def __init__(self, nchan, held_tokens, blocks, steps):
        self.per = QH // nchan
        self.tokens = held_tokens
        self.owner_rows = held_tokens // LANES
        self.value = held_tokens
        self.small = 2 * held_tokens
        self.query = 2 + self.owner_rows
        self.conv = self.query + self.per
        self.conv_rows = steps * blocks
        self.small_rows = round_up(self.conv + 2 * self.conv_rows, 16)
        self.rows = self.small + self.small_rows


def pack_kernel(
    nchan,
    lay,
    query_hbm,
    newkv_hbm,
    pages_hbm,
    conv_hbm,
    owner_hbm,
    index_hbm,
    lengths_hbm,
    state_hbm,
    *refs,
):
    outs, (same, cross) = refs[:nchan], refs[nchan : nchan + 2]
    query, newkv, pages, conv, owners, indexes, lengths, state, sems = refs[nchan + 2 :]
    moves = (
        (pages_hbm, pages),
        (conv_hbm, conv),
        (query_hbm, query),
        (newkv_hbm, newkv),
        (owner_hbm, owners),
        (index_hbm, indexes),
        (lengths_hbm, lengths),
        (state_hbm, state),
    )
    copies = [pltpu.make_async_copy(src, dst, sems.at[i]) for i, (src, dst) in enumerate(moves)]
    for copy in copies:
        copy.start()
    c = lax.axis_index("src")
    page_tokens = pages.shape[1]
    cols = conv.shape[2] // (2 * nchan)
    blocks = cols // LANES
    steps = conv.shape[0]
    rep = nchan // KVH
    for copy in copies[1:-1]:
        copy.wait()
    lane = lax.broadcasted_iota(jnp.int32, (1, LANES), 1)
    per_row = LANES // page_tokens
    owner_rows = []
    for i in range(lay.owner_rows):
        found = jnp.full((1, LANES), -1, jnp.int32)
        for j in range(per_row):
            owner = owners[i * per_row + j]
            left = lengths[owner] - indexes[i * per_row + j] * page_tokens
            found = jnp.where((lane // page_tokens == j) & (lane % page_tokens < left), owner, found)
        owner_rows.append(found.astype(F32))
    targets = [jnp.bitwise_xor(lax.axis_index("chan"), k) for k in range(nchan)]
    for d, out_ref in zip(targets, outs):
        at = lax.div(d, rep) * HD
        small = [newkv[0:1, pl.ds(pl.multiple_of(x, HD), HD)].astype(F32) for x in (at, KVH * HD + at)] + owner_rows
        for h in range(lay.per):
            place = pl.multiple_of((d * lay.per + h) * HD, HD)
            small.append(query[0:1, pl.ds(place, HD)].astype(F32))
        for half in (c, 1 - c):
            first = (half * nchan + d) * cols
            for b in range(blocks):
                lanes = pl.ds(pl.multiple_of(first + b * LANES, LANES), LANES)
                for w in range(steps):
                    small.append(conv[w, 0:1, lanes])
        if lay.small_rows > len(small):
            small.append(jnp.zeros((lay.small_rows - len(small), LANES), F32))
        out_ref[lay.small : lay.rows, :] = jnp.concatenate(small, axis=0).astype(BF16)
    copies[0].wait()
    for d, out_ref in zip(targets, outs):
        at = lax.div(d, rep) * HD
        keys = pl.ds(pl.multiple_of(at, HD), HD)
        values = pl.ds(pl.multiple_of(KVH * HD + at, HD), HD)
        out_ref[0 : lay.tokens, :] = pages[:, :, keys].reshape(lay.tokens, HD)
        out_ref[lay.value : lay.small, :] = pages[:, :, values].reshape(lay.tokens, HD)
    copies[-1].wait()
    for ref, half in ((same, c), (cross, 1 - c)):
        for d in range(nchan):
            lanes = pl.ds(pl.multiple_of((half * nchan + d) * cols, cols), cols)
            ref[d] = state[0, :, lanes].astype(BF16)


def attend_kernel(lay, nchan, *refs):
    recv, other = refs[:nchan], refs[nchan : 2 * nchan]
    out_ref, conv_own, conv_other, queries, scores, result = refs[2 * nchan :]
    d = lax.axis_index("chan")
    per, tokens = lay.per, lay.tokens
    c = lax.axis_index("src")
    count = nchan * per
    scale = 1.0 / math.sqrt(HD)
    contract = (((1,), (1,)), ((), ()))
    new_keys, new_values, owners = [], [], []
    spare = conv_own.shape[1] - lay.conv_rows
    for blocks, conv_out, at in ((recv, conv_own, lay.conv), (other, conv_other, lay.conv + lay.conv_rows)):
        for k, ref in enumerate(blocks):
            s = jnp.bitwise_xor(d, k)
            small = ref[lay.small : lay.rows, :].astype(F32)
            conv = small[at : at + lay.conv_rows, :]
            conv_out[s] = jnp.concatenate([conv, jnp.zeros((spare, LANES), F32)], axis=0) if spare else conv
            owners.append(jnp.concatenate([small[2 + i : 3 + i, :] for i in range(lay.owner_rows)], axis=1))
            if blocks is recv:
                queries[pl.ds(pl.multiple_of(s * per, per), per), :] = small[lay.query : lay.query + per, :]
                new_keys.append(small[0:1, :])
                new_values.append(small[1:2, :])
    fill = round_up(nchan, 16) - nchan
    if fill:
        new_keys.append(jnp.zeros((fill, HD), F32))
        new_values.append(jnp.zeros((fill, HD), F32))
    new_keys = jnp.concatenate(new_keys, axis=0).astype(BF16)
    new_values = jnp.concatenate(new_values, axis=0).astype(BF16)
    place = lax.broadcasted_iota(jnp.int32, (count, 1), 0) // per
    lane = lax.broadcasted_iota(jnp.int32, (1, nchan + fill), 1)
    q = queries[...].astype(BF16)
    new_scores = lax.dot_general(q, new_keys, contract, preferred_element_type=F32) * scale
    new_scores = jnp.where(jnp.bitwise_xor(place, d) == lane, new_scores, NEGATIVE)
    wide = (c * nchan + place).astype(F32)
    sources = list(recv) + list(other)
    highest = None
    for i, ref in enumerate(sources):
        part = lax.dot_general(q, ref[0:tokens, :], contract, preferred_element_type=F32) * scale
        part = jnp.where(wide == owners[i], part, NEGATIVE)
        scores[:, i * tokens : (i + 1) * tokens] = part
        highest = part if highest is None else jnp.maximum(highest, part)
    peak = jnp.maximum(jnp.max(highest, axis=1, keepdims=True), jnp.max(new_scores, axis=1, keepdims=True))
    new_weight = jnp.exp(new_scores - peak)
    numer = jnp.dot(new_weight.astype(BF16), new_values, preferred_element_type=F32)
    summed = None
    for i, ref in enumerate(sources):
        weight = jnp.exp(scores[:, i * tokens : (i + 1) * tokens] - peak)
        summed = weight if summed is None else summed + weight
        numer = numer + jnp.dot(weight.astype(BF16), ref[lay.value : lay.small, :], preferred_element_type=F32)
    total = jnp.sum(summed, axis=1, keepdims=True) + jnp.sum(new_weight, axis=1, keepdims=True)
    result[...] = numer / total
    heads = [result[pl.ds(h, nchan, stride=per), :] for h in range(per)]
    block = jnp.concatenate(heads, axis=0).astype(BF16)
    for i in range(nchan):
        out_ref[i] = block


def in_order(own, other, c):
    return jnp.where(c == 0, jnp.concatenate([own, other], axis=0), jnp.concatenate([other, own], axis=0))


def own_first(x, c):
    half = x.shape[0] // 2
    return in_order(x[:half], x[half:], c)


def stream(weight, buffer, sems, starts):
    depth = buffer.shape[0] // len(starts)
    copies = []
    for i, start in enumerate(starts):
        rows = pl.ds(pl.multiple_of(start, depth), depth)
        copies.append(pltpu.make_async_copy(weight.at[rows, :], buffer.at[pl.ds(i * depth, depth), :], sems.at[i]))
        copies[-1].start()
    return copies


def row_starts(nchan, depth, own):
    c = lax.axis_index("src")
    half = c if own else 1 - c
    return [(half * nchan + i) * depth for i in range(nchan)]


def half_dot(copies, lhs, total, buffer, rows):
    depth = lhs.shape[2]
    for i, copy in enumerate(copies):
        copy.wait()
        block = buffer[i * depth : (i + 1) * depth, :]
        part = jnp.dot(lhs[i, 0:rows, :], block, preferred_element_type=F32)
        total = part if total is None else total + part
    return total


def own_kernel(lhs, weight, out_ref, buffer, sems):
    nchan, depth = lhs.shape[0], lhs.shape[2]
    copies = stream(weight, buffer, sems, row_starts(nchan, depth, True))
    out_ref[...] = half_dot(copies, lhs, None, buffer, out_ref.shape[0])


def halves_dot(copies, own, other, buffer, count):
    nchan, depth = own.shape[0], own.shape[2]
    total = None
    for i, copy in enumerate(copies):
        ref = own if i < nchan else other
        copy.wait()
        part = jnp.dot(ref[i % nchan, 0:count, :], buffer[i * depth : (i + 1) * depth, :], preferred_element_type=F32)
        total = part if total is None else total + part
    return total


def fetch_kernel(weight, out_ref, sems):
    depth = out_ref.shape[0] // sems.shape[0]
    for copy in stream(weight, out_ref, sems, [i * depth for i in range(sems.shape[0])]):
        copy.wait()


def out_kernel(lay, own, other, residual, cross, fetched, weight, hidden_out, out_ref, buffer, sems):
    c = lax.axis_index("src")
    nchan, rows = own.shape[0], residual.shape[0]
    depth = lay.per * HD
    ready = fetched.shape[0] // depth
    copies = stream(weight, buffer, sems, [i * depth for i in range(ready, nchan)])
    for i in range(nchan):
        out_ref[i, rows : rows + NS, :] = cross[i]
    product = residual[...].astype(F32)
    for i in range(nchan):
        mine, rest = own[i].astype(F32), other[i].astype(F32)
        heads = [slice(h * nchan, (h + 1) * nchan) for h in range(lay.per)]
        lhs = jnp.concatenate([in_order(mine[h], rest[h], c) for h in heads], axis=1).astype(BF16)
        if i < ready:
            block = fetched[i * depth : (i + 1) * depth, :]
        else:
            copies[i - ready].wait()
            block = buffer[(i - ready) * depth : (i - ready + 1) * depth, :]
        product = product + jnp.dot(lhs, block, preferred_element_type=F32)
    hidden = product.astype(BF16)
    hidden_out[...] = hidden
    for i in range(nchan):
        out_ref[i, 0:rows, :] = hidden


def values_kernel(
    lay, own, other, own_conv, other_conv, taps, offset, state_proj, same, partial, weight,
    conv_out, act_out, rms_out, proj_out, buffer, sems,
):
    copies = stream(weight, buffer, sems, row_starts(own.shape[0], own.shape[2], False))
    c = lax.axis_index("src")
    nchan = own.shape[0]
    rows, cols = act_out.shape
    squares = jnp.zeros((rows, own.shape[2]), F32)
    for ref in (own, other):
        for i in range(nchan):
            wide = ref[i, 0:rows, :].astype(F32)
            squares = squares + wide * wide
    inverse = lax.rsqrt(jnp.sum(squares, axis=1, keepdims=True) / D + 1e-06)
    rms_out[...] = jnp.broadcast_to(inverse, rms_out.shape)
    steps = conv_out.shape[0]
    blocks = cols // LANES
    for i in range(nchan):
        for b in range(blocks):
            proj_out[i, b * NS : (b + 1) * NS, :] = same[i, :, b * LANES : (b + 1) * LANES]
    tails = (own_conv[...], other_conv[...])
    window = []
    for w in range(steps):
        sides = [jnp.concatenate([t[:, b * steps + w, :] for b in range(blocks)], axis=1) for t in tails]
        window.append(in_order(sides[0], sides[1], c))
    window.append(half_dot(copies, other, partial[...], buffer, rows) * inverse)
    mixed = jnp.zeros((rows, cols), F32)
    for w in range(steps + 1):
        mixed = mixed + window[w] * taps[w : w + 1, :]
        if w > 0:
            conv_out[w - 1] = window[w]
    mixed = mixed + offset[...]
    act = mixed / (1.0 + jnp.exp(-mixed))
    act_out[...] = act
    part = lax.dot_general(act.astype(BF16), state_proj[...], (((1,), (1,)), ((), ())), preferred_element_type=F32)
    spare = round_up(part.shape[1], LANES) - part.shape[1]
    part = jnp.concatenate([part, jnp.zeros((rows, spare), F32)], axis=1).astype(BF16)
    base = blocks * NS
    for i in range(nchan):
        for b in range(part.shape[1] // LANES):
            proj_out[i, base + b * rows : base + (b + 1) * rows, :] = part[:, b * LANES : (b + 1) * LANES]


def gates_kernel(own, other, rms, weight, down_hbm, out_ref, down_out, buffer, sems, down_sems):
    nchan, depth = own.shape[0], own.shape[2]
    copies = stream(
        weight,
        buffer,
        sems,
        row_starts(nchan, depth, True) + row_starts(nchan, depth, False),
    )
    part_down = down_stream(down_hbm, down_out, down_sems, (1 - lax.axis_index("src"),), 0)
    gate = halves_dot(copies, own, other, buffer, out_ref.shape[0]) * rms[:, 0:1]
    out_ref[...] = gate / (1.0 + jnp.exp(-gate))
    for copy in part_down:
        copy.wait()


def down_stream(weight, buffer, sems, halves, first):
    width = weight.shape[1] // 2
    step = buffer.shape[1] // sems.shape[0]
    blocks = [(half, i) for half in halves for i in range(width // step)]
    copies = []
    for half, i in blocks[first : first + sems.shape[0]]:
        slot = len(copies)
        columns = pl.ds(pl.multiple_of(half * width + i * step, step), step)
        target = buffer.at[:, pl.ds(slot * step, step)]
        copies.append(pltpu.make_async_copy(weight.at[:, columns], target, sems.at[slot]))
        copies[-1].start()
    return copies


def down_product(copies, gated, fetched, buffer, out_ref):
    cols = out_ref.shape[2]
    step = buffer.shape[1] // len(copies)
    ready = 0 if fetched is None else fetched.shape[1] // step
    each = step // cols
    for slot in range(ready + len(copies)):
        if slot < ready:
            block = fetched[:, slot * step : (slot + 1) * step]
        else:
            copies[slot - ready].wait()
            block = buffer[:, (slot - ready) * step : (slot - ready + 1) * step]
        part = jnp.dot(gated, block, preferred_element_type=F32).astype(out_ref.dtype)
        for j in range(each):
            out_ref[slot * each + j] = part[:, j * cols : (j + 1) * cols]


def scan_kernel(
    own,
    other,
    hid_other,
    act_ref,
    gate_ref,
    step_proj,
    step_bias,
    decay_log,
    skip_gain,
    fetched,
    weight,
    next_hbm,
    gated_out,
    send_out,
    turned,
    mixed,
    next_out,
    buffer,
    sems,
    save_sem,
):
    c = lax.axis_index("src")
    copies = down_stream(weight, buffer, sems, (1 - c,), DOWN_READY)
    nchan = own.shape[0]
    rows, cols = act_ref.shape
    blocks = cols // LANES
    base = blocks * NS
    summed = jnp.zeros((own.shape[1] - base, LANES), F32)
    for ref in (own, other):
        for i in range(nchan):
            summed = summed + ref[i, base:, :].astype(F32)
    parts = [summed[b * rows : (b + 1) * rows, :] for b in range(summed.shape[0] // rows)]
    low = jnp.concatenate(parts[: DTR // LANES], axis=1).astype(BF16)
    act = act_ref[...]
    raw = jnp.dot(low, step_proj[...], preferred_element_type=F32) + step_bias[...]
    step = jnp.maximum(raw, 0.0) + jnp.log1p(jnp.exp(-jnp.abs(raw)))
    turned[...] = jnp.zeros_like(turned)
    turned[0:rows, :] = own_first(parts[DTR // LANES], c)
    mats = turned[...].T
    rate = -jnp.exp(decay_log[...])
    fed = own_first(step * act, c)
    step = own_first(step, c)
    for side in range(2):
        for s in range(nchan):
            q = side * nchan + s
            place = (c if side == 0 else 1 - c) * nchan + s
            b_col = mats[0:NS, q : q + 1]
            c_col = mats[NS : 2 * NS, q : q + 1]
            for b in range(blocks):
                lanes = slice(b * LANES, (b + 1) * LANES)
                if side == 0:
                    state = own[s, b * NS : (b + 1) * NS, :].astype(F32)
                else:
                    state = hid_other[s, rows : rows + NS, lanes].astype(F32)
                after = jnp.exp(step[q : q + 1, lanes] * rate[:, lanes]) * state + fed[q : q + 1, lanes] * b_col
                next_out[place, :, lanes] = after
                mixed[q : q + 1, lanes] = jnp.sum(after * c_col, axis=0, keepdims=True)
    save = pltpu.make_async_copy(next_out, next_hbm, save_sem)
    save.start()
    gated = ((own_first(mixed[...], c) + skip_gain[...] * act) * gate_ref[...]).astype(BF16)
    gated_out[...] = gated
    down_product(copies, gated, fetched, buffer, send_out)
    save.wait()


def down_kernel(gated, weight, out_ref, buffer, sems):
    copies = down_stream(weight, buffer, sems, (lax.axis_index("src"),), 0)
    down_product(copies, gated[...], None, buffer, out_ref)


def finish_kernel(final, hidden, out_ref):
    total = None
    for i in range(final.shape[0]):
        part = final[i].astype(F32)
        total = part if total is None else total + part
    out_ref[...] = (hidden[...].astype(F32) + total).astype(BF16)


def on_device(
    residual_input,
    query_heads,
    new_keyval,
    cache_pages,
    prompt_lengths,
    page_owner,
    page_index,
    mamba_state,
    conv_state,
    out_heads,
    in_values,
    in_gates,
    conv_taps,
    conv_offset,
    state_proj,
    step_proj,
    step_bias,
    decay_log,
    skip_gain,
    mamba_down,
):
    nchan = lax.axis_size("chan")
    rows, cols = residual_input.shape
    steps = conv_state.shape[1]
    held, page_tokens = cache_pages.shape[0], cache_pages.shape[1]
    lay = Chunk(nchan, held * page_tokens, cols // LANES, steps)
    call = pl.pallas_call
    shape = jax.ShapeDtypeStruct

    conv_rows = jnp.transpose(conv_state, (1, 0, 2))
    chunk = shape((lay.rows, LANES), BF16)
    cut = shape((nchan, NS, cols), BF16)
    *packed, same, cross = call(
        functools.partial(pack_kernel, nchan, lay),
        out_shape=(chunk,) * nchan + (cut, cut),
        in_specs=hbm(8),
        out_specs=tuple(vmem(nchan + 2)),
        scratch_shapes=[
            VM(query_heads.shape, BF16),
            VM(new_keyval.shape, BF16),
            VM(cache_pages.shape, BF16),
            VM(conv_rows.shape, F32),
            pltpu.SMEM(page_owner.shape, jnp.int32),
            pltpu.SMEM(page_index.shape, jnp.int32),
            pltpu.SMEM(prompt_lengths.shape, jnp.int32),
            VM(mamba_state.shape, F32),
            pltpu.SemaphoreType.DMA((8,)),
        ],
        compiler_params=pltpu.CompilerParams(vmem_limit_bytes=64 * 2**20 - 2**18),
        name="pack",
    )(query_heads, new_keyval, cache_pages, conv_rows, page_owner, page_index, prompt_lengths, mamba_state)
    arrived = [packed[0]]
    for k in range(1, nchan):
        arrived.append(lax.ppermute(packed[k], "chan", [(i, i ^ k) for i in range(nchan)]))
    other_arrived = [swap(block) for block in arrived]
    arrived[0] = swap(other_arrived[0])
    pairs = nchan * lay.per
    conv_cut = shape((nchan, round_up(lay.conv_rows, 8), LANES), F32)
    attended, conv_own, conv_other = call(
        functools.partial(attend_kernel, lay, nchan),
        out_shape=(shape((nchan, pairs, LANES), BF16), conv_cut, conv_cut),
        in_specs=vmem(2 * nchan),
        out_specs=tuple(vmem(3)),
        scratch_shapes=[VM((pairs, HD), F32), VM((pairs, 2 * nchan * lay.tokens), F32), VM((pairs, HD), F32)],
        compiler_params=params(4 if held < 16 else 44),
        name="attend",
    )(*arrived, *other_arrived)
    att_own, out_weight = lax.optimization_barrier((exchange(attended), out_heads))
    att_other = swap(att_own)
    fetched_rows = D // 4
    out_fetched = call(
        fetch_kernel,
        out_shape=shape((fetched_rows, cols), BF16),
        in_specs=hbm(1),
        out_specs=vmem(1)[0],
        scratch_shapes=[pltpu.SemaphoreType.DMA((4,))],
        compiler_params=params(STREAM_MIB),
        cost_estimate=cost(SHORT, 0),
        name="fetch",
    )(out_weight)
    hidden, hid_send = call(
        functools.partial(out_kernel, lay),
        out_shape=(shape((rows, cols), BF16), shape((nchan, rows + NS, cols), BF16)),
        in_specs=vmem(5) + hbm(1),
        out_specs=tuple(vmem(2)),
        scratch_shapes=[
            VM((D - fetched_rows, cols), BF16),
            pltpu.SemaphoreType.DMA(((D - fetched_rows) // (lay.per * HD),)),
        ],
        compiler_params=params(STREAM_MIB),
        name="out",
    )(att_own, att_other, residual_input, cross, out_fetched, out_heads)
    half_streamed = [VM((D // 2, cols), BF16), pltpu.SemaphoreType.DMA((nchan,))]
    streamed = [VM((D, cols), BF16), pltpu.SemaphoreType.DMA((2 * nchan,))]
    hid_own = exchange(hid_send)
    hid_other = swap(hid_own)
    values_partial = call(
        own_kernel,
        out_shape=shape((rows, cols), F32),
        in_specs=vmem(1) + hbm(1),
        out_specs=vmem(1)[0],
        scratch_shapes=half_streamed,
        compiler_params=params(STREAM_MIB),
        cost_estimate=cost(SHORT, 0),
        name="values_own",
    )(hid_own, in_values)

    sent_rows = (cols // LANES) * NS + (round_up(state_proj.shape[1], LANES) // LANES) * rows
    conv_next, act, rms, part = call(
        functools.partial(values_kernel, lay),
        out_shape=(
            shape((steps, rows, cols), F32),
            shape((rows, cols), F32),
            shape((rows, LANES), F32),
            shape((nchan, sent_rows, LANES), BF16),
        ),
        in_specs=vmem(9) + hbm(1),
        out_specs=tuple(vmem(4)),
        scratch_shapes=half_streamed,
        compiler_params=params(STREAM_MIB),
        name="values",
    )(hid_own, hid_other, conv_own, conv_other, conv_taps, conv_offset[None, :], state_proj.T, same, values_partial, in_values)
    part, down_weight = lax.optimization_barrier((part, mamba_down))
    proj_own = exchange(part)
    pieces = 8
    piece = D // pieces
    gate, down_fetched = call(
        gates_kernel,
        out_shape=(shape((rows, cols), F32), shape((cols, DOWN_READY * piece), BF16)),
        in_specs=vmem(3) + hbm(2),
        out_specs=tuple(vmem(2)),
        scratch_shapes=streamed + [pltpu.SemaphoreType.DMA((DOWN_READY,))],
        compiler_params=params(STREAM_MIB),
        cost_estimate=cost(SHORT, 0),
        name="gates",
    )(hid_own, hid_other, rms, in_gates, down_weight)
    proj_own, gate, down_fetched = lax.optimization_barrier((proj_own, gate, down_fetched))
    proj_other = swap(proj_own)

    down_streamed = [
        VM((rows, NS, cols), F32),
        VM((cols, D // 2 - DOWN_READY * piece), BF16),
        pltpu.SemaphoreType.DMA((pieces // 2 - DOWN_READY,)),
        pltpu.SemaphoreType.DMA,
    ]
    mamba_next, gated, send = call(
        scan_kernel,
        out_shape=(
            shape((rows, NS, cols), F32),
            shape((rows, cols), BF16),
            shape((nchan, rows, cols), BF16),
        ),
        in_specs=vmem(10) + hbm(1),
        out_specs=tuple(hbm(1) + vmem(2)),
        scratch_shapes=[VM((LANES, LANES), F32), VM((rows, cols), F32)] + down_streamed,
        compiler_params=params(STREAM_MIB),
        name="scan",
    )(
        proj_own,
        proj_other,
        hid_other,
        act,
        gate,
        step_proj,
        step_bias[None, :],
        decay_log,
        skip_gain[None, :],
        down_fetched,
        mamba_down,
    )
    taken = swap(send)
    keep = call(
        down_kernel,
        out_shape=shape((nchan, rows, cols), F32),
        in_specs=vmem(1) + hbm(1),
        out_specs=vmem(1)[0],
        scratch_shapes=[VM((cols, D // 2), BF16), pltpu.SemaphoreType.DMA((pieces // 2,))],
        compiler_params=params(STREAM_MIB),
        cost_estimate=cost(SHORT, 0),
        name="down",
    )(gated, mamba_down)
    summed = (keep + taken.astype(F32)).astype(BF16)
    hidden_out = call(
        finish_kernel,
        out_shape=shape((rows, cols), BF16),
        in_specs=vmem(2),
        out_specs=vmem(1)[0],
        compiler_params=params(4),
        name="finish",
    )(exchange(summed), hidden)
    return (hidden_out, mamba_next, jnp.transpose(conv_next, (1, 0, 2)))


def solution(mesh):
    owners = ("groups", "src", "chan")
    channels = ("src", "chan")
    placed = (
        P("groups", channels),
        P(owners, None),
        P(owners, None),
        P(owners, None, None),
        P("groups"),
        P(owners),
        P(owners),
        P(owners, None, None),
        P(owners, None, None),
        P(None, channels),
        P(None, channels),
        P(None, channels),
        P(None, channels),
        P(channels),
        P(channels, None),
        P(None, channels),
        P(channels),
        P(None, channels),
        P(channels),
        P(channels, None),
    )
    return jax.shard_map(
        on_device,
        mesh=mesh,
        in_specs=placed,
        out_specs=(P("groups", channels), P("groups", None, channels), P("groups", None, channels)),
        check_vma=False,
    )
```

```python
import functools
import math

import jax
import jax.numpy as jnp
from jax import lax
from jax.experimental import pallas as pl
from jax.experimental.pallas import tpu as pltpu
from jax.sharding import PartitionSpec as P

D = 8192
NS = 16
DTR = 512
QH = 64
KVH = 8
HD = 128
G = QH // KVH
LANES = 128
NEGATIVE = -1e30
STREAM_MIB = 50
DOWN_READY = 1
SHORT = 3 * 10**9
F32 = jnp.float32
BF16 = jnp.bfloat16
VM = pltpu.VMEM


def round_up(value, step):
    return -(-value // step) * step


def vmem(count):
    return [pl.BlockSpec(memory_space=pltpu.VMEM)] * count


def smem(count):
    return [pl.BlockSpec(memory_space=pltpu.SMEM)] * count


def hbm(count):
    return [pl.BlockSpec(memory_space=pltpu.HBM)] * count


def params(mib):
    return pltpu.CompilerParams(vmem_limit_bytes=mib * 2**20)


def cost(flops, nbytes):
    return pl.CostEstimate(flops=flops, bytes_accessed=nbytes, transcendentals=0)


def swap(x):
    return lax.ppermute(x, "src", [(0, 1), (1, 0)])


def exchange(x):
    return lax.all_to_all(x, "chan", split_axis=0, concat_axis=0, tiled=True)


class Chunk:
    def __init__(self, nchan, held_tokens, blocks, steps):
        self.per = QH // nchan
        self.tokens = held_tokens
        self.owner_rows = held_tokens // LANES
        self.value = held_tokens
        self.small = 2 * held_tokens
        self.query = 2 + self.owner_rows
        self.conv = self.query + self.per
        self.conv_rows = steps * blocks
        self.small_rows = round_up(self.conv + 2 * self.conv_rows, 16)
        self.rows = self.small + self.small_rows


def pack_kernel(
    nchan,
    lay,
    query_hbm,
    newkv_hbm,
    pages_hbm,
    conv_hbm,
    owner_hbm,
    index_hbm,
    lengths_hbm,
    *refs,
):
    outs, (query, newkv, pages, conv, owners, indexes, lengths, sems) = refs[:nchan], refs[nchan:]
    moves = (
        (pages_hbm, pages),
        (conv_hbm, conv),
        (query_hbm, query),
        (newkv_hbm, newkv),
        (owner_hbm, owners),
        (index_hbm, indexes),
        (lengths_hbm, lengths),
    )
    copies = [pltpu.make_async_copy(src, dst, sems.at[i]) for i, (src, dst) in enumerate(moves)]
    for copy in copies:
        copy.start()
    c = lax.axis_index("src")
    page_tokens = pages.shape[1]
    cols = conv.shape[2] // (2 * nchan)
    blocks = cols // LANES
    steps = conv.shape[0]
    rep = nchan // KVH
    for copy in copies[1:]:
        copy.wait()
    lane = lax.broadcasted_iota(jnp.int32, (1, LANES), 1)
    per_row = LANES // page_tokens
    owner_rows = []
    for i in range(lay.owner_rows):
        found = jnp.full((1, LANES), -1, jnp.int32)
        for j in range(per_row):
            owner = owners[i * per_row + j]
            left = lengths[owner] - indexes[i * per_row + j] * page_tokens
            found = jnp.where((lane // page_tokens == j) & (lane % page_tokens < left), owner, found)
        owner_rows.append(found.astype(F32))
    targets = [jnp.bitwise_xor(lax.axis_index("chan"), k) for k in range(nchan)]
    for d, out_ref in zip(targets, outs):
        at = lax.div(d, rep) * HD
        small = [newkv[0:1, pl.ds(pl.multiple_of(x, HD), HD)].astype(F32) for x in (at, KVH * HD + at)] + owner_rows
        for h in range(lay.per):
            place = pl.multiple_of((d * lay.per + h) * HD, HD)
            small.append(query[0:1, pl.ds(place, HD)].astype(F32))
        for half in (c, 1 - c):
            first = (half * nchan + d) * cols
            for b in range(blocks):
                lanes = pl.ds(pl.multiple_of(first + b * LANES, LANES), LANES)
                for w in range(steps):
                    small.append(conv[w, 0:1, lanes])
        if lay.small_rows > len(small):
            small.append(jnp.zeros((lay.small_rows - len(small), LANES), F32))
        out_ref[lay.small : lay.rows, :] = jnp.concatenate(small, axis=0).astype(BF16)
    copies[0].wait()
    for d, out_ref in zip(targets, outs):
        at = lax.div(d, rep) * HD
        keys = pl.ds(pl.multiple_of(at, HD), HD)
        values = pl.ds(pl.multiple_of(KVH * HD + at, HD), HD)
        out_ref[0 : lay.tokens, :] = pages[:, :, keys].reshape(lay.tokens, HD)
        out_ref[lay.value : lay.small, :] = pages[:, :, values].reshape(lay.tokens, HD)


def load_kernel(residual, state, residual_out, same, cross):
    c = lax.axis_index("src")
    nchan, _, cols = same.shape
    residual_out[...] = residual[...]
    for ref, half in ((same, c), (cross, 1 - c)):
        for d in range(nchan):
            lanes = pl.ds(pl.multiple_of((half * nchan + d) * cols, cols), cols)
            ref[d] = state[0, :, lanes].astype(BF16)


def attend_kernel(lay, nchan, *refs):
    recv, other = refs[:nchan], refs[nchan : 2 * nchan]
    out_ref, conv_own, conv_other, queries, scores, result = refs[2 * nchan :]
    d = lax.axis_index("chan")
    per, tokens = lay.per, lay.tokens
    c = lax.axis_index("src")
    count = nchan * per
    scale = 1.0 / math.sqrt(HD)
    contract = (((1,), (1,)), ((), ()))
    new_keys, new_values, owners = [], [], []
    spare = conv_own.shape[1] - lay.conv_rows
    for blocks, conv_out, at in ((recv, conv_own, lay.conv), (other, conv_other, lay.conv + lay.conv_rows)):
        for k, ref in enumerate(blocks):
            s = jnp.bitwise_xor(d, k)
            small = ref[lay.small : lay.rows, :].astype(F32)
            conv = small[at : at + lay.conv_rows, :]
            conv_out[s] = jnp.concatenate([conv, jnp.zeros((spare, LANES), F32)], axis=0) if spare else conv
            owners.append(jnp.concatenate([small[2 + i : 3 + i, :] for i in range(lay.owner_rows)], axis=1))
            if blocks is recv:
                queries[pl.ds(pl.multiple_of(s * per, per), per), :] = small[lay.query : lay.query + per, :]
                new_keys.append(small[0:1, :])
                new_values.append(small[1:2, :])
    fill = round_up(nchan, 16) - nchan
    if fill:
        new_keys.append(jnp.zeros((fill, HD), F32))
        new_values.append(jnp.zeros((fill, HD), F32))
    new_keys = jnp.concatenate(new_keys, axis=0).astype(BF16)
    new_values = jnp.concatenate(new_values, axis=0).astype(BF16)
    place = lax.broadcasted_iota(jnp.int32, (count, 1), 0) // per
    lane = lax.broadcasted_iota(jnp.int32, (1, nchan + fill), 1)
    q = queries[...].astype(BF16)
    new_scores = lax.dot_general(q, new_keys, contract, preferred_element_type=F32) * scale
    new_scores = jnp.where(jnp.bitwise_xor(place, d) == lane, new_scores, NEGATIVE)
    wide = (c * nchan + place).astype(F32)
    sources = list(recv) + list(other)
    highest = None
    for i, ref in enumerate(sources):
        part = lax.dot_general(q, ref[0:tokens, :], contract, preferred_element_type=F32) * scale
        part = jnp.where(wide == owners[i], part, NEGATIVE)
        scores[:, i * tokens : (i + 1) * tokens] = part
        highest = part if highest is None else jnp.maximum(highest, part)
    peak = jnp.maximum(jnp.max(highest, axis=1, keepdims=True), jnp.max(new_scores, axis=1, keepdims=True))
    new_weight = jnp.exp(new_scores - peak)
    numer = jnp.dot(new_weight.astype(BF16), new_values, preferred_element_type=F32)
    summed = None
    for i, ref in enumerate(sources):
        weight = jnp.exp(scores[:, i * tokens : (i + 1) * tokens] - peak)
        summed = weight if summed is None else summed + weight
        numer = numer + jnp.dot(weight.astype(BF16), ref[lay.value : lay.small, :], preferred_element_type=F32)
    total = jnp.sum(summed, axis=1, keepdims=True) + jnp.sum(new_weight, axis=1, keepdims=True)
    result[...] = numer / total
    heads = [result[pl.ds(h, nchan, stride=per), :] for h in range(per)]
    block = jnp.concatenate(heads, axis=0).astype(BF16)
    for i in range(nchan):
        out_ref[i] = block


def in_order(own, other, c):
    return jnp.where(c == 0, jnp.concatenate([own, other], axis=0), jnp.concatenate([other, own], axis=0))


def own_first(x, c):
    half = x.shape[0] // 2
    return in_order(x[:half], x[half:], c)


def stream(weight, buffer, sems, starts):
    depth = buffer.shape[0] // len(starts)
    copies = []
    for i, start in enumerate(starts):
        rows = pl.ds(pl.multiple_of(start, depth), depth)
        copies.append(pltpu.make_async_copy(weight.at[rows, :], buffer.at[pl.ds(i * depth, depth), :], sems.at[i]))
        copies[-1].start()
    return copies


def row_starts(nchan, depth, own):
    c = lax.axis_index("src")
    half = c if own else 1 - c
    return [(half * nchan + i) * depth for i in range(nchan)]


def half_dot(copies, lhs, total, buffer, rows):
    depth = lhs.shape[2]
    for i, copy in enumerate(copies):
        copy.wait()
        block = buffer[i * depth : (i + 1) * depth, :]
        part = jnp.dot(lhs[i, 0:rows, :], block, preferred_element_type=F32)
        total = part if total is None else total + part
    return total


def own_kernel(lhs, weight, out_ref, buffer, sems):
    nchan, depth = lhs.shape[0], lhs.shape[2]
    copies = stream(weight, buffer, sems, row_starts(nchan, depth, True))
    out_ref[...] = half_dot(copies, lhs, None, buffer, out_ref.shape[0])


def halves_dot(copies, own, other, buffer, count):
    nchan, depth = own.shape[0], own.shape[2]
    total = None
    for i, copy in enumerate(copies):
        ref = own if i < nchan else other
        copy.wait()
        part = jnp.dot(ref[i % nchan, 0:count, :], buffer[i * depth : (i + 1) * depth, :], preferred_element_type=F32)
        total = part if total is None else total + part
    return total


def fetch_kernel(weight, out_ref, sems):
    depth = out_ref.shape[0] // sems.shape[0]
    for copy in stream(weight, out_ref, sems, [i * depth for i in range(sems.shape[0])]):
        copy.wait()


def out_kernel(lay, own, other, residual, cross, fetched, weight, hidden_out, out_ref, buffer, sems):
    c = lax.axis_index("src")
    nchan, rows = own.shape[0], residual.shape[0]
    depth = lay.per * HD
    ready = fetched.shape[0] // depth
    copies = stream(weight, buffer, sems, [i * depth for i in range(ready, nchan)])
    for i in range(nchan):
        out_ref[i, rows : rows + NS, :] = cross[i]
    product = residual[...].astype(F32)
    for i in range(nchan):
        mine, rest = own[i].astype(F32), other[i].astype(F32)
        heads = [slice(h * nchan, (h + 1) * nchan) for h in range(lay.per)]
        lhs = jnp.concatenate([in_order(mine[h], rest[h], c) for h in heads], axis=1).astype(BF16)
        if i < ready:
            block = fetched[i * depth : (i + 1) * depth, :]
        else:
            copies[i - ready].wait()
            block = buffer[(i - ready) * depth : (i - ready + 1) * depth, :]
        product = product + jnp.dot(lhs, block, preferred_element_type=F32)
    hidden = product.astype(BF16)
    hidden_out[...] = hidden
    for i in range(nchan):
        out_ref[i, 0:rows, :] = hidden


def values_kernel(
    lay, own, other, own_conv, other_conv, taps, offset, state_proj, same, partial, weight,
    conv_out, act_out, rms_out, proj_out, buffer, sems,
):
    copies = stream(weight, buffer, sems, row_starts(own.shape[0], own.shape[2], False))
    c = lax.axis_index("src")
    nchan = own.shape[0]
    rows, cols = act_out.shape
    squares = jnp.zeros((rows, own.shape[2]), F32)
    for ref in (own, other):
        for i in range(nchan):
            wide = ref[i, 0:rows, :].astype(F32)
            squares = squares + wide * wide
    inverse = lax.rsqrt(jnp.sum(squares, axis=1, keepdims=True) / D + 1e-06)
    rms_out[...] = jnp.broadcast_to(inverse, rms_out.shape)
    steps = conv_out.shape[0]
    blocks = cols // LANES
    for i in range(nchan):
        for b in range(blocks):
            proj_out[i, b * NS : (b + 1) * NS, :] = same[i, :, b * LANES : (b + 1) * LANES]
    tails = (own_conv[...], other_conv[...])
    window = []
    for w in range(steps):
        sides = [jnp.concatenate([t[:, b * steps + w, :] for b in range(blocks)], axis=1) for t in tails]
        window.append(in_order(sides[0], sides[1], c))
    window.append(half_dot(copies, other, partial[...], buffer, rows) * inverse)
    mixed = jnp.zeros((rows, cols), F32)
    for w in range(steps + 1):
        mixed = mixed + window[w] * taps[w : w + 1, :]
        if w > 0:
            conv_out[w - 1] = window[w]
    mixed = mixed + offset[...]
    act = mixed / (1.0 + jnp.exp(-mixed))
    act_out[...] = act
    part = lax.dot_general(act.astype(BF16), state_proj[...], (((1,), (1,)), ((), ())), preferred_element_type=F32)
    spare = round_up(part.shape[1], LANES) - part.shape[1]
    part = jnp.concatenate([part, jnp.zeros((rows, spare), F32)], axis=1).astype(BF16)
    base = blocks * NS
    for i in range(nchan):
        for b in range(part.shape[1] // LANES):
            proj_out[i, base + b * rows : base + (b + 1) * rows, :] = part[:, b * LANES : (b + 1) * LANES]


def gates_kernel(own, other, rms, weight, down_hbm, out_ref, down_out, buffer, sems, down_sems):
    nchan, depth = own.shape[0], own.shape[2]
    copies = stream(
        weight,
        buffer,
        sems,
        row_starts(nchan, depth, True) + row_starts(nchan, depth, False),
    )
    part_down = down_stream(down_hbm, down_out, down_sems, (1 - lax.axis_index("src"),), 0)
    gate = halves_dot(copies, own, other, buffer, out_ref.shape[0]) * rms[:, 0:1]
    out_ref[...] = gate / (1.0 + jnp.exp(-gate))
    for copy in part_down:
        copy.wait()


def down_stream(weight, buffer, sems, halves, first):
    width = weight.shape[1] // 2
    step = buffer.shape[1] // sems.shape[0]
    blocks = [(half, i) for half in halves for i in range(width // step)]
    copies = []
    for half, i in blocks[first : first + sems.shape[0]]:
        slot = len(copies)
        columns = pl.ds(pl.multiple_of(half * width + i * step, step), step)
        target = buffer.at[:, pl.ds(slot * step, step)]
        copies.append(pltpu.make_async_copy(weight.at[:, columns], target, sems.at[slot]))
        copies[-1].start()
    return copies


def down_product(copies, gated, fetched, buffer, out_ref):
    cols = out_ref.shape[2]
    step = buffer.shape[1] // len(copies)
    ready = 0 if fetched is None else fetched.shape[1] // step
    each = step // cols
    for slot in range(ready + len(copies)):
        if slot < ready:
            block = fetched[:, slot * step : (slot + 1) * step]
        else:
            copies[slot - ready].wait()
            block = buffer[:, (slot - ready) * step : (slot - ready + 1) * step]
        part = jnp.dot(gated, block, preferred_element_type=F32).astype(out_ref.dtype)
        for j in range(each):
            out_ref[slot * each + j] = part[:, j * cols : (j + 1) * cols]


def scan_kernel(
    own,
    other,
    hid_other,
    act_ref,
    gate_ref,
    step_proj,
    step_bias,
    decay_log,
    skip_gain,
    fetched,
    weight,
    next_hbm,
    gated_out,
    send_out,
    turned,
    mixed,
    next_out,
    buffer,
    sems,
    save_sem,
):
    c = lax.axis_index("src")
    copies = down_stream(weight, buffer, sems, (1 - c,), DOWN_READY)
    nchan = own.shape[0]
    rows, cols = act_ref.shape
    blocks = cols // LANES
    base = blocks * NS
    summed = jnp.zeros((own.shape[1] - base, LANES), F32)
    for ref in (own, other):
        for i in range(nchan):
            summed = summed + ref[i, base:, :].astype(F32)
    parts = [summed[b * rows : (b + 1) * rows, :] for b in range(summed.shape[0] // rows)]
    low = jnp.concatenate(parts[: DTR // LANES], axis=1).astype(BF16)
    act = act_ref[...]
    raw = jnp.dot(low, step_proj[...], preferred_element_type=F32) + step_bias[...]
    step = jnp.maximum(raw, 0.0) + jnp.log1p(jnp.exp(-jnp.abs(raw)))
    turned[...] = jnp.zeros_like(turned)
    turned[0:rows, :] = own_first(parts[DTR // LANES], c)
    mats = turned[...].T
    rate = -jnp.exp(decay_log[...])
    fed = own_first(step * act, c)
    step = own_first(step, c)
    for side in range(2):
        for s in range(nchan):
            q = side * nchan + s
            place = (c if side == 0 else 1 - c) * nchan + s
            b_col = mats[0:NS, q : q + 1]
            c_col = mats[NS : 2 * NS, q : q + 1]
            for b in range(blocks):
                lanes = slice(b * LANES, (b + 1) * LANES)
                if side == 0:
                    state = own[s, b * NS : (b + 1) * NS, :].astype(F32)
                else:
                    state = hid_other[s, rows : rows + NS, lanes].astype(F32)
                after = jnp.exp(step[q : q + 1, lanes] * rate[:, lanes]) * state + fed[q : q + 1, lanes] * b_col
                next_out[place, :, lanes] = after
                mixed[q : q + 1, lanes] = jnp.sum(after * c_col, axis=0, keepdims=True)
    save = pltpu.make_async_copy(next_out, next_hbm, save_sem)
    save.start()
    gated = ((own_first(mixed[...], c) + skip_gain[...] * act) * gate_ref[...]).astype(BF16)
    gated_out[...] = gated
    down_product(copies, gated, fetched, buffer, send_out)
    save.wait()


def down_kernel(gated, weight, out_ref, buffer, sems):
    copies = down_stream(weight, buffer, sems, (lax.axis_index("src"),), 0)
    down_product(copies, gated[...], None, buffer, out_ref)


def finish_kernel(final, hidden, out_ref):
    total = None
    for i in range(final.shape[0]):
        part = final[i].astype(F32)
        total = part if total is None else total + part
    out_ref[...] = (hidden[...].astype(F32) + total).astype(BF16)


def on_device(
    residual_input,
    query_heads,
    new_keyval,
    cache_pages,
    prompt_lengths,
    page_owner,
    page_index,
    mamba_state,
    conv_state,
    out_heads,
    in_values,
    in_gates,
    conv_taps,
    conv_offset,
    state_proj,
    step_proj,
    step_bias,
    decay_log,
    skip_gain,
    mamba_down,
):
    nchan = lax.axis_size("chan")
    rows, cols = residual_input.shape
    steps = conv_state.shape[1]
    held, page_tokens = cache_pages.shape[0], cache_pages.shape[1]
    lay = Chunk(nchan, held * page_tokens, cols // LANES, steps)
    call = pl.pallas_call
    shape = jax.ShapeDtypeStruct

    conv_rows = jnp.transpose(conv_state, (1, 0, 2))
    chunk = shape((lay.rows, LANES), BF16)
    packed = call(
        functools.partial(pack_kernel, nchan, lay),
        out_shape=(chunk,) * nchan,
        in_specs=hbm(7),
        out_specs=tuple(vmem(nchan)),
        scratch_shapes=[
            VM(query_heads.shape, BF16),
            VM(new_keyval.shape, BF16),
            VM(cache_pages.shape, BF16),
            VM(conv_rows.shape, F32),
            pltpu.SMEM(page_owner.shape, jnp.int32),
            pltpu.SMEM(page_index.shape, jnp.int32),
            pltpu.SMEM(prompt_lengths.shape, jnp.int32),
            pltpu.SemaphoreType.DMA((7,)),
        ],
        compiler_params=pltpu.CompilerParams(vmem_limit_bytes=64 * 2**20 - 2**18),
        name="pack",
    )(query_heads, new_keyval, cache_pages, conv_rows, page_owner, page_index, prompt_lengths)
    *packed, residual_input, mamba_state = lax.optimization_barrier((*packed, residual_input, mamba_state))
    arrived = [packed[0]]
    for k in range(1, nchan):
        arrived.append(lax.ppermute(packed[k], "chan", [(i, i ^ k) for i in range(nchan)]))
    cut = shape((nchan, NS, cols), BF16)
    residual, same, cross = call(
        load_kernel,
        out_shape=(shape((rows, cols), BF16), cut, cut),
        in_specs=vmem(2),
        out_specs=tuple(vmem(3)),
        compiler_params=params(16),
        cost_estimate=cost(SHORT, 0),
        name="load",
    )(residual_input, mamba_state)

    arrived[0], residual, same, cross = lax.optimization_barrier((arrived[0], residual, same, cross))
    other_arrived = [swap(block) for block in arrived]
    pairs = nchan * lay.per
    conv_cut = shape((nchan, round_up(lay.conv_rows, 8), LANES), F32)
    attended, conv_own, conv_other = call(
        functools.partial(attend_kernel, lay, nchan),
        out_shape=(shape((nchan, pairs, LANES), BF16), conv_cut, conv_cut),
        in_specs=vmem(2 * nchan),
        out_specs=tuple(vmem(3)),
        scratch_shapes=[VM((pairs, HD), F32), VM((pairs, 2 * nchan * lay.tokens), F32), VM((pairs, HD), F32)],
        compiler_params=params(4 if held < 16 else 44),
        name="attend",
    )(*arrived, *other_arrived)
    att_own, out_weight = lax.optimization_barrier((exchange(attended), out_heads))
    att_other = swap(att_own)
    fetched_rows = D // 4
    out_fetched = call(
        fetch_kernel,
        out_shape=shape((fetched_rows, cols), BF16),
        in_specs=hbm(1),
        out_specs=vmem(1)[0],
        scratch_shapes=[pltpu.SemaphoreType.DMA((4,))],
        compiler_params=params(STREAM_MIB),
        cost_estimate=cost(SHORT, 0),
        name="fetch",
    )(out_weight)
    hidden, hid_send = call(
        functools.partial(out_kernel, lay),
        out_shape=(shape((rows, cols), BF16), shape((nchan, rows + NS, cols), BF16)),
        in_specs=vmem(5) + hbm(1),
        out_specs=tuple(vmem(2)),
        scratch_shapes=[
            VM((D - fetched_rows, cols), BF16),
            pltpu.SemaphoreType.DMA(((D - fetched_rows) // (lay.per * HD),)),
        ],
        compiler_params=params(STREAM_MIB),
        name="out",
    )(att_own, att_other, residual, cross, out_fetched, out_heads)
    half_streamed = [VM((D // 2, cols), BF16), pltpu.SemaphoreType.DMA((nchan,))]
    streamed = [VM((D, cols), BF16), pltpu.SemaphoreType.DMA((2 * nchan,))]
    hid_own = exchange(hid_send)
    hid_other = swap(hid_own)
    values_partial = call(
        own_kernel,
        out_shape=shape((rows, cols), F32),
        in_specs=vmem(1) + hbm(1),
        out_specs=vmem(1)[0],
        scratch_shapes=half_streamed,
        compiler_params=params(STREAM_MIB),
        cost_estimate=cost(SHORT, 0),
        name="values_own",
    )(hid_own, in_values)

    sent_rows = (cols // LANES) * NS + (round_up(state_proj.shape[1], LANES) // LANES) * rows
    conv_next, act, rms, part = call(
        functools.partial(values_kernel, lay),
        out_shape=(
            shape((steps, rows, cols), F32),
            shape((rows, cols), F32),
            shape((rows, LANES), F32),
            shape((nchan, sent_rows, LANES), BF16),
        ),
        in_specs=vmem(9) + hbm(1),
        out_specs=tuple(vmem(4)),
        scratch_shapes=half_streamed,
        compiler_params=params(STREAM_MIB),
        name="values",
    )(hid_own, hid_other, conv_own, conv_other, conv_taps, conv_offset[None, :], state_proj.T, same, values_partial, in_values)
    part, down_weight = lax.optimization_barrier((part, mamba_down))
    proj_own = exchange(part)
    pieces = 8
    piece = D // pieces
    gate, down_fetched = call(
        gates_kernel,
        out_shape=(shape((rows, cols), F32), shape((cols, DOWN_READY * piece), BF16)),
        in_specs=vmem(3) + hbm(2),
        out_specs=tuple(vmem(2)),
        scratch_shapes=streamed + [pltpu.SemaphoreType.DMA((DOWN_READY,))],
        compiler_params=params(STREAM_MIB),
        cost_estimate=cost(SHORT, 0),
        name="gates",
    )(hid_own, hid_other, rms, in_gates, down_weight)
    proj_own, gate, down_fetched = lax.optimization_barrier((proj_own, gate, down_fetched))
    proj_other = swap(proj_own)

    down_streamed = [
        VM((rows, NS, cols), F32),
        VM((cols, D // 2 - DOWN_READY * piece), BF16),
        pltpu.SemaphoreType.DMA((pieces // 2 - DOWN_READY,)),
        pltpu.SemaphoreType.DMA,
    ]
    mamba_next, gated, send = call(
        scan_kernel,
        out_shape=(
            shape((rows, NS, cols), F32),
            shape((rows, cols), BF16),
            shape((nchan, rows, cols), BF16),
        ),
        in_specs=vmem(10) + hbm(1),
        out_specs=tuple(hbm(1) + vmem(2)),
        scratch_shapes=[VM((LANES, LANES), F32), VM((rows, cols), F32)] + down_streamed,
        compiler_params=params(STREAM_MIB),
        name="scan",
    )(
        proj_own,
        proj_other,
        hid_other,
        act,
        gate,
        step_proj,
        step_bias[None, :],
        decay_log,
        skip_gain[None, :],
        down_fetched,
        mamba_down,
    )
    taken = swap(send)
    keep = call(
        down_kernel,
        out_shape=shape((nchan, rows, cols), F32),
        in_specs=vmem(1) + hbm(1),
        out_specs=vmem(1)[0],
        scratch_shapes=[VM((cols, D // 2), BF16), pltpu.SemaphoreType.DMA((pieces // 2,))],
        compiler_params=params(STREAM_MIB),
        cost_estimate=cost(SHORT, 0),
        name="down",
    )(gated, mamba_down)
    summed = (keep + taken.astype(F32)).astype(BF16)
    hidden_out = call(
        finish_kernel,
        out_shape=shape((rows, cols), BF16),
        in_specs=vmem(2),
        out_specs=vmem(1)[0],
        compiler_params=params(4),
        name="finish",
    )(exchange(summed), hidden)
    return (hidden_out, mamba_next, jnp.transpose(conv_next, (1, 0, 2)))


def solution(mesh):
    owners = ("groups", "src", "chan")
    channels = ("src", "chan")
    placed = (
        P("groups", channels),
        P(owners, None),
        P(owners, None),
        P(owners, None, None),
        P("groups"),
        P(owners),
        P(owners),
        P(owners, None, None),
        P(owners, None, None),
        P(None, channels),
        P(None, channels),
        P(None, channels),
        P(None, channels),
        P(channels),
        P(channels, None),
        P(None, channels),
        P(channels),
        P(None, channels),
        P(channels),
        P(channels, None),
    )
    return jax.shard_map(
        on_device,
        mesh=mesh,
        in_specs=placed,
        out_specs=(P("groups", channels), P("groups", None, channels), P("groups", None, channels)),
        check_vma=False,
    )
```
